32 devices in a mesh: segment: 4 (over x, core), blk: 8 (over z, y).
Axes of the slice: x: 2, y: 2, z: 4, core: 2. Of those that a mesh axis runs over, the one named last changes fastest.
Arguments:
- fresh: bfloat16 [256, 4096], replicated, may hold values from -6 to 6
- previous: bfloat16 [4, 256, 4096], P('segment'), may hold values from -6 to 6
- span_index: int32 [4], P('segment'), may hold values from 0 to 7
- cache_counts: int32 [4, 8], P('segment'), may hold values from 1 to 2048, 8192 in all within a row
- norm_gain: float32 [4, 4096], P('segment'), may hold values from 0.1 to 1.9
- w_query: bfloat16 [4, 4096, 4096], P('segment', None, 'blk'), may hold values from -0.375 to 0.375
- w_keyval: bfloat16 [4, 4096, 2048], P('segment', None, 'blk'), may hold values from -0.09375 to 0.09375
- w_out: bfloat16 [4, 4096, 4096], P('segment', 'blk'), may hold values from -0.09375 to 0.09375
- cache_keys: bfloat16 [4, 16384, 1024], P('segment', 'blk'), may hold values from -220 to 220
- cache_values: bfloat16 [4, 16384, 1024], P('segment', 'blk'), may hold values from -6 to 6
Outputs:
- mixed: bfloat16 [4, 256, 4096], P('segment')
The draws below stay inside these ranges and needn't reach their ends.
Inputs may be any that keep to these rules, and one draw needn't show every extreme that they name: Each row of cache_counts sums to 8192 and its largest entry is 2048.
All inputs are finite; a program needn't handle non-finite values.
Results may differ from the reference program's by a relative error of at most 0.012.
Values may be sent and summed in bfloat16 or wider, within the bound.
A program may use at most 128 MiB of HBM per device.

```python
import math
import jax
import jax.numpy as jnp
import numpy as np
from jax import lax

D = 4096
HEADS = 32
KVH = 8
HD = 128
SPAN = 256
CACHE_DEV = 2048
LAYERS = 4
CACHE = 16384
N_BLK = 8


def draw_cache_keys(key, part):
    base_key = jax.random.fold_in(key, 0)
    key_rows = jnp.clip(jax.random.normal(base_key, (LAYERS, CACHE, KVH * HD), jnp.float32), -6.0, 6.0)
    return key_rows.astype(jnp.bfloat16)


def plant(entries, own_key, low, largest):
    longest = entries.shape.index(max(entries.shape))
    spots = []
    for shift in (0, 1):
        where = [jax.random.randint(jax.random.fold_in(own_key, axis), (), 0, length) for axis, length in enumerate(entries.shape)]
        where[longest] = (where[longest] + shift) % entries.shape[longest]
        spots.append(tuple(where))
    return entries.at[spots[0]].set(low).at[spots[1]].set(largest)


def steps_of(key, dims, pieces, least, largest):
    def one(position, blocks):
        heights = jax.random.uniform(jax.random.fold_in(jax.random.fold_in(key, 6), position), (blocks,), jnp.float32, least / len(pieces), largest / len(pieces))
        return jnp.repeat(jnp.exp(heights), dims[position] // blocks).reshape((-1,) + (1,) * (len(dims) - position - 1))

    factor_of = one(*pieces[0])
    for cut in pieces[1:]:
        factor_of = factor_of * one(*cut)
    return factor_of


def profile(count, total, most, lean):
    portions = [(1 << 20) // math.isqrt(grade ** lean) + 1 for grade in range(2, count + 1)]
    rest, given = total - most - (count - 1), [1] * (count - 1)
    while rest > 0:
        candidates = [i for i in range(count - 1) if given[i] < most]
        whole, budget = sum([portions[i] for i in candidates]), rest
        for i in candidates:
            extra = min(most - given[i], max(1, budget * portions[i] // whole), rest)
            given[i] = given[i] + extra
            rest = rest - extra
    return np.array([most] + given)


def ragged(own_key, count, total, limit, lean):
    if count == 2:
        one = jax.random.randint(own_key, (), max(1, total - limit), min(limit, total - 1) + 1)
        return jnp.stack([one, total - one])
    lengths = jnp.asarray(profile(count, total, limit, lean), jnp.int32)
    couples = (count - 1) // 2
    donor, taker = lengths[1:1 + 2 * couples:2], lengths[2:2 + 2 * couples:2]
    room = jnp.minimum(donor - 1, limit - taker)
    shifted = jax.random.randint(jax.random.fold_in(own_key, 1), (couples,), 0, 1 << 20) % (room + 1)
    lengths = lengths.at[1:1 + 2 * couples:2].set(donor - shifted).at[2:2 + 2 * couples:2].set(taker + shifted)
    return lengths[jax.random.permutation(jax.random.fold_in(own_key, 2), count)]


def normal_values(own_key, shape, spread, most, shards=(), kind=jnp.bfloat16):
    array = jax.random.normal(own_key, shape, jnp.float32) * spread
    if len(shards) > 0:
        array = steps_of(own_key, shape, shards, -0.22, 0.18) * array
    return jnp.clip(array, min=-most, max=most).astype(kind)


def setup_inputs(seed: int = 0) -> dict:
    seeds = jax.random.split(jax.random.key(seed), 11)
    return {
        "fresh": normal_values(seeds[0], (SPAN, D), 1.0, 6.0),
        "previous": normal_values(seeds[1], (LAYERS, SPAN, D), 1.0, 6.0, ((0, 4),)),
        "span_index": plant(jax.random.randint(seeds[2], (LAYERS,), 0, 8), jax.random.fold_in(seeds[2], 1), 0, 7).astype(jnp.int32),
        "cache_counts": jax.vmap(lambda own: ragged(own, N_BLK, CACHE_DEV * N_BLK // 2, CACHE_DEV, 2))(jax.random.split(seeds[3], LAYERS)).reshape((LAYERS, N_BLK)).astype(jnp.int32),
        "norm_gain": jnp.clip(1.0 + 0.18 * jax.random.normal(seeds[4], (LAYERS, D), jnp.float32), 0.1, 1.9),
        "w_query": normal_values(seeds[5], (LAYERS, D, HEADS * HD), (D // 16) ** -0.5, 0.375, ((0, 4), (2, 8))),
        "w_keyval": normal_values(seeds[6], (LAYERS, D, 2 * KVH * HD), D ** -0.5, 0.09375, ((0, 4), (2, 8))),
        "w_out": normal_values(seeds[7], (LAYERS, HEADS * HD, D), (HEADS * HD) ** -0.5, 0.09375, ((0, 4), (1, 8))),
        "cache_keys": draw_cache_keys(jax.random.fold_in(seeds[10], 71), 0),
        "cache_values": normal_values(seeds[9], (LAYERS, CACHE, KVH * HD), 1.0, 6.0, ((0, 4), (1, 8))),
    }


ROPE_BASE = 500000.0
EPSILON = 1e-05

def rotate(projected, first_span):
    length = projected.shape[0]
    half_width = projected.shape[-1] // 2
    positions = (first_span * length + jnp.arange(length, dtype=jnp.int32)).astype(jnp.float32)
    inverse = ROPE_BASE ** (-(jnp.arange(half_width, dtype=jnp.float32) * 2.0) / projected.shape[-1])
    angles = positions[:, None] * inverse[None, :]
    cosine = jnp.cos(angles)[:, None, :]
    sine_table = jnp.sin(angles)[:, None, :]
    left_part = projected[..., :half_width]
    right_part = projected[..., half_width:]
    return jnp.concatenate([left_part * cosine - right_part * sine_table, right_part * cosine + left_part * sine_table], axis=-1)

def attend(queries, key_rows, value_rows, allowed):
    scores = jnp.einsum('grd,gcd->grc', queries, key_rows) * HD ** (-0.5)
    scores = jnp.where(allowed[None], scores, -jnp.inf)
    highest = lax.optimization_barrier(jnp.max(scores, axis=-1, keepdims=True))
    weights = jnp.exp(scores - highest)
    totals = lax.optimization_barrier(jnp.sum(weights, axis=-1, keepdims=True))
    rounded = lax.optimization_barrier(weights.astype(jnp.bfloat16)).astype(jnp.float32)
    partial_out = (jnp.einsum('grc,gcd->grd', rounded, value_rows) / totals).astype(jnp.bfloat16)
    return (partial_out, (highest + jnp.log(totals))[..., 0])

def layer_step(current, first_span, counts, gain, query_weight, keyval_weight, out_weight, cached_keys, cached_values):
    widened = current.astype(jnp.float32)
    span_rows = current.shape[0]
    width = current.shape[1]
    group_size = HEADS // KVH
    normed = (widened * lax.rsqrt(lax.optimization_barrier(jnp.mean(widened * widened, axis=-1, keepdims=True)) + EPSILON) * gain.astype(jnp.float32)).astype(jnp.bfloat16)
    queries = jnp.dot(normed, query_weight, preferred_element_type=jnp.float32).reshape(span_rows, HEADS, HD)
    queries = rotate(queries, first_span).astype(jnp.bfloat16)
    projected = jnp.dot(normed, keyval_weight, preferred_element_type=jnp.float32).reshape(span_rows, KVH, 2, HD)
    own_keys = rotate(projected[:, :, 0, :], first_span).astype(jnp.bfloat16)
    own_values = projected[:, :, 1, :].astype(jnp.bfloat16)
    grouped = queries.astype(jnp.float32).reshape(span_rows, KVH, group_size, HD).transpose(1, 0, 2, 3).reshape(KVH, span_rows * group_size, HD)
    row_tokens = jnp.arange(span_rows * group_size, dtype=jnp.int32) // group_size
    causal = row_tokens[:, None] >= jnp.arange(span_rows, dtype=jnp.int32)[None, :]
    own_out, own_log = attend(grouped, own_keys.astype(jnp.float32).transpose(1, 0, 2), own_values.astype(jnp.float32).transpose(1, 0, 2), causal)

    def shard_part(shard):
        start = (shard * CACHE_DEV).astype(jnp.int32)
        block_keys = lax.dynamic_slice_in_dim(cached_keys, start, CACHE_DEV, 0).astype(jnp.float32).reshape(CACHE_DEV, KVH, HD).transpose(1, 0, 2)
        block_values = lax.dynamic_slice_in_dim(cached_values, start, CACHE_DEV, 0).astype(jnp.float32).reshape(CACHE_DEV, KVH, HD).transpose(1, 0, 2)
        allowed = (jnp.arange(CACHE_DEV, dtype=jnp.int32) < counts[shard])[None, :]
        return attend(grouped, block_keys, block_values, allowed)
    shard_outs, shard_logs = lax.map(shard_part, jnp.arange(N_BLK, dtype=jnp.int32))
    all_outs = jnp.concatenate([own_out[None], shard_outs], axis=0).astype(jnp.float32)
    all_logs = jnp.concatenate([own_log[None], shard_logs], axis=0)
    ceiling = lax.optimization_barrier(jnp.max(all_logs, axis=0))
    factors = jnp.exp(all_logs - ceiling)
    attended = (lax.optimization_barrier(jnp.sum(factors[..., None] * all_outs, axis=0)) / lax.optimization_barrier(jnp.sum(factors, axis=0))[..., None]).astype(jnp.bfloat16)
    attended = attended.reshape(KVH, span_rows, group_size, HD).transpose(1, 0, 2, 3).reshape(span_rows, HEADS * HD)
    per_group = HEADS // N_BLK * HD
    head_terms = jnp.einsum('tnp,npd->ntd', attended.astype(jnp.float32).reshape(span_rows, N_BLK, per_group), out_weight.astype(jnp.float32).reshape(N_BLK, per_group, width))
    head_terms = lax.optimization_barrier(head_terms.astype(jnp.bfloat16)).astype(jnp.float32)
    return (widened + lax.optimization_barrier(jnp.sum(head_terms, axis=0))).astype(jnp.bfloat16)

def reference(fresh, previous, span_index, cache_counts, norm_gain, w_query, w_keyval, w_out, cache_keys, cache_values):
    results = []
    for segment_no in range(LAYERS):
        current = fresh if segment_no == 0 else previous[segment_no - 1]
        results.append(layer_step(current, span_index[segment_no], cache_counts[segment_no], norm_gain[segment_no], w_query[segment_no], w_keyval[segment_no], w_out[segment_no], cache_keys[segment_no], cache_values[segment_no]))
    return jnp.stack(results)
```

```python
import math

import jax
import jax.numpy as jnp
from jax import lax
from jax.experimental import pallas as pl
from jax.experimental.pallas import tpu as pltpu
from jax.sharding import PartitionSpec as P

KVH = 8
HD = 128


ROPE_BASE = 500000.0
EPSILON = 1e-05


def passed_along(block, axis, distance):
    devices = range(lax.axis_size(axis))
    route = [(i - distance, i) for i in devices if i - distance in devices]
    return lax.ppermute(block, axis, route)


def swapped(block, axis, distance):
    count = lax.axis_size(axis)
    route = []
    for low in range(count):
        high = low | 1 << distance
        if high != low and high < count:
            route += [(low, high), (high, low)]
    return lax.ppermute(block, axis, route)


def rotate(projected, first_span):
    length = projected.shape[0]
    half_width = projected.shape[-1] // 2
    positions = (first_span * length + jnp.arange(length, dtype=jnp.int32)).astype(jnp.float32)
    inverse = ROPE_BASE ** (
        -(jnp.arange(half_width, dtype=jnp.float32) * 2.0) / projected.shape[-1]
    )
    angles = positions[:, None] * inverse[None, :]
    cosine = jnp.cos(angles)[:, None, :]
    sine_table = jnp.sin(angles)[:, None, :]
    left_part = projected[..., :half_width]
    right_part = projected[..., half_width:]
    return jnp.concatenate(
        [
            left_part * cosine - right_part * sine_table,
            right_part * cosine + left_part * sine_table,
        ],
        axis=-1,
    )


def attend_rows(query_rows, key_rows, value_rows, allowed):
    scores = lax.dot_general(
        query_rows, key_rows, (((1,), (1,)), ((), ())), preferred_element_type=jnp.float32
    ) * query_rows.shape[-1] ** (-0.5)
    scores = jnp.where(allowed, scores, -jnp.inf)
    highest = jnp.max(scores, axis=-1, keepdims=True)
    weights = jnp.exp(scores - highest)
    totals = jnp.sum(weights, axis=-1, keepdims=True)
    partial_out = (
        jnp.dot(weights.astype(jnp.bfloat16), value_rows, preferred_element_type=jnp.float32)
        / totals
    ).astype(jnp.bfloat16)
    return (partial_out, (highest + jnp.log(totals))[:, 0])


def shards(
    fresh,
    previous,
    span_index,
    cache_counts,
    norm_gain,
    w_query,
    w_keyval,
    w_out,
    cache_keys,
    cache_values,
):
    blocks = lax.axis_size("blk")
    position = lax.axis_index("blk")
    span_rows = fresh.shape[0]
    arrived = passed_along(previous[0], "segment", 1)
    current = jnp.where(lax.axis_index("segment") == 0, fresh, arrived)
    widened = current.astype(jnp.float32)
    normed = (
        widened
        * lax.rsqrt(jnp.mean(widened * widened, axis=-1, keepdims=True) + EPSILON)
        * norm_gain[0]
    ).astype(jnp.bfloat16)
    first_span = span_index[0]
    heads_here = w_query.shape[2] // HD
    ratio = blocks // KVH
    queries = jnp.dot(normed, w_query[0], preferred_element_type=jnp.float32).reshape(
        span_rows, heads_here, HD
    )
    queries = rotate(queries, first_span).astype(jnp.bfloat16).reshape(span_rows, heads_here * HD)
    projected = jnp.dot(normed, w_keyval[0], preferred_element_type=jnp.float32)
    if ratio == 2:
        odd_member = position % 2 == 1
        as_key = rotate(projected[:, None, :], first_span)[:, 0, :].astype(jnp.bfloat16)
        mine = jnp.where(odd_member, projected.astype(jnp.bfloat16), as_key)
        partner = swapped(mine, "blk", 0)
        own_keys = jnp.where(odd_member, partner, mine)
        own_values = jnp.where(odd_member, mine, partner)
    else:
        own_keys = rotate(projected[:, None, :HD], first_span)[:, 0, :].astype(jnp.bfloat16)
        own_values = projected[:, HD:].astype(jnp.bfloat16)
    query_rows = queries.reshape(span_rows * heads_here, HD)
    row_tokens = jnp.arange(span_rows * heads_here, dtype=jnp.int32) // heads_here
    causal = row_tokens[:, None] >= jnp.arange(span_rows, dtype=jnp.int32)[None, :]
    own_out, own_log = attend_rows(query_rows, own_keys, own_values, causal)
    own_out = own_out.reshape(span_rows, heads_here * HD)
    own_log = own_log.reshape(span_rows, heads_here).T
    cache_rows = cache_keys.shape[1]
    offsets = jnp.arange(cache_rows, dtype=jnp.int32)
    every_query = lax.all_gather(queries, "blk", axis=0, tiled=True)
    live = cache_counts[0, position]

    def holder(source):
        query_block = lax.dynamic_slice_in_dim(
            every_query, source * span_rows, span_rows, 0
        ).reshape(span_rows * heads_here, HD)
        head_start = source // ratio * HD
        key_rows = lax.dynamic_slice_in_dim(cache_keys[0], head_start, HD, 1)
        value_rows = lax.dynamic_slice_in_dim(cache_values[0], head_start, HD, 1)
        partial_out, log_totals = attend_rows(
            query_block, key_rows, value_rows, (offsets < live)[None, :]
        )
        return (
            partial_out.reshape(span_rows, heads_here * HD),
            log_totals.reshape(span_rows, heads_here).T,
        )

    held_outs, held_logs = lax.map(holder, jnp.arange(blocks, dtype=jnp.int32))
    shard_outs = lax.all_to_all(held_outs, "blk", split_axis=0, concat_axis=0, tiled=True)
    shard_logs = lax.all_to_all(held_logs, "blk", split_axis=0, concat_axis=0, tiled=True)
    all_outs = (
        jnp.concatenate([own_out[None], shard_outs], axis=0)
        .astype(jnp.float32)
        .reshape(blocks + 1, span_rows, heads_here, HD)
    )
    all_logs = jnp.concatenate([own_log[None], shard_logs], axis=0).transpose(0, 2, 1)
    ceiling = jnp.max(all_logs, axis=0)
    factors = jnp.exp(all_logs - ceiling)
    attended = (
        jnp.sum(factors[..., None] * all_outs, axis=0) / jnp.sum(factors, axis=0)[..., None]
    ).astype(jnp.bfloat16)
    attended = attended.reshape(span_rows, heads_here * HD)
    head_terms = lax.optimization_barrier(
        jnp.dot(attended, w_out[0], preferred_element_type=jnp.float32).astype(jnp.bfloat16)
    ).astype(jnp.float32)
    summed = lax.psum(head_terms.astype(jnp.bfloat16), "blk").astype(jnp.float32)
    mixed = (widened + summed).astype(jnp.bfloat16)
    return mixed[None]


ROWS = 4
MESH = pl.DeviceIdType.MESH


def near_first(z, step):
    half = z // 2
    if isinstance(step, int):
        return (z, z + 1 - 2 * (z % 2), 2 - half, 3 - 3 * half)[step]
    pair = z + 1 - 2 * (z % 2)
    later = jnp.where(step == 2, 2 - half, 3 - 3 * half)
    return jnp.where(step == 0, z, jnp.where(step == 1, pair, later))


def head_columns(rows):
    return jnp.concatenate([rows] * 16, axis=0).T


def head_rows(columns):
    return columns.T[:8]


def plane_kernel(
    q_ref, ok_ref, ov_ref, bias_ref, cur_hbm, kc_hbm, vc_hbm, wo_hbm, out_ref,
    qall, kbuf, vbuf, wo, cur, o_keep, l_keep, oy_tx, ly_tx, oy_rx, ly_rx,
    oz_tx, lz_tx, oz_rx, lz_rx, att, hk, hy_tx, hy_rx, hz_tx, hz_rx,
    load_sem, q_up, q_down, q_side, q_in, oy_out, oy_in, ly_out, ly_in,
    oz_out, oz_in, lz_out, lz_in, hy_out, hy_in, hz_out, hz_in,
    r_up, r_down, r_side, r_in,
):
    me = lax.axis_index("blk")
    z, y = me // 2, me % 2
    other = z * 2 + 1 - y
    width = q_ref.shape[1]
    heads = width // HD
    tokens = q_ref.shape[0]
    scale = HD ** (-0.5)
    to_exp2 = scale * math.log2(math.e)

    def own_cols(c):
        return pl.ds(pl.multiple_of(c * width, width), width)

    loads = [
        pltpu.make_async_copy(kc_hbm, kbuf, load_sem.at[0]),
        pltpu.make_async_copy(vc_hbm, vbuf, load_sem.at[1]),
        pltpu.make_async_copy(wo_hbm, wo, load_sem.at[2]),
        pltpu.make_async_copy(cur_hbm.at[:, own_cols(me)], cur, load_sem.at[3]),
    ]
    for load in loads:
        load.start()

    barrier = pltpu.get_barrier_semaphore()
    pl.semaphore_signal(barrier, inc=1, device_id={"blk": other}, device_id_type=MESH)
    for step in range(1, ROWS):
        pl.semaphore_signal(
            barrier, inc=1, device_id={"blk": near_first(z, step) * 2 + y}, device_id_type=MESH
        )
    pl.semaphore_wait(barrier, ROWS)

    def remote(src, dst, out_sem, in_sem, device):
        return pltpu.make_async_remote_copy(
            src_ref=src, dst_ref=dst, send_sem=out_sem, recv_sem=in_sem,
            device_id={"blk": device}, device_id_type=MESH,
        )

    def spread(view, up, down, side, arrived, row, act):
        part = view(row * 2 + y)
        in_sem = arrived.at[row * 2 + y]

        @pl.when(jnp.logical_and(row <= z, z < ROWS - 1))
        def _():
            act(remote(part, part, up.at[row], in_sem, me + 2))

        @pl.when(jnp.logical_and(row >= z, z > 0))
        def _():
            act(remote(part, part, down.at[row], in_sem, me - 2))

        act(remote(part, part, side.at[row], in_sem, other))

    def start(copy):
        copy.start()

    def finish(copy):
        copy.wait_send()

    def q_view(c):
        return qall.at[c]

    def out_view(c):
        return out_ref.at[:, own_cols(c)]

    def q_spread(row, act):
        spread(q_view, q_up, q_down, q_side, q_in, row, act)

    def out_spread(row, act):
        spread(out_view, r_up, r_down, r_side, r_in, row, act)

    lanes = lax.broadcasted_iota(jnp.int32, (tokens, HD), 1)

    def one_head(q_part, k_part, v_part, bias):
        scores = lax.dot_general(
            q_part, k_part, (((1,), (1,)), ((), ())), preferred_element_type=jnp.float32
        ) + bias
        highest = jnp.max(scores, axis=-1, keepdims=True)
        weights = jnp.exp2((scores - highest) * to_exp2)
        totals = jnp.sum(weights, axis=-1, keepdims=True)
        partial = jnp.dot(
            weights.astype(jnp.bfloat16), v_part, preferred_element_type=jnp.float32
        ) / totals
        return partial.astype(jnp.bfloat16), highest * scale + jnp.log(totals)

    def y_copies(row):
        return (
            remote(oy_tx.at[row], oy_rx.at[row], oy_out.at[row], oy_in.at[row], other),
            remote(ly_tx.at[row], ly_rx.at[row], ly_out.at[row], ly_in.at[row], other),
        )

    def z_copies(row):
        peer = row * 2 + y
        return (
            remote(oz_tx.at[row], oz_rx.at[z], oz_out.at[row], oz_in.at[z], peer),
            remote(lz_tx.at[row], lz_rx.at[z], lz_out.at[row], lz_in.at[z], peer),
        )

    def merge(row, away):
        for copy in y_copies(row):
            copy.wait_recv()
        l_a, l_b = l_keep[row], head_columns(ly_rx[row])
        top = jnp.maximum(l_a, l_b)
        f_a, f_b = jnp.exp(l_a - top), jnp.exp(l_b - top)
        total = f_a + f_b
        f_a, f_b = f_a / total, f_b / total
        o_dst, l_dst, at = (oz_tx, lz_tx, row) if away else (oz_rx, lz_rx, z)
        l_dst[at] = head_rows(top + jnp.log(total))
        for h in range(heads):
            cols = slice(h * HD, (h + 1) * HD)
            o_dst[at, :, cols] = (
                f_a[:, h : h + 1] * o_keep[row, :, cols].astype(jnp.float32)
                + f_b[:, h : h + 1] * oy_rx[row, :, cols].astype(jnp.float32)
            ).astype(jnp.bfloat16)
        if away:
            for copy in z_copies(row):
                copy.start()

    qall[me] = q_ref[...]

    def visit(t, carry):
        j, second = t // 2, t % 2
        row = near_first(z, j)
        c = row * 2 + jnp.where(second == 0, y, 1 - y)

        @pl.when(t > 0)
        def _():
            remote(q_view(c), q_view(c), q_side.at[row], q_in.at[c], other).wait_recv()

        @pl.when(second == 0)
        def _():
            q_spread(row, start)

        @pl.when(t == 0)
        def _():
            loads[0].wait()
            loads[1].wait()

        group = pl.ds(pl.multiple_of(c * HD, HD), HD)
        logs = jnp.zeros((tokens, HD), jnp.float32)
        for h in range(heads):
            cols = slice(h * HD, (h + 1) * HD)
            partial, log_total = one_head(
                qall[c, :, cols], kbuf[:, group], vbuf[:, group], bias_ref[...]
            )
            logs = jnp.where(lanes == h, log_total, logs)

            @pl.when(second == 0)
            def _():
                o_keep[row, :, cols] = partial

            @pl.when(second == 1)
            def _():
                oy_tx[row, :, cols] = partial

        @pl.when(second == 0)
        def _():
            l_keep[row] = logs

        @pl.when(second == 1)
        def _():
            ly_tx[row] = head_rows(logs)
            for copy in y_copies(row):
                copy.start()

        @pl.when(t == 3)
        def _():
            merge(near_first(z, 0), False)

        @pl.when(t == 5)
        def _():
            merge(near_first(z, 1), True)

        @pl.when(t == 7)
        def _():
            merge(near_first(z, 2), True)

        return carry

    lax.fori_loop(0, 2 * ROWS, visit, 0)

    row_no = lax.broadcasted_iota(jnp.int32, (tokens, tokens), 0)
    col_no = lax.broadcasted_iota(jnp.int32, (tokens, tokens), 1)
    causal = jnp.where(row_no >= col_no, 0.0, -jnp.inf)
    own = []
    own_logs = jnp.zeros((tokens, HD), jnp.float32)
    for h in range(heads):
        partial, log_total = one_head(
            q_ref[:, h * HD : (h + 1) * HD], ok_ref[...], ov_ref[...], causal
        )
        own_logs = jnp.where(lanes == h, log_total, own_logs)
        own.append(partial)

    merge(near_first(z, 3), True)

    def from_row(row):
        return (
            remote(oz_tx.at[row], oz_rx.at[row], oz_out.at[row], oz_in.at[row], row * 2 + y),
            remote(lz_tx.at[row], lz_rx.at[row], lz_out.at[row], lz_in.at[row], row * 2 + y),
        )

    for step in range(1, ROWS):
        for copy in from_row(near_first(z, step)):
            copy.wait_recv()
    all_logs = [own_logs] + [head_columns(lz_rx[row]) for row in range(ROWS)]
    top = all_logs[0]
    for logs in all_logs[1:]:
        top = jnp.maximum(top, logs)
    factors = [jnp.exp(logs - top) for logs in all_logs]
    total = factors[0]
    for factor in factors[1:]:
        total = total + factor
    factors = [factor / total for factor in factors]
    for h in range(heads):
        cols = slice(h * HD, (h + 1) * HD)
        summed = factors[0][:, h : h + 1] * own[h].astype(jnp.float32)
        for row in range(ROWS):
            summed = summed + factors[row + 1][:, h : h + 1] * oz_rx[row, :, cols].astype(
                jnp.float32
            )
        att[:, cols] = summed.astype(jnp.bfloat16)

    def term(c):
        return jnp.dot(att[...], wo[:, own_cols(c)], preferred_element_type=jnp.float32)

    def side_terms(row):
        return remote(hy_tx.at[row], hy_rx.at[row], hy_out.at[row], hy_in.at[row], other)

    def row_terms(row, slot):
        return remote(hz_tx.at[row], hz_rx.at[slot], hz_out.at[row], hz_in.at[slot], row * 2 + y)

    loads[2].wait()
    loads[3].wait()

    def send_side(i, carry):
        row = near_first(z, ROWS - 1 - i)
        hy_tx[row] = term(row * 2 + 1 - y).astype(jnp.bfloat16)
        side_terms(row).start()
        return carry

    def keep_own(i, carry):
        row = near_first(z, ROWS - 1 - i)
        hk[row] = term(row * 2 + y)
        return carry

    lax.fori_loop(0, ROWS, send_side, 0)
    lax.fori_loop(0, ROWS, keep_own, 0)
    for step in range(ROWS - 1, 0, -1):
        row = near_first(z, step)
        side_terms(row).wait_recv()
        hz_tx[row] = (hk[row] + hy_rx[row].astype(jnp.float32)).astype(jnp.bfloat16)
        row_terms(row, z).start()
    side_terms(z).wait_recv()
    summed = cur[...].astype(jnp.float32) + hk[z] + hy_rx[z].astype(jnp.float32)
    for step in range(1, ROWS):
        row = near_first(z, step)
        row_terms(row, row).wait_recv()
        summed = summed + hz_rx[row].astype(jnp.float32)
    out_ref[:, own_cols(me)] = summed.astype(jnp.bfloat16)

    out_spread(z, start)
    for step in range(1, ROWS):
        row = near_first(z, step)
        c = row * 2 + y
        remote(out_view(c), out_view(c), r_side.at[row], r_in.at[c], other).wait_recv()
        out_spread(row, start)
    for row in range(ROWS):
        c = row * 2 + 1 - y
        remote(out_view(c), out_view(c), r_side.at[row], r_in.at[c], other).wait_recv()

    for row in range(ROWS):
        q_spread(row, finish)
        out_spread(row, finish)
        side_terms(row).wait_send()
        for copy in y_copies(row):
            copy.wait_send()
    for step in range(1, ROWS):
        row = near_first(z, step)
        for copy in z_copies(row):
            copy.wait_send()
        row_terms(row, z).wait_send()


def plane_call(queries, own_keys, own_values, bias, current, keys, values, w_out):
    tokens, width = queries.shape
    slots = keys.shape[0]
    chunk = (tokens, width)
    few = (ROWS, 8, tokens)
    bf16, f32 = jnp.bfloat16, jnp.float32
    vmem = pl.BlockSpec(memory_space=pltpu.VMEM)
    anywhere = pl.BlockSpec(memory_space=pl.ANY)
    rows_of = lambda kind: pltpu.VMEM((ROWS,) + chunk, kind)
    sems = lambda count: pltpu.SemaphoreType.DMA((count,))
    logs = pltpu.VMEM(few, f32)
    return pl.pallas_call(
        plane_kernel,
        out_shape=jax.ShapeDtypeStruct(current.shape, bf16),
        in_specs=[vmem] * 4 + [anywhere] * 4,
        out_specs=vmem,
        scratch_shapes=[
            pltpu.VMEM((2 * ROWS,) + chunk, bf16),
            pltpu.VMEM(keys.shape, bf16),
            pltpu.VMEM(values.shape, bf16),
            pltpu.VMEM(w_out.shape, bf16),
            pltpu.VMEM(chunk, bf16),
            rows_of(bf16), pltpu.VMEM((ROWS, tokens, HD), f32),
            rows_of(bf16), logs, rows_of(bf16), logs,
            rows_of(bf16), logs, rows_of(bf16), logs,
            pltpu.VMEM(chunk, bf16),
            rows_of(f32), rows_of(bf16), rows_of(bf16), rows_of(bf16), rows_of(bf16),
            sems(4),
            sems(ROWS), sems(ROWS), sems(ROWS), sems(2 * ROWS),
        ] + [sems(ROWS)] * 12 + [
            sems(ROWS), sems(ROWS), sems(ROWS), sems(2 * ROWS),
        ],
        compiler_params=pltpu.CompilerParams(
            collective_id=0, has_side_effects=True, vmem_limit_bytes=56 * 1024 * 1024
        ),
        cost_estimate=pl.CostEstimate(
            flops=4 * tokens * width * slots * 8, bytes_accessed=16 << 20,
            transcendentals=tokens * slots * 32,
        ),
    )(queries, own_keys, own_values, bias, current, keys, values, w_out)


def plane_shards(
    fresh, previous, span_index, cache_counts, norm_gain,
    w_query, w_keyval, w_out, cache_keys, cache_values,
):
    position = lax.axis_index("blk")
    span_rows = fresh.shape[0]
    arrived = passed_along(previous[0], "segment", 1)
    current = jnp.where(lax.axis_index("segment") == 0, fresh, arrived)
    widened = current.astype(jnp.float32)
    normed = (
        widened
        * lax.rsqrt(jnp.mean(widened * widened, axis=-1, keepdims=True) + EPSILON)
        * norm_gain[0]
    ).astype(jnp.bfloat16)
    first_span = span_index[0]
    width = w_query.shape[2]
    queries = jnp.dot(normed, w_query[0], preferred_element_type=jnp.float32)
    queries = rotate(queries.reshape(span_rows, width // HD, HD), first_span)
    queries = queries.astype(jnp.bfloat16).reshape(span_rows, width)
    projected = jnp.dot(normed, w_keyval[0], preferred_element_type=jnp.float32)
    own_keys = rotate(projected[:, None, :HD], first_span)[:, 0, :].astype(jnp.bfloat16)
    own_values = projected[:, HD:].astype(jnp.bfloat16)
    offsets = jnp.arange(cache_keys.shape[1], dtype=jnp.int32)
    bias = jnp.where(offsets < cache_counts[0, position], 0.0, -jnp.inf)[None, :]
    mixed = plane_call(
        queries, own_keys, own_values, bias, current,
        cache_keys[0], cache_values[0], w_out[0],
    )
    return mixed[None]


def solution(mesh):
    placed = (
        P(),
        P("segment", None, None),
        P("segment"),
        P("segment", None),
        P("segment", None),
        P("segment", None, "blk"),
        P("segment", None, "blk"),
        P("segment", "blk", None),
        P("segment", "blk", None),
        P("segment", "blk", None),
    )
    body = plane_shards if mesh.shape["blk"] == KVH else shards
    return jax.shard_map(
        body, mesh=mesh, in_specs=placed, out_specs=P("segment", None, None), check_vma=False
    )
```

```python
import math

import jax
import jax.numpy as jnp
from jax import lax
from jax.experimental import pallas as pl
from jax.experimental.pallas import tpu as pltpu
from jax.sharding import PartitionSpec as P

KVH = 8
HD = 128


ROPE_BASE = 500000.0
EPSILON = 1e-05


def passed_along(block, axis, distance):
    devices = range(lax.axis_size(axis))
    route = [(i - distance, i) for i in devices if i - distance in devices]
    return lax.ppermute(block, axis, route)


def swapped(block, axis, distance):
    count = lax.axis_size(axis)
    route = []
    for low in range(count):
        high = low | 1 << distance
        if high != low and high < count:
            route += [(low, high), (high, low)]
    return lax.ppermute(block, axis, route)


def rotate(projected, first_span):
    length = projected.shape[0]
    half_width = projected.shape[-1] // 2
    positions = (first_span * length + jnp.arange(length, dtype=jnp.int32)).astype(jnp.float32)
    inverse = ROPE_BASE ** (
        -(jnp.arange(half_width, dtype=jnp.float32) * 2.0) / projected.shape[-1]
    )
    angles = positions[:, None] * inverse[None, :]
    cosine = jnp.cos(angles)[:, None, :]
    sine_table = jnp.sin(angles)[:, None, :]
    left_part = projected[..., :half_width]
    right_part = projected[..., half_width:]
    return jnp.concatenate(
        [
            left_part * cosine - right_part * sine_table,
            right_part * cosine + left_part * sine_table,
        ],
        axis=-1,
    )


def attend_rows(query_rows, key_rows, value_rows, allowed):
    scores = lax.dot_general(
        query_rows, key_rows, (((1,), (1,)), ((), ())), preferred_element_type=jnp.float32
    ) * query_rows.shape[-1] ** (-0.5)
    scores = jnp.where(allowed, scores, -jnp.inf)
    highest = jnp.max(scores, axis=-1, keepdims=True)
    weights = jnp.exp(scores - highest)
    totals = jnp.sum(weights, axis=-1, keepdims=True)
    partial_out = (
        jnp.dot(weights.astype(jnp.bfloat16), value_rows, preferred_element_type=jnp.float32)
        / totals
    ).astype(jnp.bfloat16)
    return (partial_out, (highest + jnp.log(totals))[:, 0])


def shards(
    fresh,
    previous,
    span_index,
    cache_counts,
    norm_gain,
    w_query,
    w_keyval,
    w_out,
    cache_keys,
    cache_values,
):
    blocks = lax.axis_size("blk")
    position = lax.axis_index("blk")
    span_rows = fresh.shape[0]
    arrived = passed_along(previous[0], "segment", 1)
    current = jnp.where(lax.axis_index("segment") == 0, fresh, arrived)
    widened = current.astype(jnp.float32)
    normed = (
        widened
        * lax.rsqrt(jnp.mean(widened * widened, axis=-1, keepdims=True) + EPSILON)
        * norm_gain[0]
    ).astype(jnp.bfloat16)
    first_span = span_index[0]
    heads_here = w_query.shape[2] // HD
    ratio = blocks // KVH
    queries = jnp.dot(normed, w_query[0], preferred_element_type=jnp.float32).reshape(
        span_rows, heads_here, HD
    )
    queries = rotate(queries, first_span).astype(jnp.bfloat16).reshape(span_rows, heads_here * HD)
    projected = jnp.dot(normed, w_keyval[0], preferred_element_type=jnp.float32)
    if ratio == 2:
        odd_member = position % 2 == 1
        as_key = rotate(projected[:, None, :], first_span)[:, 0, :].astype(jnp.bfloat16)
        mine = jnp.where(odd_member, projected.astype(jnp.bfloat16), as_key)
        partner = swapped(mine, "blk", 0)
        own_keys = jnp.where(odd_member, partner, mine)
        own_values = jnp.where(odd_member, mine, partner)
    else:
        own_keys = rotate(projected[:, None, :HD], first_span)[:, 0, :].astype(jnp.bfloat16)
        own_values = projected[:, HD:].astype(jnp.bfloat16)
    query_rows = queries.reshape(span_rows * heads_here, HD)
    row_tokens = jnp.arange(span_rows * heads_here, dtype=jnp.int32) // heads_here
    causal = row_tokens[:, None] >= jnp.arange(span_rows, dtype=jnp.int32)[None, :]
    own_out, own_log = attend_rows(query_rows, own_keys, own_values, causal)
    own_out = own_out.reshape(span_rows, heads_here * HD)
    own_log = own_log.reshape(span_rows, heads_here).T
    cache_rows = cache_keys.shape[1]
    offsets = jnp.arange(cache_rows, dtype=jnp.int32)
    every_query = lax.all_gather(queries, "blk", axis=0, tiled=True)
    live = cache_counts[0, position]

    def holder(source):
        query_block = lax.dynamic_slice_in_dim(
            every_query, source * span_rows, span_rows, 0
        ).reshape(span_rows * heads_here, HD)
        head_start = source // ratio * HD
        key_rows = lax.dynamic_slice_in_dim(cache_keys[0], head_start, HD, 1)
        value_rows = lax.dynamic_slice_in_dim(cache_values[0], head_start, HD, 1)
        partial_out, log_totals = attend_rows(
            query_block, key_rows, value_rows, (offsets < live)[None, :]
        )
        return (
            partial_out.reshape(span_rows, heads_here * HD),
            log_totals.reshape(span_rows, heads_here).T,
        )

    held_outs, held_logs = lax.map(holder, jnp.arange(blocks, dtype=jnp.int32))
    shard_outs = lax.all_to_all(held_outs, "blk", split_axis=0, concat_axis=0, tiled=True)
    shard_logs = lax.all_to_all(held_logs, "blk", split_axis=0, concat_axis=0, tiled=True)
    all_outs = (
        jnp.concatenate([own_out[None], shard_outs], axis=0)
        .astype(jnp.float32)
        .reshape(blocks + 1, span_rows, heads_here, HD)
    )
    all_logs = jnp.concatenate([own_log[None], shard_logs], axis=0).transpose(0, 2, 1)
    ceiling = jnp.max(all_logs, axis=0)
    factors = jnp.exp(all_logs - ceiling)
    attended = (
        jnp.sum(factors[..., None] * all_outs, axis=0) / jnp.sum(factors, axis=0)[..., None]
    ).astype(jnp.bfloat16)
    attended = attended.reshape(span_rows, heads_here * HD)
    head_terms = lax.optimization_barrier(
        jnp.dot(attended, w_out[0], preferred_element_type=jnp.float32).astype(jnp.bfloat16)
    ).astype(jnp.float32)
    summed = lax.psum(head_terms.astype(jnp.bfloat16), "blk").astype(jnp.float32)
    mixed = (widened + summed).astype(jnp.bfloat16)
    return mixed[None]


ROWS = 4
PIECES = 8
MESH = pl.DeviceIdType.MESH


def near_first(z, step):
    half = z // 2
    if isinstance(step, int):
        return (z, z + 1 - 2 * (z % 2), 2 - half, 3 - 3 * half)[step]
    pair = z + 1 - 2 * (z % 2)
    later = jnp.where(step == 2, 2 - half, 3 - 3 * half)
    return jnp.where(step == 0, z, jnp.where(step == 1, pair, later))


def plane_kernel(
    counts_ref, gain_ref, cos_ref, sin_ref, fresh_hbm, prev_hbm, wq_hbm, wkv_hbm,
    kc_hbm, vc_hbm, wo_hbm, out_ref,
    cur, normed, wq, wkv, own_k, own_v, bias,
    qall, kbuf, vbuf, wo, parts, logs, oy_rx, ly_rx,
    oz_tx, lz_tx, oz_rx, lz_rx, att, hk, hy_tx, hy_rx, hz_tx, hz_rx,
    load_sem, x_out, x_side, x_in, q_up, q_down, q_side, q_in, oy_out, oy_in, ly_out, ly_in,
    oz_out, oz_in, lz_out, lz_in, hy_out, hy_in, hz_out, hz_in,
    r_up, r_down, r_side, r_in,
):
    me = lax.axis_index("blk")
    layer = lax.axis_index("segment")
    layers = lax.axis_size("segment")
    z, y = me // 2, me % 2
    other = z * 2 + 1 - y
    tokens, width = qall.shape[1:]
    heads = width // HD
    to_log2 = HD ** (-0.5) * math.log2(math.e)
    piece = tokens // PIECES

    def own_cols(c):
        return pl.ds(pl.multiple_of(c * width, width), width)

    loads = [
        pltpu.make_async_copy(wq_hbm, wq, load_sem.at[0]),
        pltpu.make_async_copy(wkv_hbm, wkv, load_sem.at[1]),
        pltpu.make_async_copy(kc_hbm, kbuf, load_sem.at[2]),
        pltpu.make_async_copy(vc_hbm, vbuf, load_sem.at[3]),
        pltpu.make_async_copy(wo_hbm, wo, load_sem.at[4]),
    ]
    fresh_load = pltpu.make_async_copy(fresh_hbm, cur, load_sem.at[5])

    @pl.when(layer == 0)
    def _():
        fresh_load.start()

    for load in loads:
        load.start()

    has_source, has_next = layer > 0, layer < layers - 1
    barrier = pltpu.get_barrier_semaphore()
    pl.semaphore_signal(barrier, inc=1, device_id={"blk": other}, device_id_type=MESH)
    for step in range(1, ROWS):
        pl.semaphore_signal(
            barrier, inc=1, device_id={"blk": near_first(z, step) * 2 + y}, device_id_type=MESH
        )

    @pl.when(has_source)
    def _():
        pl.semaphore_signal(
            barrier, inc=1, device_id={"segment": layer - 1}, device_id_type=MESH
        )

    @pl.when(has_next)
    def _():
        pl.semaphore_signal(
            barrier, inc=1, device_id={"segment": layer + 1}, device_id_type=MESH
        )

    pl.semaphore_wait(
        barrier, ROWS + has_source.astype(jnp.int32) + has_next.astype(jnp.int32)
    )

    def remote(src, dst, out_sem, in_sem, device):
        return pltpu.make_async_remote_copy(
            src_ref=src, dst_ref=dst, send_sem=out_sem, recv_sem=in_sem,
            device_id={"blk": device}, device_id_type=MESH,
        )

    def rows_of_piece(p):
        return pl.ds(pl.multiple_of(p * piece, piece), piece)

    def shift_copy(p):
        rows = rows_of_piece(p)
        return pltpu.make_async_remote_copy(
            src_ref=prev_hbm.at[rows], dst_ref=cur.at[rows],
            send_sem=x_out.at[p], recv_sem=x_in.at[p],
            device_id={"segment": layer + 1}, device_id_type=MESH,
        )

    def shift_side(p):
        rows = rows_of_piece(p)
        return remote(cur.at[rows], cur.at[rows], x_side.at[p], x_in.at[p], other)

    def piece_at(i):
        return (y * (PIECES // 2) + i) % PIECES

    to_core = layer % 2 == 0
    takes_half = jnp.logical_and(has_source, to_core)

    def each_shift(act):
        def step(i, carry):
            @pl.when(jnp.logical_and(has_next, jnp.logical_or(to_core, i < PIECES // 2)))
            def _():
                act(shift_copy(piece_at(i)))

            return carry

        lax.fori_loop(0, PIECES, step, 0)

    def spread(view, up, down, side, arrived, row, act):
        part = view(row * 2 + y)
        in_sem = arrived.at[row * 2 + y]

        @pl.when(jnp.logical_and(row <= z, z < ROWS - 1))
        def _():
            act(remote(part, part, up.at[row], in_sem, me + 2))

        @pl.when(jnp.logical_and(row >= z, z > 0))
        def _():
            act(remote(part, part, down.at[row], in_sem, me - 2))

        act(remote(part, part, side.at[row], in_sem, other))

    def start(copy):
        copy.start()

    def finish(copy):
        copy.wait_send()

    each_shift(start)

    def q_view(c):
        return qall.at[c]

    def out_view(c):
        return out_ref.at[:, own_cols(c)]

    def q_spread(row, act):
        spread(q_view, q_up, q_down, q_side, q_in, row, act)

    def out_spread(row, act):
        spread(out_view, r_up, r_down, r_side, r_in, row, act)

    slot_no = lax.broadcasted_iota(jnp.int32, bias.shape, 0)
    bias[...] = jnp.where(slot_no < counts_ref[0, me], 0.0, -jnp.inf)

    def normalize(i, carry):
        p = piece_at(i)

        @pl.when(has_source)
        def _():
            shift_side(p).wait_recv()

        @pl.when(jnp.logical_and(takes_half, i < PIECES // 2))
        def _():
            shift_side(p).start()

        @pl.when(jnp.logical_and(layer == 0, i == 0))
        def _():
            fresh_load.wait()

        rows = rows_of_piece(p)
        widened = cur[rows, :].astype(jnp.float32)
        normed[rows, :] = (
            widened
            * lax.rsqrt(jnp.mean(widened * widened, axis=-1, keepdims=True) + EPSILON)
            * gain_ref[...]
        ).astype(jnp.bfloat16)
        return carry

    lax.fori_loop(0, PIECES, normalize, 0)

    def rotated(part):
        half = HD // 2
        turned = jnp.concatenate([part[:, half:], part[:, :half]], axis=1)
        return part * cos_ref[...] + turned * sin_ref[...]

    loads[0].wait()
    projected = jnp.dot(normed[...], wq[...], preferred_element_type=jnp.float32)
    for h in range(heads):
        cols = slice(h * HD, (h + 1) * HD)
        qall[me, :, cols] = (rotated(projected[:, cols]) * to_log2).astype(jnp.bfloat16)

    def one_head(k_part, q_part, v_turned, masked):
        scores = lax.dot_general(
            k_part, q_part, (((1,), (1,)), ((), ())), preferred_element_type=jnp.float32
        ) + masked
        highest = jnp.max(scores, axis=0, keepdims=True)
        weights = jnp.exp2(scores - highest).astype(jnp.bfloat16)
        mixed = jnp.dot(v_turned, weights, preferred_element_type=jnp.float32)
        totals = mixed[HD : HD + 1]
        partial = (mixed[:HD] / totals).astype(jnp.bfloat16)
        return partial, highest + jnp.log2(totals)

    def with_ones(v_part):
        return jnp.concatenate(
            [v_part.T, jnp.ones((16, v_part.shape[0]), jnp.bfloat16)], axis=0
        )

    def log_rows(rows):
        return jnp.concatenate(rows + [jnp.zeros((8 - heads, tokens), jnp.float32)], axis=0)

    def y_copies(row):
        return (
            remote(parts.at[ROWS + row], oy_rx.at[row], oy_out.at[row], oy_in.at[row], other),
            remote(logs.at[ROWS + row], ly_rx.at[row], ly_out.at[row], ly_in.at[row], other),
        )

    def z_copies(row):
        peer = row * 2 + y
        return (
            remote(oz_tx.at[row], oz_rx.at[z], oz_out.at[row], oz_in.at[z], peer),
            remote(lz_tx.at[row], lz_rx.at[z], lz_out.at[row], lz_in.at[z], peer),
        )

    def merge(row, away):
        for copy in y_copies(row):
            copy.wait_recv()
        l_a, l_b = logs[row], ly_rx[row]
        top = jnp.maximum(l_a, l_b)
        f_a, f_b = jnp.exp2(l_a - top), jnp.exp2(l_b - top)
        total = f_a + f_b
        f_a, f_b = f_a / total, f_b / total
        o_dst, l_dst, at = (oz_tx, lz_tx, row) if away else (oz_rx, lz_rx, z)
        l_dst[at] = top + jnp.log2(total)
        for h in range(heads):
            part = slice(h * HD, (h + 1) * HD)
            o_dst[at, part, :] = (
                f_a[h : h + 1] * parts[row, part, :].astype(jnp.float32)
                + f_b[h : h + 1] * oy_rx[row, part, :].astype(jnp.float32)
            ).astype(jnp.bfloat16)
        if away:
            for copy in z_copies(row):
                copy.start()

    def visit(t, carry):
        j, second = t // 2, t % 2
        row = near_first(z, j)
        c = row * 2 + jnp.where(second == 0, y, 1 - y)

        @pl.when(t > 0)
        def _():
            remote(q_view(c), q_view(c), q_side.at[row], q_in.at[c], other).wait_recv()

        @pl.when(second == 0)
        def _():
            q_spread(row, start)

        @pl.when(t == 0)
        def _():
            loads[1].wait()
            both = jnp.dot(normed[...], wkv[...], preferred_element_type=jnp.float32)
            own_k[...] = rotated(both[:, :HD]).astype(jnp.bfloat16)
            own_v[...] = both[:, HD:].astype(jnp.bfloat16)
            loads[2].wait()
            loads[3].wait()

        group = pl.ds(pl.multiple_of(c * HD, HD), HD)
        k_part, v_turned = kbuf[:, group], with_ones(vbuf[:, group])
        masked = jnp.concatenate([bias[...]] * (tokens // HD), axis=1)
        to = second * ROWS + row
        totals = []
        for h in range(heads):
            partial, log_total = one_head(
                k_part, qall[c, :, h * HD : (h + 1) * HD], v_turned, masked
            )
            parts[to, h * HD : (h + 1) * HD, :] = partial
            totals.append(log_total)
        logs[to] = log_rows(totals)

        @pl.when(second == 1)
        def _():
            for copy in y_copies(row):
                copy.start()

        @pl.when(t == 3)
        def _():
            merge(near_first(z, 0), False)

        @pl.when(t == 5)
        def _():
            merge(near_first(z, 1), True)

        @pl.when(t == 7)
        def _():
            merge(near_first(z, 2), True)

        return carry

    lax.fori_loop(0, 2 * ROWS, visit, 0)

    key_no = lax.broadcasted_iota(jnp.int32, (tokens, tokens), 0)
    token_no = lax.broadcasted_iota(jnp.int32, (tokens, tokens), 1)
    causal = jnp.where(token_no >= key_no, 0.0, -jnp.inf)
    own, own_logs = [], []
    own_turned = with_ones(own_v[...])
    for h in range(heads):
        partial, log_total = one_head(
            own_k[...], qall[me, :, h * HD : (h + 1) * HD], own_turned, causal
        )
        own_logs.append(log_total)
        own.append(partial)

    merge(near_first(z, 3), True)

    def from_row(row):
        return (
            remote(oz_tx.at[row], oz_rx.at[row], oz_out.at[row], oz_in.at[row], row * 2 + y),
            remote(lz_tx.at[row], lz_rx.at[row], lz_out.at[row], lz_in.at[row], row * 2 + y),
        )

    for step in range(1, ROWS):
        for copy in from_row(near_first(z, step)):
            copy.wait_recv()
    all_logs = [log_rows(own_logs)] + [lz_rx[row] for row in range(ROWS)]
    top = all_logs[0]
    for log_total in all_logs[1:]:
        top = jnp.maximum(top, log_total)
    factors = [jnp.exp2(log_total - top) for log_total in all_logs]
    total = factors[0]
    for factor in factors[1:]:
        total = total + factor
    factors = [factor / total for factor in factors]
    for h in range(heads):
        part = slice(h * HD, (h + 1) * HD)
        summed = factors[0][h : h + 1] * own[h].astype(jnp.float32)
        for row in range(ROWS):
            summed = summed + factors[row + 1][h : h + 1] * oz_rx[row, part, :].astype(
                jnp.float32
            )
        att[:, part] = summed.T.astype(jnp.bfloat16)

    def term(c):
        return jnp.dot(att[...], wo[:, own_cols(c)], preferred_element_type=jnp.float32)

    def side_terms(row):
        return remote(hy_tx.at[row], hy_rx.at[row], hy_out.at[row], hy_in.at[row], other)

    def row_terms(row, slot):
        return remote(hz_tx.at[row], hz_rx.at[slot], hz_out.at[row], hz_in.at[slot], row * 2 + y)

    loads[4].wait()

    def send_side(i, carry):
        row = near_first(z, ROWS - 1 - i)
        hy_tx[row] = term(row * 2 + 1 - y).astype(jnp.bfloat16)
        side_terms(row).start()
        return carry

    def keep_own(i, carry):
        row = near_first(z, ROWS - 1 - i)
        hk[row] = term(row * 2 + y)
        return carry

    lax.fori_loop(0, ROWS, send_side, 0)
    lax.fori_loop(0, ROWS, keep_own, 0)
    for step in range(ROWS - 1, 0, -1):
        row = near_first(z, step)
        side_terms(row).wait_recv()
        hz_tx[row] = (hk[row] + hy_rx[row].astype(jnp.float32)).astype(jnp.bfloat16)
        row_terms(row, z).start()
    side_terms(z).wait_recv()
    summed = cur[:, own_cols(me)].astype(jnp.float32) + hk[z] + hy_rx[z].astype(jnp.float32)
    for step in range(1, ROWS):
        row = near_first(z, step)
        row_terms(row, row).wait_recv()
        summed = summed + hz_rx[row].astype(jnp.float32)
    out_ref[:, own_cols(me)] = summed.astype(jnp.bfloat16)

    out_spread(z, start)
    for step in range(1, ROWS):
        row = near_first(z, step)
        c = row * 2 + y
        remote(out_view(c), out_view(c), r_side.at[row], r_in.at[c], other).wait_recv()
        out_spread(row, start)
    for row in range(ROWS):
        c = row * 2 + 1 - y
        remote(out_view(c), out_view(c), r_side.at[row], r_in.at[c], other).wait_recv()

    each_shift(finish)

    def side_done(i, carry):
        @pl.when(takes_half)
        def _():
            shift_side(piece_at(i)).wait_send()

        return carry

    lax.fori_loop(0, PIECES // 2, side_done, 0)
    for row in range(ROWS):
        q_spread(row, finish)
        out_spread(row, finish)
        side_terms(row).wait_send()
        for copy in y_copies(row):
            copy.wait_send()
    for step in range(1, ROWS):
        row = near_first(z, step)
        for copy in z_copies(row):
            copy.wait_send()
        row_terms(row, z).wait_send()


def plane_call(counts, gain, cosine, sine, fresh, previous, w_query, w_keyval, keys, values, w_out):
    tokens, features = fresh.shape
    width = w_query.shape[1]
    slots = keys.shape[0]
    bf16, f32 = jnp.bfloat16, jnp.float32
    vmem = pl.BlockSpec(memory_space=pltpu.VMEM)
    anywhere = pl.BlockSpec(memory_space=pl.ANY)
    turned = lambda count: pltpu.VMEM((count, width, tokens), bf16)
    chunks = lambda count, kind: pltpu.VMEM((count, tokens, width), kind)
    logs = lambda count: pltpu.VMEM((count, 8, tokens), f32)
    sems = lambda count: pltpu.SemaphoreType.DMA((count,))
    like = lambda array: pltpu.VMEM(array.shape, array.dtype)
    return pl.pallas_call(
        plane_kernel,
        out_shape=jax.ShapeDtypeStruct(fresh.shape, bf16),
        in_specs=[pl.BlockSpec(memory_space=pltpu.SMEM)] + [vmem] * 3 + [anywhere] * 7,
        out_specs=vmem,
        scratch_shapes=[
            like(fresh), like(fresh), like(w_query), like(w_keyval),
            pltpu.VMEM((tokens, HD), bf16), pltpu.VMEM((tokens, HD), bf16),
            pltpu.VMEM((slots, HD), f32),
            chunks(2 * ROWS, bf16), like(keys), like(values), like(w_out),
            turned(2 * ROWS), logs(2 * ROWS), turned(ROWS), logs(ROWS),
            turned(ROWS), logs(ROWS), turned(ROWS), logs(ROWS),
            pltpu.VMEM((tokens, width), bf16),
            chunks(ROWS, f32), chunks(ROWS, bf16), chunks(ROWS, bf16),
            chunks(ROWS, bf16), chunks(ROWS, bf16),
            sems(6), sems(PIECES), sems(PIECES), sems(PIECES),
            sems(ROWS), sems(ROWS), sems(ROWS), sems(2 * ROWS),
        ] + [sems(ROWS)] * 12 + [
            sems(ROWS), sems(ROWS), sems(ROWS), sems(2 * ROWS),
        ],
        compiler_params=pltpu.CompilerParams(
            collective_id=0, has_side_effects=True, vmem_limit_bytes=60 * 1024 * 1024
        ),
        cost_estimate=pl.CostEstimate(
            flops=4 * tokens * width * slots * 8, bytes_accessed=20 << 20,
            transcendentals=tokens * slots * 32,
        ),
    )(counts, gain, cosine, sine, fresh, previous, w_query, w_keyval, keys, values, w_out)


def plane_shards(
    fresh, previous, span_index, cache_counts, norm_gain,
    w_query, w_keyval, w_out, cache_keys, cache_values,
):
    length = fresh.shape[0]
    half_width = HD // 2
    positions = (span_index[0] * length + jnp.arange(length, dtype=jnp.int32)).astype(jnp.float32)
    inverse = ROPE_BASE ** (-(jnp.arange(half_width, dtype=jnp.float32) * 2.0) / HD)
    angles = positions[:, None] * inverse[None, :]
    cosine, sine = jnp.cos(angles), jnp.sin(angles)
    mixed = plane_call(
        cache_counts, norm_gain,
        jnp.concatenate([cosine, cosine], axis=1), jnp.concatenate([-sine, sine], axis=1),
        fresh, previous[0], w_query[0], w_keyval[0], cache_keys[0], cache_values[0], w_out[0],
    )
    return mixed[None]


def solution(mesh):
    placed = (
        P(),
        P("segment", None, None),
        P("segment"),
        P("segment", None),
        P("segment", None),
        P("segment", None, "blk"),
        P("segment", None, "blk"),
        P("segment", "blk", None),
        P("segment", "blk", None),
        P("segment", "blk", None),
    )
    body = plane_shards if mesh.shape["blk"] == KVH else shards
    return jax.shard_map(
        body, mesh=mesh, in_specs=placed, out_specs=P("segment", None, None), check_vma=False
    )
```

```python
import math

import jax
import jax.numpy as jnp
from jax import lax
from jax.experimental import pallas as pl
from jax.experimental.pallas import tpu as pltpu
from jax.sharding import PartitionSpec as P

KVH = 8
HD = 128


ROPE_BASE = 500000.0
EPSILON = 1e-05


def passed_along(block, axis, distance):
    devices = range(lax.axis_size(axis))
    route = [(i - distance, i) for i in devices if i - distance in devices]
    return lax.ppermute(block, axis, route)


def swapped(block, axis, distance):
    count = lax.axis_size(axis)
    route = []
    for low in range(count):
        high = low | 1 << distance
        if high != low and high < count:
            route += [(low, high), (high, low)]
    return lax.ppermute(block, axis, route)


def rotate(projected, first_span):
    length = projected.shape[0]
    half_width = projected.shape[-1] // 2
    positions = (first_span * length + jnp.arange(length, dtype=jnp.int32)).astype(jnp.float32)
    inverse = ROPE_BASE ** (
        -(jnp.arange(half_width, dtype=jnp.float32) * 2.0) / projected.shape[-1]
    )
    angles = positions[:, None] * inverse[None, :]
    cosine = jnp.cos(angles)[:, None, :]
    sine_table = jnp.sin(angles)[:, None, :]
    left_part = projected[..., :half_width]
    right_part = projected[..., half_width:]
    return jnp.concatenate(
        [
            left_part * cosine - right_part * sine_table,
            right_part * cosine + left_part * sine_table,
        ],
        axis=-1,
    )


def attend_rows(query_rows, key_rows, value_rows, allowed):
    scores = lax.dot_general(
        query_rows, key_rows, (((1,), (1,)), ((), ())), preferred_element_type=jnp.float32
    ) * query_rows.shape[-1] ** (-0.5)
    scores = jnp.where(allowed, scores, -jnp.inf)
    highest = jnp.max(scores, axis=-1, keepdims=True)
    weights = jnp.exp(scores - highest)
    totals = jnp.sum(weights, axis=-1, keepdims=True)
    partial_out = (
        jnp.dot(weights.astype(jnp.bfloat16), value_rows, preferred_element_type=jnp.float32)
        / totals
    ).astype(jnp.bfloat16)
    return (partial_out, (highest + jnp.log(totals))[:, 0])


def shards(
    fresh,
    previous,
    span_index,
    cache_counts,
    norm_gain,
    w_query,
    w_keyval,
    w_out,
    cache_keys,
    cache_values,
):
    blocks = lax.axis_size("blk")
    position = lax.axis_index("blk")
    span_rows = fresh.shape[0]
    arrived = passed_along(previous[0], "segment", 1)
    current = jnp.where(lax.axis_index("segment") == 0, fresh, arrived)
    widened = current.astype(jnp.float32)
    normed = (
        widened
        * lax.rsqrt(jnp.mean(widened * widened, axis=-1, keepdims=True) + EPSILON)
        * norm_gain[0]
    ).astype(jnp.bfloat16)
    first_span = span_index[0]
    heads_here = w_query.shape[2] // HD
    ratio = blocks // KVH
    queries = jnp.dot(normed, w_query[0], preferred_element_type=jnp.float32).reshape(
        span_rows, heads_here, HD
    )
    queries = rotate(queries, first_span).astype(jnp.bfloat16).reshape(span_rows, heads_here * HD)
    projected = jnp.dot(normed, w_keyval[0], preferred_element_type=jnp.float32)
    if ratio == 2:
        odd_member = position % 2 == 1
        as_key = rotate(projected[:, None, :], first_span)[:, 0, :].astype(jnp.bfloat16)
        mine = jnp.where(odd_member, projected.astype(jnp.bfloat16), as_key)
        partner = swapped(mine, "blk", 0)
        own_keys = jnp.where(odd_member, partner, mine)
        own_values = jnp.where(odd_member, mine, partner)
    else:
        own_keys = rotate(projected[:, None, :HD], first_span)[:, 0, :].astype(jnp.bfloat16)
        own_values = projected[:, HD:].astype(jnp.bfloat16)
    query_rows = queries.reshape(span_rows * heads_here, HD)
    row_tokens = jnp.arange(span_rows * heads_here, dtype=jnp.int32) // heads_here
    causal = row_tokens[:, None] >= jnp.arange(span_rows, dtype=jnp.int32)[None, :]
    own_out, own_log = attend_rows(query_rows, own_keys, own_values, causal)
    own_out = own_out.reshape(span_rows, heads_here * HD)
    own_log = own_log.reshape(span_rows, heads_here).T
    cache_rows = cache_keys.shape[1]
    offsets = jnp.arange(cache_rows, dtype=jnp.int32)
    every_query = lax.all_gather(queries, "blk", axis=0, tiled=True)
    live = cache_counts[0, position]

    def holder(source):
        query_block = lax.dynamic_slice_in_dim(
            every_query, source * span_rows, span_rows, 0
        ).reshape(span_rows * heads_here, HD)
        head_start = source // ratio * HD
        key_rows = lax.dynamic_slice_in_dim(cache_keys[0], head_start, HD, 1)
        value_rows = lax.dynamic_slice_in_dim(cache_values[0], head_start, HD, 1)
        partial_out, log_totals = attend_rows(
            query_block, key_rows, value_rows, (offsets < live)[None, :]
        )
        return (
            partial_out.reshape(span_rows, heads_here * HD),
            log_totals.reshape(span_rows, heads_here).T,
        )

    held_outs, held_logs = lax.map(holder, jnp.arange(blocks, dtype=jnp.int32))
    shard_outs = lax.all_to_all(held_outs, "blk", split_axis=0, concat_axis=0, tiled=True)
    shard_logs = lax.all_to_all(held_logs, "blk", split_axis=0, concat_axis=0, tiled=True)
    all_outs = (
        jnp.concatenate([own_out[None], shard_outs], axis=0)
        .astype(jnp.float32)
        .reshape(blocks + 1, span_rows, heads_here, HD)
    )
    all_logs = jnp.concatenate([own_log[None], shard_logs], axis=0).transpose(0, 2, 1)
    ceiling = jnp.max(all_logs, axis=0)
    factors = jnp.exp(all_logs - ceiling)
    attended = (
        jnp.sum(factors[..., None] * all_outs, axis=0) / jnp.sum(factors, axis=0)[..., None]
    ).astype(jnp.bfloat16)
    attended = attended.reshape(span_rows, heads_here * HD)
    head_terms = lax.optimization_barrier(
        jnp.dot(attended, w_out[0], preferred_element_type=jnp.float32).astype(jnp.bfloat16)
    ).astype(jnp.float32)
    summed = lax.psum(head_terms.astype(jnp.bfloat16), "blk").astype(jnp.float32)
    mixed = (widened + summed).astype(jnp.bfloat16)
    return mixed[None]


ROWS = 4
PIECES = 8
BLOCKS = 4
FINE = 4
DEAD = -1e30
MESH = pl.DeviceIdType.MESH


def near_first(z, step):
    half = z // 2
    if isinstance(step, int):
        return (z, z + 1 - 2 * (z % 2), 2 - half, 3 - 3 * half)[step]
    pair = z + 1 - 2 * (z % 2)
    later = jnp.where(step == 2, 2 - half, 3 - 3 * half)
    return jnp.where(step == 0, z, jnp.where(step == 1, pair, later))


def plane_kernel(
    counts_ref, gain_ref, cos_ref, sin_ref, fresh_hbm, prev_hbm, wq_hbm, wkv_hbm,
    kc_hbm, vc_hbm, wo_hbm, out_ref,
    cur, normed, wq, wkv, own_k, own_v, hidden, s_buf, p_buf, v_turn,
    qall, kbuf, vbuf, wo, parts, logs, oy_rx, ly_rx,
    oz_tx, lz_tx, oz_rx, lz_rx, att, hk, hy_tx, hy_rx, hz_tx, hz_rx,
    load_sem, x_out, x_side, x_in, q_up, q_down, q_side, q_in, oy_out, oy_in, ly_out, ly_in,
    oz_out, oz_in, lz_out, lz_in, hy_out, hy_in, hz_out, hz_in,
    r_up, r_down, r_side, r_in,
):
    me = lax.axis_index("blk")
    layer = lax.axis_index("segment")
    layers = lax.axis_size("segment")
    z, y = me // 2, me % 2
    other = z * 2 + 1 - y
    tokens, width = qall.shape[1:]
    heads = width // HD
    to_log2 = HD ** (-0.5) * math.log2(math.e)
    piece = tokens // PIECES

    def own_cols(c):
        return pl.ds(pl.multiple_of(c * width, width), width)

    loads = [
        pltpu.make_async_copy(wq_hbm, wq, load_sem.at[0]),
        pltpu.make_async_copy(wkv_hbm, wkv, load_sem.at[1]),
        pltpu.make_async_copy(kc_hbm, kbuf, load_sem.at[2]),
        pltpu.make_async_copy(vc_hbm, vbuf, load_sem.at[3]),
        pltpu.make_async_copy(wo_hbm, wo, load_sem.at[4]),
    ]
    fresh_load = pltpu.make_async_copy(fresh_hbm, cur, load_sem.at[5])

    @pl.when(layer == 0)
    def _():
        fresh_load.start()

    for load in loads:
        load.start()

    has_source, has_next = layer > 0, layer < layers - 1
    barrier = pltpu.get_barrier_semaphore()
    pl.semaphore_signal(barrier, inc=1, device_id={"blk": other}, device_id_type=MESH)
    for step in range(1, ROWS):
        pl.semaphore_signal(
            barrier, inc=1, device_id={"blk": near_first(z, step) * 2 + y}, device_id_type=MESH
        )

    @pl.when(has_source)
    def _():
        pl.semaphore_signal(
            barrier, inc=1, device_id={"segment": layer - 1}, device_id_type=MESH
        )

    @pl.when(has_next)
    def _():
        pl.semaphore_signal(
            barrier, inc=1, device_id={"segment": layer + 1}, device_id_type=MESH
        )

    pl.semaphore_wait(
        barrier, ROWS + has_source.astype(jnp.int32) + has_next.astype(jnp.int32)
    )

    def remote(src, dst, out_sem, in_sem, device):
        return pltpu.make_async_remote_copy(
            src_ref=src, dst_ref=dst, send_sem=out_sem, recv_sem=in_sem,
            device_id={"blk": device}, device_id_type=MESH,
        )

    def rows_of_piece(p):
        return pl.ds(pl.multiple_of(p * piece, piece), piece)

    def shift_copy(p):
        rows = rows_of_piece(p)
        return pltpu.make_async_remote_copy(
            src_ref=prev_hbm.at[rows], dst_ref=cur.at[rows],
            send_sem=x_out.at[p], recv_sem=x_in.at[p],
            device_id={"segment": layer + 1}, device_id_type=MESH,
        )

    def shift_side(p):
        rows = rows_of_piece(p)
        return remote(cur.at[rows], cur.at[rows], x_side.at[p], x_in.at[p], other)

    def piece_at(i):
        return (y * (PIECES // 2) + i) % PIECES

    to_core = layer % 2 == 0
    takes_half = jnp.logical_and(has_source, to_core)

    def each_shift(act):
        def step(i, carry):
            @pl.when(jnp.logical_and(has_next, jnp.logical_or(to_core, i < PIECES // 2)))
            def _():
                act(shift_copy(piece_at(i)))

            return carry

        lax.fori_loop(0, PIECES, step, 0)

    def spread(view, up, down, side, arrived, row, act):
        part = view(row * 2 + y)
        in_sem = arrived.at[row * 2 + y]

        @pl.when(jnp.logical_and(row <= z, z < ROWS - 1))
        def _():
            act(remote(part, part, up.at[row], in_sem, me + 2))

        @pl.when(jnp.logical_and(row >= z, z > 0))
        def _():
            act(remote(part, part, down.at[row], in_sem, me - 2))

        act(remote(part, part, side.at[row], in_sem, other))

    def start(copy):
        copy.start()

    def finish(copy):
        copy.wait_send()

    each_shift(start)

    def q_view(c):
        return qall.at[c]

    def out_view(c):
        return out_ref.at[:, own_cols(c)]

    def q_spread(row, act):
        spread(q_view, q_up, q_down, q_side, q_in, row, act)

    def out_spread(row, act):
        spread(out_view, r_up, r_down, r_side, r_in, row, act)

    slot_no = lax.broadcasted_iota(jnp.int32, hidden.shape, 0)
    lane_no = lax.broadcasted_iota(jnp.int32, hidden.shape, 1)
    dead = jnp.logical_and(slot_no >= counts_ref[0, me], lane_no == 0)
    hidden[...] = jnp.where(dead, DEAD, 0.0).astype(jnp.bfloat16)
    v_turn[HD:, :] = jnp.ones((16, v_turn.shape[1]), jnp.bfloat16)
    first_lane = jnp.where(
        lax.broadcasted_iota(jnp.int32, (tokens, HD), 1) == 0, 1.0, 0.0
    ).astype(jnp.bfloat16)
    slots = hidden.shape[0]
    block = slots // BLOCKS

    def normalize(i, carry):
        p = piece_at(i)

        @pl.when(has_source)
        def _():
            shift_side(p).wait_recv()

        @pl.when(jnp.logical_and(takes_half, i < PIECES // 2))
        def _():
            shift_side(p).start()

        @pl.when(jnp.logical_and(layer == 0, i == 0))
        def _():
            fresh_load.wait()

        rows = rows_of_piece(p)
        widened = cur[rows, :].astype(jnp.float32)
        normed[rows, :] = (
            widened
            * lax.rsqrt(jnp.mean(widened * widened, axis=-1, keepdims=True) + EPSILON)
            * gain_ref[...]
        ).astype(jnp.bfloat16)
        return carry

    lax.fori_loop(0, PIECES, normalize, 0)

    def rotated(part):
        half = HD // 2
        turned = jnp.concatenate([part[:, half:], part[:, :half]], axis=1)
        return part * cos_ref[...] + turned * sin_ref[...]

    loads[0].wait()
    projected = jnp.dot(normed[...], wq[...], preferred_element_type=jnp.float32)
    for h in range(heads):
        cols = slice(h * HD, (h + 1) * HD)
        qall[me, :, cols] = (rotated(projected[:, cols]) * to_log2).astype(jnp.bfloat16)

    def one_head(k_part, q_part, v_turned, masked):
        scores = lax.dot_general(
            k_part, q_part, (((1,), (1,)), ((), ())), preferred_element_type=jnp.float32
        ) + masked
        highest = jnp.max(scores, axis=0, keepdims=True)
        weights = jnp.exp2(scores - highest).astype(jnp.bfloat16)
        mixed = jnp.dot(v_turned, weights, preferred_element_type=jnp.float32)
        totals = mixed[HD : HD + 1]
        partial = (mixed[:HD] / totals).astype(jnp.bfloat16)
        return partial, highest + jnp.log2(totals)

    def with_ones(v_part):
        return jnp.concatenate(
            [v_part.T, jnp.ones((16, v_part.shape[0]), jnp.bfloat16)], axis=0
        )

    def log_rows(rows):
        return jnp.concatenate(rows + [jnp.zeros((8 - heads, tokens), jnp.float32)], axis=0)

    def y_copies(row):
        return (
            remote(parts.at[ROWS + row], oy_rx.at[row], oy_out.at[row], oy_in.at[row], other),
            remote(logs.at[ROWS + row], ly_rx.at[row], ly_out.at[row], ly_in.at[row], other),
        )

    def z_copies(row):
        peer = row * 2 + y
        return (
            remote(oz_tx.at[row], oz_rx.at[z], oz_out.at[row], oz_in.at[z], peer),
            remote(lz_tx.at[row], lz_rx.at[z], lz_out.at[row], lz_in.at[z], peer),
        )

    def merge(row, away):
        for copy in y_copies(row):
            copy.wait_recv()
        l_a, l_b = logs[row], ly_rx[row]
        top = jnp.maximum(l_a, l_b)
        f_a, f_b = jnp.exp2(l_a - top), jnp.exp2(l_b - top)
        total = f_a + f_b
        f_a, f_b = f_a / total, f_b / total
        o_dst, l_dst, at = (oz_tx, lz_tx, row) if away else (oz_rx, lz_rx, z)
        l_dst[at] = top + jnp.log2(total)
        for h in range(heads):
            part = slice(h * HD, (h + 1) * HD)
            o_dst[at, part, :] = (
                f_a[h : h + 1] * parts[row, part, :].astype(jnp.float32)
                + f_b[h : h + 1] * oy_rx[row, part, :].astype(jnp.float32)
            ).astype(jnp.bfloat16)
        if away:
            for copy in z_copies(row):
                copy.start()

    def visit(t, carry):
        j, second = t // 2, t % 2
        row = near_first(z, j)
        c = row * 2 + jnp.where(second == 0, y, 1 - y)

        @pl.when(t > 0)
        def _():
            remote(q_view(c), q_view(c), q_side.at[row], q_in.at[c], other).wait_recv()

        @pl.when(second == 0)
        def _():
            q_spread(row, start)

        @pl.when(t == 0)
        def _():
            loads[1].wait()
            both = jnp.dot(normed[...], wkv[...], preferred_element_type=jnp.float32)
            own_k[...] = rotated(both[:, :HD]).astype(jnp.bfloat16)
            own_v[...] = both[:, HD:].astype(jnp.bfloat16)
            loads[2].wait()
            loads[3].wait()

        group = pl.ds(pl.multiple_of(c * HD, HD), HD)
        to = second * ROWS + row
        v_turn[:HD, :] = vbuf[:, group].T

        def score_block(h, b, highest):
            rows = slice(b * block, (b + 1) * block)
            keys = jnp.concatenate([kbuf[rows, group], hidden[rows, :]], axis=1)
            asked = jnp.concatenate(
                [qall[c, :, h * HD : (h + 1) * HD], first_lane], axis=1
            )
            scores = lax.dot_general(
                keys, asked, (((1,), (1,)), ((), ())), preferred_element_type=jnp.float32
            )
            s_buf[h % 2, rows, :] = scores
            here = jnp.max(scores, axis=0, keepdims=True)
            return here if highest is None else jnp.maximum(highest, here)

        def weigh_block(h, b, highest):
            fine = block // FINE
            for i in range(FINE):
                rows = slice(b * block + i * fine, b * block + (i + 1) * fine)
                p_buf[h % 2, rows, :] = jnp.exp2(s_buf[h % 2, rows, :] - highest).astype(
                    jnp.bfloat16
                )

        def value_block(h, b, total):
            rows = slice(b * block, (b + 1) * block)
            here = jnp.dot(
                v_turn[:, rows], p_buf[h % 2, rows, :], preferred_element_type=jnp.float32
            )
            return here if total is None else total + here

        totals = []
        highest = None
        for b in range(BLOCKS):
            highest = score_block(0, b, highest)
        for h in range(heads):
            following, mixed = None, None
            for b in range(BLOCKS):
                if h + 1 < heads:
                    following = score_block(h + 1, b, following)
                weigh_block(h, b, highest)
                if b > 0:
                    mixed = value_block(h, b - 1, mixed)
            mixed = value_block(h, BLOCKS - 1, mixed)
            total = mixed[HD : HD + 1]
            parts[to, h * HD : (h + 1) * HD, :] = (mixed[:HD] / total).astype(jnp.bfloat16)
            totals.append(highest + jnp.log2(total))
            highest = following
        logs[to] = log_rows(totals)

        @pl.when(second == 1)
        def _():
            for copy in y_copies(row):
                copy.start()

        @pl.when(t == 3)
        def _():
            merge(near_first(z, 0), False)

        @pl.when(t == 5)
        def _():
            merge(near_first(z, 1), True)

        @pl.when(t == 7)
        def _():
            merge(near_first(z, 2), True)

        return carry

    lax.fori_loop(0, 2 * ROWS, visit, 0)

    key_no = lax.broadcasted_iota(jnp.int32, (tokens, tokens), 0)
    token_no = lax.broadcasted_iota(jnp.int32, (tokens, tokens), 1)
    causal = jnp.where(token_no >= key_no, 0.0, -jnp.inf)
    own, own_logs = [], []
    own_turned = with_ones(own_v[...])
    for h in range(heads):
        partial, log_total = one_head(
            own_k[...], qall[me, :, h * HD : (h + 1) * HD], own_turned, causal
        )
        own_logs.append(log_total)
        own.append(partial)

    merge(near_first(z, 3), True)

    def from_row(row):
        return (
            remote(oz_tx.at[row], oz_rx.at[row], oz_out.at[row], oz_in.at[row], row * 2 + y),
            remote(lz_tx.at[row], lz_rx.at[row], lz_out.at[row], lz_in.at[row], row * 2 + y),
        )

    for step in range(1, ROWS):
        for copy in from_row(near_first(z, step)):
            copy.wait_recv()
    all_logs = [log_rows(own_logs)] + [lz_rx[row] for row in range(ROWS)]
    top = all_logs[0]
    for log_total in all_logs[1:]:
        top = jnp.maximum(top, log_total)
    factors = [jnp.exp2(log_total - top) for log_total in all_logs]
    total = factors[0]
    for factor in factors[1:]:
        total = total + factor
    factors = [factor / total for factor in factors]
    for h in range(heads):
        part = slice(h * HD, (h + 1) * HD)
        summed = factors[0][h : h + 1] * own[h].astype(jnp.float32)
        for row in range(ROWS):
            summed = summed + factors[row + 1][h : h + 1] * oz_rx[row, part, :].astype(
                jnp.float32
            )
        att[:, part] = summed.T.astype(jnp.bfloat16)

    def term(c):
        return jnp.dot(att[...], wo[:, own_cols(c)], preferred_element_type=jnp.float32)

    def side_terms(row):
        return remote(hy_tx.at[row], hy_rx.at[row], hy_out.at[row], hy_in.at[row], other)

    def row_terms(row, slot):
        return remote(hz_tx.at[row], hz_rx.at[slot], hz_out.at[row], hz_in.at[slot], row * 2 + y)

    loads[4].wait()

    def send_side(i, carry):
        row = near_first(z, ROWS - 1 - i)
        hy_tx[row] = term(row * 2 + 1 - y).astype(jnp.bfloat16)
        side_terms(row).start()
        return carry

    def keep_own(i, carry):
        row = near_first(z, ROWS - 1 - i)
        hk[row] = term(row * 2 + y)
        return carry

    lax.fori_loop(0, ROWS, send_side, 0)
    lax.fori_loop(0, ROWS, keep_own, 0)
    for step in range(ROWS - 1, 0, -1):
        row = near_first(z, step)
        side_terms(row).wait_recv()
        hz_tx[row] = (hk[row] + hy_rx[row].astype(jnp.float32)).astype(jnp.bfloat16)
        row_terms(row, z).start()
    side_terms(z).wait_recv()
    summed = cur[:, own_cols(me)].astype(jnp.float32) + hk[z] + hy_rx[z].astype(jnp.float32)
    for step in range(1, ROWS):
        row = near_first(z, step)
        row_terms(row, row).wait_recv()
        summed = summed + hz_rx[row].astype(jnp.float32)
    out_ref[:, own_cols(me)] = summed.astype(jnp.bfloat16)

    out_spread(z, start)
    for step in range(1, ROWS):
        row = near_first(z, step)
        c = row * 2 + y
        remote(out_view(c), out_view(c), r_side.at[row], r_in.at[c], other).wait_recv()
        out_spread(row, start)
    for row in range(ROWS):
        c = row * 2 + 1 - y
        remote(out_view(c), out_view(c), r_side.at[row], r_in.at[c], other).wait_recv()

    each_shift(finish)

    def side_done(i, carry):
        @pl.when(takes_half)
        def _():
            shift_side(piece_at(i)).wait_send()

        return carry

    lax.fori_loop(0, PIECES // 2, side_done, 0)
    for row in range(ROWS):
        q_spread(row, finish)
        out_spread(row, finish)
        side_terms(row).wait_send()
        for copy in y_copies(row):
            copy.wait_send()
    for step in range(1, ROWS):
        row = near_first(z, step)
        for copy in z_copies(row):
            copy.wait_send()
        row_terms(row, z).wait_send()


def plane_call(counts, gain, cosine, sine, fresh, previous, w_query, w_keyval, keys, values, w_out):
    tokens, features = fresh.shape
    width = w_query.shape[1]
    slots = keys.shape[0]
    bf16, f32 = jnp.bfloat16, jnp.float32
    vmem = pl.BlockSpec(memory_space=pltpu.VMEM)
    anywhere = pl.BlockSpec(memory_space=pl.ANY)
    turned = lambda count: pltpu.VMEM((count, width, tokens), bf16)
    chunks = lambda count, kind: pltpu.VMEM((count, tokens, width), kind)
    logs = lambda count: pltpu.VMEM((count, 8, tokens), f32)
    sems = lambda count: pltpu.SemaphoreType.DMA((count,))
    like = lambda array: pltpu.VMEM(array.shape, array.dtype)
    return pl.pallas_call(
        plane_kernel,
        out_shape=jax.ShapeDtypeStruct(fresh.shape, bf16),
        in_specs=[pl.BlockSpec(memory_space=pltpu.SMEM)] + [vmem] * 3 + [anywhere] * 7,
        out_specs=vmem,
        scratch_shapes=[
            like(fresh), like(fresh), like(w_query), like(w_keyval),
            pltpu.VMEM((tokens, HD), bf16), pltpu.VMEM((tokens, HD), bf16),
            pltpu.VMEM((slots, HD), bf16),
            pltpu.VMEM((2, slots, tokens), f32), pltpu.VMEM((2, slots, tokens), bf16),
            pltpu.VMEM((HD + 16, slots), bf16),
            chunks(2 * ROWS, bf16), like(keys), like(values), like(w_out),
            turned(2 * ROWS), logs(2 * ROWS), turned(ROWS), logs(ROWS),
            turned(ROWS), logs(ROWS), turned(ROWS), logs(ROWS),
            pltpu.VMEM((tokens, width), bf16),
            chunks(ROWS, f32), chunks(ROWS, bf16), chunks(ROWS, bf16),
            chunks(ROWS, bf16), chunks(ROWS, bf16),
            sems(6), sems(PIECES), sems(PIECES), sems(PIECES),
            sems(ROWS), sems(ROWS), sems(ROWS), sems(2 * ROWS),
        ] + [sems(ROWS)] * 12 + [
            sems(ROWS), sems(ROWS), sems(ROWS), sems(2 * ROWS),
        ],
        compiler_params=pltpu.CompilerParams(
            collective_id=0, has_side_effects=True, vmem_limit_bytes=60 * 1024 * 1024
        ),
        cost_estimate=pl.CostEstimate(
            flops=4 * tokens * width * slots * 8, bytes_accessed=20 << 20,
            transcendentals=tokens * slots * 32,
        ),
    )(counts, gain, cosine, sine, fresh, previous, w_query, w_keyval, keys, values, w_out)


def plane_shards(
    fresh, previous, span_index, cache_counts, norm_gain,
    w_query, w_keyval, w_out, cache_keys, cache_values,
):
    length = fresh.shape[0]
    half_width = HD // 2
    positions = (span_index[0] * length + jnp.arange(length, dtype=jnp.int32)).astype(jnp.float32)
    inverse = ROPE_BASE ** (-(jnp.arange(half_width, dtype=jnp.float32) * 2.0) / HD)
    angles = positions[:, None] * inverse[None, :]
    cosine, sine = jnp.cos(angles), jnp.sin(angles)
    mixed = plane_call(
        cache_counts, norm_gain,
        jnp.concatenate([cosine, cosine], axis=1), jnp.concatenate([-sine, sine], axis=1),
        fresh, previous[0], w_query[0], w_keyval[0], cache_keys[0], cache_values[0], w_out[0],
    )
    return mixed[None]


def solution(mesh):
    placed = (
        P(),
        P("segment", None, None),
        P("segment"),
        P("segment", None),
        P("segment", None),
        P("segment", None, "blk"),
        P("segment", None, "blk"),
        P("segment", "blk", None),
        P("segment", "blk", None),
        P("segment", "blk", None),
    )
    body = plane_shards if mesh.shape["blk"] == KVH else shards
    return jax.shard_map(
        body, mesh=mesh, in_specs=placed, out_specs=P("segment", None, None), check_vma=False
    )
```

```python
import math

import jax
import jax.numpy as jnp
from jax import lax
from jax.experimental import pallas as pl
from jax.experimental.pallas import tpu as pltpu
from jax.sharding import PartitionSpec as P

KVH = 8
HD = 128


ROPE_BASE = 500000.0
EPSILON = 1e-05


def passed_along(block, axis, distance):
    devices = range(lax.axis_size(axis))
    route = [(i - distance, i) for i in devices if i - distance in devices]
    return lax.ppermute(block, axis, route)


def swapped(block, axis, distance):
    count = lax.axis_size(axis)
    route = []
    for low in range(count):
        high = low | 1 << distance
        if high != low and high < count:
            route += [(low, high), (high, low)]
    return lax.ppermute(block, axis, route)


def rotate(projected, first_span):
    length = projected.shape[0]
    half_width = projected.shape[-1] // 2
    positions = (first_span * length + jnp.arange(length, dtype=jnp.int32)).astype(jnp.float32)
    inverse = ROPE_BASE ** (
        -(jnp.arange(half_width, dtype=jnp.float32) * 2.0) / projected.shape[-1]
    )
    angles = positions[:, None] * inverse[None, :]
    cosine = jnp.cos(angles)[:, None, :]
    sine_table = jnp.sin(angles)[:, None, :]
    left_part = projected[..., :half_width]
    right_part = projected[..., half_width:]
    return jnp.concatenate(
        [
            left_part * cosine - right_part * sine_table,
            right_part * cosine + left_part * sine_table,
        ],
        axis=-1,
    )


def attend_rows(query_rows, key_rows, value_rows, allowed):
    scores = lax.dot_general(
        query_rows, key_rows, (((1,), (1,)), ((), ())), preferred_element_type=jnp.float32
    ) * query_rows.shape[-1] ** (-0.5)
    scores = jnp.where(allowed, scores, -jnp.inf)
    highest = jnp.max(scores, axis=-1, keepdims=True)
    weights = jnp.exp(scores - highest)
    totals = jnp.sum(weights, axis=-1, keepdims=True)
    partial_out = (
        jnp.dot(weights.astype(jnp.bfloat16), value_rows, preferred_element_type=jnp.float32)
        / totals
    ).astype(jnp.bfloat16)
    return (partial_out, (highest + jnp.log(totals))[:, 0])


def shards(
    fresh,
    previous,
    span_index,
    cache_counts,
    norm_gain,
    w_query,
    w_keyval,
    w_out,
    cache_keys,
    cache_values,
):
    blocks = lax.axis_size("blk")
    position = lax.axis_index("blk")
    span_rows = fresh.shape[0]
    arrived = passed_along(previous[0], "segment", 1)
    current = jnp.where(lax.axis_index("segment") == 0, fresh, arrived)
    widened = current.astype(jnp.float32)
    normed = (
        widened
        * lax.rsqrt(jnp.mean(widened * widened, axis=-1, keepdims=True) + EPSILON)
        * norm_gain[0]
    ).astype(jnp.bfloat16)
    first_span = span_index[0]
    heads_here = w_query.shape[2] // HD
    ratio = blocks // KVH
    queries = jnp.dot(normed, w_query[0], preferred_element_type=jnp.float32).reshape(
        span_rows, heads_here, HD
    )
    queries = rotate(queries, first_span).astype(jnp.bfloat16).reshape(span_rows, heads_here * HD)
    projected = jnp.dot(normed, w_keyval[0], preferred_element_type=jnp.float32)
    if ratio == 2:
        odd_member = position % 2 == 1
        as_key = rotate(projected[:, None, :], first_span)[:, 0, :].astype(jnp.bfloat16)
        mine = jnp.where(odd_member, projected.astype(jnp.bfloat16), as_key)
        partner = swapped(mine, "blk", 0)
        own_keys = jnp.where(odd_member, partner, mine)
        own_values = jnp.where(odd_member, mine, partner)
    else:
        own_keys = rotate(projected[:, None, :HD], first_span)[:, 0, :].astype(jnp.bfloat16)
        own_values = projected[:, HD:].astype(jnp.bfloat16)
    query_rows = queries.reshape(span_rows * heads_here, HD)
    row_tokens = jnp.arange(span_rows * heads_here, dtype=jnp.int32) // heads_here
    causal = row_tokens[:, None] >= jnp.arange(span_rows, dtype=jnp.int32)[None, :]
    own_out, own_log = attend_rows(query_rows, own_keys, own_values, causal)
    own_out = own_out.reshape(span_rows, heads_here * HD)
    own_log = own_log.reshape(span_rows, heads_here).T
    cache_rows = cache_keys.shape[1]
    offsets = jnp.arange(cache_rows, dtype=jnp.int32)
    every_query = lax.all_gather(queries, "blk", axis=0, tiled=True)
    live = cache_counts[0, position]

    def holder(source):
        query_block = lax.dynamic_slice_in_dim(
            every_query, source * span_rows, span_rows, 0
        ).reshape(span_rows * heads_here, HD)
        head_start = source // ratio * HD
        key_rows = lax.dynamic_slice_in_dim(cache_keys[0], head_start, HD, 1)
        value_rows = lax.dynamic_slice_in_dim(cache_values[0], head_start, HD, 1)
        partial_out, log_totals = attend_rows(
            query_block, key_rows, value_rows, (offsets < live)[None, :]
        )
        return (
            partial_out.reshape(span_rows, heads_here * HD),
            log_totals.reshape(span_rows, heads_here).T,
        )

    held_outs, held_logs = lax.map(holder, jnp.arange(blocks, dtype=jnp.int32))
    shard_outs = lax.all_to_all(held_outs, "blk", split_axis=0, concat_axis=0, tiled=True)
    shard_logs = lax.all_to_all(held_logs, "blk", split_axis=0, concat_axis=0, tiled=True)
    all_outs = (
        jnp.concatenate([own_out[None], shard_outs], axis=0)
        .astype(jnp.float32)
        .reshape(blocks + 1, span_rows, heads_here, HD)
    )
    all_logs = jnp.concatenate([own_log[None], shard_logs], axis=0).transpose(0, 2, 1)
    ceiling = jnp.max(all_logs, axis=0)
    factors = jnp.exp(all_logs - ceiling)
    attended = (
        jnp.sum(factors[..., None] * all_outs, axis=0) / jnp.sum(factors, axis=0)[..., None]
    ).astype(jnp.bfloat16)
    attended = attended.reshape(span_rows, heads_here * HD)
    head_terms = lax.optimization_barrier(
        jnp.dot(attended, w_out[0], preferred_element_type=jnp.float32).astype(jnp.bfloat16)
    ).astype(jnp.float32)
    summed = lax.psum(head_terms.astype(jnp.bfloat16), "blk").astype(jnp.float32)
    mixed = (widened + summed).astype(jnp.bfloat16)
    return mixed[None]


ROWS = 4
PIECES = 8
BLOCKS = 4
FINE = 4
DEAD = -1e30
MESH = pl.DeviceIdType.MESH


def near_first(z, step):
    half = z // 2
    if isinstance(step, int):
        return (z, z + 1 - 2 * (z % 2), 2 - half, 3 - 3 * half)[step]
    pair = z + 1 - 2 * (z % 2)
    later = jnp.where(step == 2, 2 - half, 3 - 3 * half)
    return jnp.where(step == 0, z, jnp.where(step == 1, pair, later))


def plane_kernel(
    counts_ref, gain_ref, cos_ref, sin_ref, fresh_hbm, prev_hbm, wq_hbm, wkv_hbm,
    kc_hbm, vc_hbm, wo_hbm, out_ref,
    cur, normed, wq, wkv, own_k, own_v, hidden, s_buf, p_buf, v_turn,
    qall, kbuf, vbuf, wo, parts, logs, oy_rx, ly_rx,
    oz_tx, lz_tx, oz_rx, lz_rx, att, hk, hy_tx, hy_rx, hz_tx, hz_rx,
    load_sem, x_out, x_side, x_in, q_up, q_down, q_side, q_in, oy_out, oy_in, ly_out, ly_in,
    oz_out, oz_in, lz_out, lz_in, hy_out, hy_in, hz_out, hz_in,
    r_up, r_down, r_side, r_in,
):
    me = lax.axis_index("blk")
    layer = lax.axis_index("segment")
    layers = lax.axis_size("segment")
    z, y = me // 2, me % 2
    other = z * 2 + 1 - y
    width, tokens = qall.shape[1:]
    heads = width // HD
    to_log2 = HD ** (-0.5) * math.log2(math.e)
    piece = tokens // PIECES

    def own_cols(c):
        return pl.ds(pl.multiple_of(c * width, width), width)

    loads = [
        pltpu.make_async_copy(wq_hbm, wq, load_sem.at[0]),
        pltpu.make_async_copy(wkv_hbm, wkv, load_sem.at[1]),
        pltpu.make_async_copy(kc_hbm, kbuf, load_sem.at[2]),
        pltpu.make_async_copy(vc_hbm, vbuf, load_sem.at[3]),
        pltpu.make_async_copy(wo_hbm, wo, load_sem.at[4]),
    ]
    fresh_load = pltpu.make_async_copy(fresh_hbm, cur, load_sem.at[5])

    @pl.when(layer == 0)
    def _():
        fresh_load.start()

    for load in loads:
        load.start()

    has_source, has_next = layer > 0, layer < layers - 1
    barrier = pltpu.get_barrier_semaphore()
    pl.semaphore_signal(barrier, inc=1, device_id={"blk": other}, device_id_type=MESH)
    for step in range(1, ROWS):
        pl.semaphore_signal(
            barrier, inc=1, device_id={"blk": near_first(z, step) * 2 + y}, device_id_type=MESH
        )

    @pl.when(has_source)
    def _():
        pl.semaphore_signal(
            barrier, inc=1, device_id={"segment": layer - 1}, device_id_type=MESH
        )

    @pl.when(has_next)
    def _():
        pl.semaphore_signal(
            barrier, inc=1, device_id={"segment": layer + 1}, device_id_type=MESH
        )

    pl.semaphore_wait(
        barrier, ROWS + has_source.astype(jnp.int32) + has_next.astype(jnp.int32)
    )

    def remote(src, dst, out_sem, in_sem, device):
        return pltpu.make_async_remote_copy(
            src_ref=src, dst_ref=dst, send_sem=out_sem, recv_sem=in_sem,
            device_id={"blk": device}, device_id_type=MESH,
        )

    def rows_of_piece(p):
        return pl.ds(pl.multiple_of(p * piece, piece), piece)

    def shift_copy(p):
        rows = rows_of_piece(p)
        return pltpu.make_async_remote_copy(
            src_ref=prev_hbm.at[rows], dst_ref=cur.at[rows],
            send_sem=x_out.at[p], recv_sem=x_in.at[p],
            device_id={"segment": layer + 1}, device_id_type=MESH,
        )

    def shift_side(p):
        rows = rows_of_piece(p)
        return remote(cur.at[rows], cur.at[rows], x_side.at[p], x_in.at[p], other)

    def piece_at(i):
        return (y * (PIECES // 2) + i) % PIECES

    to_core = layer % 2 == 0
    takes_half = jnp.logical_and(has_source, to_core)

    def each_shift(act):
        def step(i, carry):
            @pl.when(jnp.logical_and(has_next, jnp.logical_or(to_core, i < PIECES // 2)))
            def _():
                act(shift_copy(piece_at(i)))

            return carry

        lax.fori_loop(0, PIECES, step, 0)

    def spread(view, up, down, side, arrived, row, act):
        part = view(row * 2 + y)
        in_sem = arrived.at[row * 2 + y]

        @pl.when(jnp.logical_and(row <= z, z < ROWS - 1))
        def _():
            act(remote(part, part, up.at[row], in_sem, me + 2))

        @pl.when(jnp.logical_and(row >= z, z > 0))
        def _():
            act(remote(part, part, down.at[row], in_sem, me - 2))

        act(remote(part, part, side.at[row], in_sem, other))

    def start(copy):
        copy.start()

    def finish(copy):
        copy.wait_send()

    each_shift(start)

    def q_view(c):
        return qall.at[c]

    def out_view(c):
        return out_ref.at[:, own_cols(c)]

    def q_spread(row, act):
        spread(q_view, q_up, q_down, q_side, q_in, row, act)

    def out_spread(row, act):
        spread(out_view, r_up, r_down, r_side, r_in, row, act)

    slot_no = lax.broadcasted_iota(jnp.int32, hidden.shape, 0)
    lane_no = lax.broadcasted_iota(jnp.int32, hidden.shape, 1)
    dead = jnp.logical_and(slot_no >= counts_ref[0, me], lane_no == 0)
    hidden[...] = jnp.where(dead, DEAD, 0.0).astype(jnp.bfloat16)
    for slot in range(2):
        v_turn[slot, HD:, :] = jnp.ones((16, v_turn.shape[2]), jnp.bfloat16)
    first_row = jnp.where(
        lax.broadcasted_iota(jnp.int32, (HD, tokens), 0) == 0, 1.0, 0.0
    ).astype(jnp.bfloat16)
    slots = hidden.shape[0]
    block = slots // BLOCKS

    def normalize(i, carry):
        p = piece_at(i)

        @pl.when(has_source)
        def _():
            shift_side(p).wait_recv()

        @pl.when(jnp.logical_and(takes_half, i < PIECES // 2))
        def _():
            shift_side(p).start()

        @pl.when(jnp.logical_and(layer == 0, i == 0))
        def _():
            fresh_load.wait()

        rows = rows_of_piece(p)
        widened = cur[rows, :].astype(jnp.float32)
        normed[rows, :] = (
            widened
            * lax.rsqrt(jnp.mean(widened * widened, axis=-1, keepdims=True) + EPSILON)
            * gain_ref[...]
        ).astype(jnp.bfloat16)
        return carry

    lax.fori_loop(0, PIECES, normalize, 0)

    def rotated(part):
        half = HD // 2
        turned = jnp.concatenate([part[:, half:], part[:, :half]], axis=1)
        return part * cos_ref[...] + turned * sin_ref[...]

    loads[0].wait()
    projected = jnp.dot(normed[...], wq[...], preferred_element_type=jnp.float32)
    for h in range(heads):
        cols = slice(h * HD, (h + 1) * HD)
        qall[me, cols, :] = (rotated(projected[:, cols]) * to_log2).T.astype(jnp.bfloat16)

    def one_head(k_part, q_part, v_turned, masked):
        scores = jnp.dot(k_part, q_part, preferred_element_type=jnp.float32) + masked
        highest = jnp.max(scores, axis=0, keepdims=True)
        weights = jnp.exp2(scores - highest).astype(jnp.bfloat16)
        mixed = jnp.dot(v_turned, weights, preferred_element_type=jnp.float32)
        totals = mixed[HD : HD + 1]
        partial = (mixed[:HD] / totals).astype(jnp.bfloat16)
        return partial, highest + jnp.log2(totals)

    def with_ones(v_part):
        return jnp.concatenate(
            [v_part.T, jnp.ones((16, v_part.shape[0]), jnp.bfloat16)], axis=0
        )

    def log_rows(rows):
        return jnp.concatenate(rows + [jnp.zeros((8 - heads, tokens), jnp.float32)], axis=0)

    def y_copies(row):
        return (
            remote(parts.at[ROWS + row], oy_rx.at[row], oy_out.at[row], oy_in.at[row], other),
            remote(logs.at[ROWS + row], ly_rx.at[row], ly_out.at[row], ly_in.at[row], other),
        )

    def z_copies(row):
        peer = row * 2 + y
        return (
            remote(oz_tx.at[row], oz_rx.at[z], oz_out.at[row], oz_in.at[z], peer),
            remote(lz_tx.at[row], lz_rx.at[z], lz_out.at[row], lz_in.at[z], peer),
        )

    def merge(row, away):
        for copy in y_copies(row):
            copy.wait_recv()
        l_a, l_b = logs[row], ly_rx[row]
        top = jnp.maximum(l_a, l_b)
        f_a, f_b = jnp.exp2(l_a - top), jnp.exp2(l_b - top)
        total = f_a + f_b
        f_a, f_b = f_a / total, f_b / total
        o_dst, l_dst, at = (oz_tx, lz_tx, row) if away else (oz_rx, lz_rx, z)
        l_dst[at] = top + jnp.log2(total)
        for h in range(heads):
            part = slice(h * HD, (h + 1) * HD)
            o_dst[at, part, :] = (
                f_a[h : h + 1] * parts[row, part, :].astype(jnp.float32)
                + f_b[h : h + 1] * oy_rx[row, part, :].astype(jnp.float32)
            ).astype(jnp.bfloat16)
        if away:
            for copy in z_copies(row):
                copy.start()

    def chunk_at(t):
        row = near_first(z, t // 2)
        return row, row * 2 + jnp.where(t % 2 == 0, y, 1 - y)

    def group_of(c):
        return pl.ds(pl.multiple_of(c * HD, HD), HD)

    def turn_values(c, slot, b):
        rows = slice(b * block, (b + 1) * block)
        v_turn[slot, :HD, rows] = vbuf[rows, group_of(c)].T

    q_spread(z, start)
    loads[1].wait()
    both = jnp.dot(normed[...], wkv[...], preferred_element_type=jnp.float32)
    own_k[...] = rotated(both[:, :HD]).astype(jnp.bfloat16)
    own_v[...] = both[:, HD:].astype(jnp.bfloat16)
    loads[2].wait()
    loads[3].wait()
    for b in range(BLOCKS):
        turn_values(me, 0, b)

    def visit(t, carry):
        second = t % 2
        row, c = chunk_at(t)
        following_c = chunk_at(t + 1)[1]

        @pl.when(t > 0)
        def _():
            remote(q_view(c), q_view(c), q_side.at[row], q_in.at[c], other).wait_recv()

        @pl.when(jnp.logical_and(t > 0, second == 0))
        def _():
            q_spread(row, start)

        group = group_of(c)
        to = second * ROWS + row

        def score_block(h, b, highest):
            rows = slice(b * block, (b + 1) * block)
            keys = jnp.concatenate([kbuf[rows, group], hidden[rows, :]], axis=1)
            asked = jnp.concatenate(
                [qall[c, h * HD : (h + 1) * HD, :], first_row], axis=0
            )
            scores = jnp.dot(keys, asked, preferred_element_type=jnp.float32)
            s_buf[h % 2, rows, :] = scores
            here = jnp.max(scores, axis=0, keepdims=True)
            return here if highest is None else jnp.maximum(highest, here)

        def weigh_block(h, b, highest):
            fine = block // FINE
            for i in range(FINE):
                rows = slice(b * block + i * fine, b * block + (i + 1) * fine)
                p_buf[h % 2, rows, :] = jnp.exp2(s_buf[h % 2, rows, :] - highest).astype(
                    jnp.bfloat16
                )

        def value_block(h, b, total):
            rows = slice(b * block, (b + 1) * block)
            here = jnp.dot(
                v_turn[second, :, rows], p_buf[h % 2, rows, :], preferred_element_type=jnp.float32
            )
            return here if total is None else total + here

        totals = []
        highest = None
        for b in range(BLOCKS):
            highest = score_block(0, b, highest)
        for h in range(heads):
            following, mixed = None, None
            for b in range(BLOCKS):
                if h + 1 < heads:
                    following = score_block(h + 1, b, following)
                weigh_block(h, b, highest)
                if b == heads - 1 - h:
                    turn_values(following_c, 1 - second, h)
                if b > 0:
                    mixed = value_block(h, b - 1, mixed)
            mixed = value_block(h, BLOCKS - 1, mixed)
            total = mixed[HD : HD + 1]
            parts[to, h * HD : (h + 1) * HD, :] = (mixed[:HD] / total).astype(jnp.bfloat16)
            totals.append(highest + jnp.log2(total))
            highest = following
        logs[to] = log_rows(totals)

        @pl.when(second == 1)
        def _():
            for copy in y_copies(row):
                copy.start()

        @pl.when(t == 3)
        def _():
            merge(near_first(z, 0), False)

        @pl.when(t == 5)
        def _():
            merge(near_first(z, 1), True)

        @pl.when(t == 7)
        def _():
            merge(near_first(z, 2), True)

        return carry

    lax.fori_loop(0, 2 * ROWS, visit, 0)

    key_no = lax.broadcasted_iota(jnp.int32, (tokens, tokens), 0)
    token_no = lax.broadcasted_iota(jnp.int32, (tokens, tokens), 1)
    causal = jnp.where(token_no >= key_no, 0.0, -jnp.inf)
    own, own_logs = [], []
    own_turned = with_ones(own_v[...])
    for h in range(heads):
        partial, log_total = one_head(
            own_k[...], qall[me, h * HD : (h + 1) * HD, :], own_turned, causal
        )
        own_logs.append(log_total)
        own.append(partial)

    merge(near_first(z, 3), True)

    def from_row(row):
        return (
            remote(oz_tx.at[row], oz_rx.at[row], oz_out.at[row], oz_in.at[row], row * 2 + y),
            remote(lz_tx.at[row], lz_rx.at[row], lz_out.at[row], lz_in.at[row], row * 2 + y),
        )

    for step in range(1, ROWS):
        for copy in from_row(near_first(z, step)):
            copy.wait_recv()
    all_logs = [log_rows(own_logs)] + [lz_rx[row] for row in range(ROWS)]
    top = all_logs[0]
    for log_total in all_logs[1:]:
        top = jnp.maximum(top, log_total)
    factors = [jnp.exp2(log_total - top) for log_total in all_logs]
    total = factors[0]
    for factor in factors[1:]:
        total = total + factor
    factors = [factor / total for factor in factors]
    for h in range(heads):
        part = slice(h * HD, (h + 1) * HD)
        summed = factors[0][h : h + 1] * own[h].astype(jnp.float32)
        for row in range(ROWS):
            summed = summed + factors[row + 1][h : h + 1] * oz_rx[row, part, :].astype(
                jnp.float32
            )
        att[:, part] = summed.T.astype(jnp.bfloat16)

    def term(c):
        return jnp.dot(att[...], wo[:, own_cols(c)], preferred_element_type=jnp.float32)

    def side_terms(row):
        return remote(hy_tx.at[row], hy_rx.at[row], hy_out.at[row], hy_in.at[row], other)

    def row_terms(row, slot):
        return remote(hz_tx.at[row], hz_rx.at[slot], hz_out.at[row], hz_in.at[slot], row * 2 + y)

    loads[4].wait()

    def send_side(i, carry):
        row = near_first(z, ROWS - 1 - i)
        hy_tx[row] = term(row * 2 + 1 - y).astype(jnp.bfloat16)
        side_terms(row).start()
        return carry

    def keep_own(i, carry):
        row = near_first(z, ROWS - 1 - i)
        hk[row] = term(row * 2 + y)
        return carry

    lax.fori_loop(0, ROWS, send_side, 0)
    lax.fori_loop(0, ROWS, keep_own, 0)
    for step in range(ROWS - 1, 0, -1):
        row = near_first(z, step)
        side_terms(row).wait_recv()
        hz_tx[row] = (hk[row] + hy_rx[row].astype(jnp.float32)).astype(jnp.bfloat16)
        row_terms(row, z).start()
    side_terms(z).wait_recv()
    summed = cur[:, own_cols(me)].astype(jnp.float32) + hk[z] + hy_rx[z].astype(jnp.float32)
    for step in range(1, ROWS):
        row = near_first(z, step)
        row_terms(row, row).wait_recv()
        summed = summed + hz_rx[row].astype(jnp.float32)
    out_ref[:, own_cols(me)] = summed.astype(jnp.bfloat16)

    out_spread(z, start)
    for step in range(1, ROWS):
        row = near_first(z, step)
        c = row * 2 + y
        remote(out_view(c), out_view(c), r_side.at[row], r_in.at[c], other).wait_recv()
        out_spread(row, start)
    for row in range(ROWS):
        c = row * 2 + 1 - y
        remote(out_view(c), out_view(c), r_side.at[row], r_in.at[c], other).wait_recv()

    each_shift(finish)

    def side_done(i, carry):
        @pl.when(takes_half)
        def _():
            shift_side(piece_at(i)).wait_send()

        return carry

    lax.fori_loop(0, PIECES // 2, side_done, 0)
    for row in range(ROWS):
        q_spread(row, finish)
        out_spread(row, finish)
        side_terms(row).wait_send()
        for copy in y_copies(row):
            copy.wait_send()
    for step in range(1, ROWS):
        row = near_first(z, step)
        for copy in z_copies(row):
            copy.wait_send()
        row_terms(row, z).wait_send()


def plane_call(counts, gain, cosine, sine, fresh, previous, w_query, w_keyval, keys, values, w_out):
    tokens, features = fresh.shape
    width = w_query.shape[1]
    slots = keys.shape[0]
    bf16, f32 = jnp.bfloat16, jnp.float32
    vmem = pl.BlockSpec(memory_space=pltpu.VMEM)
    anywhere = pl.BlockSpec(memory_space=pl.ANY)
    turned = lambda count: pltpu.VMEM((count, width, tokens), bf16)
    chunks = lambda count, kind: pltpu.VMEM((count, tokens, width), kind)
    logs = lambda count: pltpu.VMEM((count, 8, tokens), f32)
    sems = lambda count: pltpu.SemaphoreType.DMA((count,))
    like = lambda array: pltpu.VMEM(array.shape, array.dtype)
    return pl.pallas_call(
        plane_kernel,
        out_shape=jax.ShapeDtypeStruct(fresh.shape, bf16),
        in_specs=[pl.BlockSpec(memory_space=pltpu.SMEM)] + [vmem] * 3 + [anywhere] * 7,
        out_specs=vmem,
        scratch_shapes=[
            like(fresh), like(fresh), like(w_query), like(w_keyval),
            pltpu.VMEM((tokens, HD), bf16), pltpu.VMEM((tokens, HD), bf16),
            pltpu.VMEM((slots, HD), bf16),
            pltpu.VMEM((2, slots, tokens), f32), pltpu.VMEM((2, slots, tokens), bf16),
            pltpu.VMEM((2, HD + 16, slots), bf16),
            turned(2 * ROWS), like(keys), like(values), like(w_out),
            turned(2 * ROWS), logs(2 * ROWS), turned(ROWS), logs(ROWS),
            turned(ROWS), logs(ROWS), turned(ROWS), logs(ROWS),
            pltpu.VMEM((tokens, width), bf16),
            chunks(ROWS, f32), chunks(ROWS, bf16), chunks(ROWS, bf16),
            chunks(ROWS, bf16), chunks(ROWS, bf16),
            sems(6), sems(PIECES), sems(PIECES), sems(PIECES),
            sems(ROWS), sems(ROWS), sems(ROWS), sems(2 * ROWS),
        ] + [sems(ROWS)] * 12 + [
            sems(ROWS), sems(ROWS), sems(ROWS), sems(2 * ROWS),
        ],
        compiler_params=pltpu.CompilerParams(
            collective_id=0, has_side_effects=True, vmem_limit_bytes=60 * 1024 * 1024
        ),
        cost_estimate=pl.CostEstimate(
            flops=4 * tokens * width * slots * 8, bytes_accessed=20 << 20,
            transcendentals=tokens * slots * 32,
        ),
    )(counts, gain, cosine, sine, fresh, previous, w_query, w_keyval, keys, values, w_out)


def plane_shards(
    fresh, previous, span_index, cache_counts, norm_gain,
    w_query, w_keyval, w_out, cache_keys, cache_values,
):
    length = fresh.shape[0]
    half_width = HD // 2
    positions = (span_index[0] * length + jnp.arange(length, dtype=jnp.int32)).astype(jnp.float32)
    inverse = ROPE_BASE ** (-(jnp.arange(half_width, dtype=jnp.float32) * 2.0) / HD)
    angles = positions[:, None] * inverse[None, :]
    cosine, sine = jnp.cos(angles), jnp.sin(angles)
    mixed = plane_call(
        cache_counts, norm_gain,
        jnp.concatenate([cosine, cosine], axis=1), jnp.concatenate([-sine, sine], axis=1),
        fresh, previous[0], w_query[0], w_keyval[0], cache_keys[0], cache_values[0], w_out[0],
    )
    return mixed[None]


def solution(mesh):
    placed = (
        P(),
        P("segment", None, None),
        P("segment"),
        P("segment", None),
        P("segment", None),
        P("segment", None, "blk"),
        P("segment", None, "blk"),
        P("segment", "blk", None),
        P("segment", "blk", None),
        P("segment", "blk", None),
    )
    body = plane_shards if mesh.shape["blk"] == KVH else shards
    return jax.shard_map(
        body, mesh=mesh, in_specs=placed, out_specs=P("segment", None, None), check_vma=False
    )
```

```python
import math

import jax
import jax.numpy as jnp
from jax import lax
from jax.experimental import pallas as pl
from jax.experimental.pallas import tpu as pltpu
from jax.sharding import PartitionSpec as P

KVH = 8
HD = 128


ROPE_BASE = 500000.0
EPSILON = 1e-05


def passed_along(block, axis, distance):
    devices = range(lax.axis_size(axis))
    route = [(i - distance, i) for i in devices if i - distance in devices]
    return lax.ppermute(block, axis, route)


def swapped(block, axis, distance):
    count = lax.axis_size(axis)
    route = []
    for low in range(count):
        high = low | 1 << distance
        if high != low and high < count:
            route += [(low, high), (high, low)]
    return lax.ppermute(block, axis, route)


def rotate(projected, first_span):
    length = projected.shape[0]
    half_width = projected.shape[-1] // 2
    positions = (first_span * length + jnp.arange(length, dtype=jnp.int32)).astype(jnp.float32)
    inverse = ROPE_BASE ** (
        -(jnp.arange(half_width, dtype=jnp.float32) * 2.0) / projected.shape[-1]
    )
    angles = positions[:, None] * inverse[None, :]
    cosine = jnp.cos(angles)[:, None, :]
    sine_table = jnp.sin(angles)[:, None, :]
    left_part = projected[..., :half_width]
    right_part = projected[..., half_width:]
    return jnp.concatenate(
        [
            left_part * cosine - right_part * sine_table,
            right_part * cosine + left_part * sine_table,
        ],
        axis=-1,
    )


def attend_rows(query_rows, key_rows, value_rows, allowed):
    scores = lax.dot_general(
        query_rows, key_rows, (((1,), (1,)), ((), ())), preferred_element_type=jnp.float32
    ) * query_rows.shape[-1] ** (-0.5)
    scores = jnp.where(allowed, scores, -jnp.inf)
    highest = jnp.max(scores, axis=-1, keepdims=True)
    weights = jnp.exp(scores - highest)
    totals = jnp.sum(weights, axis=-1, keepdims=True)
    partial_out = (
        jnp.dot(weights.astype(jnp.bfloat16), value_rows, preferred_element_type=jnp.float32)
        / totals
    ).astype(jnp.bfloat16)
    return (partial_out, (highest + jnp.log(totals))[:, 0])


def shards(
    fresh,
    previous,
    span_index,
    cache_counts,
    norm_gain,
    w_query,
    w_keyval,
    w_out,
    cache_keys,
    cache_values,
):
    blocks = lax.axis_size("blk")
    position = lax.axis_index("blk")
    span_rows = fresh.shape[0]
    arrived = passed_along(previous[0], "segment", 1)
    current = jnp.where(lax.axis_index("segment") == 0, fresh, arrived)
    widened = current.astype(jnp.float32)
    normed = (
        widened
        * lax.rsqrt(jnp.mean(widened * widened, axis=-1, keepdims=True) + EPSILON)
        * norm_gain[0]
    ).astype(jnp.bfloat16)
    first_span = span_index[0]
    heads_here = w_query.shape[2] // HD
    ratio = blocks // KVH
    queries = jnp.dot(normed, w_query[0], preferred_element_type=jnp.float32).reshape(
        span_rows, heads_here, HD
    )
    queries = rotate(queries, first_span).astype(jnp.bfloat16).reshape(span_rows, heads_here * HD)
    projected = jnp.dot(normed, w_keyval[0], preferred_element_type=jnp.float32)
    if ratio == 2:
        odd_member = position % 2 == 1
        as_key = rotate(projected[:, None, :], first_span)[:, 0, :].astype(jnp.bfloat16)
        mine = jnp.where(odd_member, projected.astype(jnp.bfloat16), as_key)
        partner = swapped(mine, "blk", 0)
        own_keys = jnp.where(odd_member, partner, mine)
        own_values = jnp.where(odd_member, mine, partner)
    else:
        own_keys = rotate(projected[:, None, :HD], first_span)[:, 0, :].astype(jnp.bfloat16)
        own_values = projected[:, HD:].astype(jnp.bfloat16)
    query_rows = queries.reshape(span_rows * heads_here, HD)
    row_tokens = jnp.arange(span_rows * heads_here, dtype=jnp.int32) // heads_here
    causal = row_tokens[:, None] >= jnp.arange(span_rows, dtype=jnp.int32)[None, :]
    own_out, own_log = attend_rows(query_rows, own_keys, own_values, causal)
    own_out = own_out.reshape(span_rows, heads_here * HD)
    own_log = own_log.reshape(span_rows, heads_here).T
    cache_rows = cache_keys.shape[1]
    offsets = jnp.arange(cache_rows, dtype=jnp.int32)
    every_query = lax.all_gather(queries, "blk", axis=0, tiled=True)
    live = cache_counts[0, position]

    def holder(source):
        query_block = lax.dynamic_slice_in_dim(
            every_query, source * span_rows, span_rows, 0
        ).reshape(span_rows * heads_here, HD)
        head_start = source // ratio * HD
        key_rows = lax.dynamic_slice_in_dim(cache_keys[0], head_start, HD, 1)
        value_rows = lax.dynamic_slice_in_dim(cache_values[0], head_start, HD, 1)
        partial_out, log_totals = attend_rows(
            query_block, key_rows, value_rows, (offsets < live)[None, :]
        )
        return (
            partial_out.reshape(span_rows, heads_here * HD),
            log_totals.reshape(span_rows, heads_here).T,
        )

    held_outs, held_logs = lax.map(holder, jnp.arange(blocks, dtype=jnp.int32))
    shard_outs = lax.all_to_all(held_outs, "blk", split_axis=0, concat_axis=0, tiled=True)
    shard_logs = lax.all_to_all(held_logs, "blk", split_axis=0, concat_axis=0, tiled=True)
    all_outs = (
        jnp.concatenate([own_out[None], shard_outs], axis=0)
        .astype(jnp.float32)
        .reshape(blocks + 1, span_rows, heads_here, HD)
    )
    all_logs = jnp.concatenate([own_log[None], shard_logs], axis=0).transpose(0, 2, 1)
    ceiling = jnp.max(all_logs, axis=0)
    factors = jnp.exp(all_logs - ceiling)
    attended = (
        jnp.sum(factors[..., None] * all_outs, axis=0) / jnp.sum(factors, axis=0)[..., None]
    ).astype(jnp.bfloat16)
    attended = attended.reshape(span_rows, heads_here * HD)
    head_terms = lax.optimization_barrier(
        jnp.dot(attended, w_out[0], preferred_element_type=jnp.float32).astype(jnp.bfloat16)
    ).astype(jnp.float32)
    summed = lax.psum(head_terms.astype(jnp.bfloat16), "blk").astype(jnp.float32)
    mixed = (widened + summed).astype(jnp.bfloat16)
    return mixed[None]


ROWS = 4
PIECES = 8
PAIR = 2
HALVES = 2
BLOCKS = 4
FINE = 4
DEAD = -1e30
MESH = pl.DeviceIdType.MESH


def near_first(z, step):
    half = z // 2
    if isinstance(step, int):
        return (z, z + 1 - 2 * (z % 2), 2 - half, 3 - 3 * half)[step]
    pair = z + 1 - 2 * (z % 2)
    later = jnp.where(step == 2, 2 - half, 3 - 3 * half)
    return jnp.where(step == 0, z, jnp.where(step == 1, pair, later))


def plane_kernel(
    counts_ref, gain_ref, cos_ref, sin_ref, fresh_hbm, prev_hbm, wq_hbm, wkv_hbm,
    kc_hbm, vc_hbm, wo_hbm, out_ref,
    cur, normed, wq, wkv, own_k, own_v, hidden, s_buf, p_buf, v_turn,
    qall, kbuf, vbuf, wo, parts, logs, oy_rx, ly_rx,
    oz_tx, lz_tx, oz_rx, lz_rx, att, hk, hy_tx, hy_rx, hz_tx, hz_rx,
    load_sem, x_out, x_side, x_in, q_up, q_down, q_side, q_in, oy_out, oy_in, ly_out, ly_in,
    oz_out, oz_in, lz_out, lz_in, hy_out, hy_in, hz_out, hz_in,
    r_up, r_down, r_side, r_in,
):
    me = lax.axis_index("blk")
    layer = lax.axis_index("segment")
    layers = lax.axis_size("segment")
    z, y = me // 2, me % 2
    other = z * 2 + 1 - y
    tokens, width = cur.shape[0], wq.shape[1]
    heads = width // HD
    to_log2 = HD ** (-0.5) * math.log2(math.e)
    piece = tokens // PIECES

    def own_cols(c):
        return pl.ds(pl.multiple_of(c * width, width), width)

    loads = [
        pltpu.make_async_copy(wq_hbm, wq, load_sem.at[0]),
        pltpu.make_async_copy(wkv_hbm, wkv, load_sem.at[1]),
        pltpu.make_async_copy(kc_hbm, kbuf, load_sem.at[2]),
        pltpu.make_async_copy(vc_hbm, vbuf, load_sem.at[3]),
        pltpu.make_async_copy(wo_hbm, wo, load_sem.at[4]),
    ]
    fresh_load = pltpu.make_async_copy(fresh_hbm, cur, load_sem.at[5])

    @pl.when(layer == 0)
    def _():
        fresh_load.start()

    for load in loads:
        load.start()

    has_source, has_next = layer > 0, layer < layers - 1
    barrier = pltpu.get_barrier_semaphore()
    pl.semaphore_signal(barrier, inc=1, device_id={"blk": other}, device_id_type=MESH)
    for step in range(1, ROWS):
        pl.semaphore_signal(
            barrier, inc=1, device_id={"blk": near_first(z, step) * 2 + y}, device_id_type=MESH
        )

    @pl.when(has_source)
    def _():
        pl.semaphore_signal(
            barrier, inc=1, device_id={"segment": layer - 1}, device_id_type=MESH
        )

    @pl.when(has_next)
    def _():
        pl.semaphore_signal(
            barrier, inc=1, device_id={"segment": layer + 1}, device_id_type=MESH
        )

    pl.semaphore_wait(
        barrier, ROWS + has_source.astype(jnp.int32) + has_next.astype(jnp.int32)
    )

    def remote(src, dst, out_sem, in_sem, device):
        return pltpu.make_async_remote_copy(
            src_ref=src, dst_ref=dst, send_sem=out_sem, recv_sem=in_sem,
            device_id={"blk": device}, device_id_type=MESH,
        )

    def rows_of_piece(p):
        return pl.ds(pl.multiple_of(p * piece, piece), piece)

    def shift_copy(p):
        rows = rows_of_piece(p)
        return pltpu.make_async_remote_copy(
            src_ref=prev_hbm.at[rows], dst_ref=cur.at[rows],
            send_sem=x_out.at[p], recv_sem=x_in.at[p],
            device_id={"segment": layer + 1}, device_id_type=MESH,
        )

    def shift_side(p):
        rows = rows_of_piece(p)
        return remote(cur.at[rows], cur.at[rows], x_side.at[p], x_in.at[p], other)

    def piece_at(i):
        return (y * (PIECES // 2) + i) % PIECES

    to_core = layer % 2 == 0
    takes_half = jnp.logical_and(has_source, to_core)

    def each_shift(act):
        def step(i, carry):
            @pl.when(jnp.logical_and(has_next, jnp.logical_or(to_core, i < PIECES // 2)))
            def _():
                act(shift_copy(piece_at(i)))

            return carry

        lax.fori_loop(0, PIECES, step, 0)

    def spread(view, up, down, side, arrived, row, act, half=0):
        part = view(row * 2 + y, half)
        in_sem = arrived.at[half * 2 * ROWS + row * 2 + y]
        slot = half * ROWS + row

        @pl.when(jnp.logical_and(row <= z, z < ROWS - 1))
        def _():
            act(remote(part, part, up.at[slot], in_sem, me + 2))

        @pl.when(jnp.logical_and(row >= z, z > 0))
        def _():
            act(remote(part, part, down.at[slot], in_sem, me - 2))

        act(remote(part, part, side.at[slot], in_sem, other))

    def start(copy):
        copy.start()

    def finish(copy):
        copy.wait_send()

    each_shift(start)

    def q_view(c, half=0):
        return qall.at[c]

    def half_rows(half):
        return pl.ds(half * (tokens // HALVES), tokens // HALVES)

    def out_view(c, half):
        return out_ref.at[half_rows(half), own_cols(c)]

    def q_spread(row, act):
        spread(q_view, q_up, q_down, q_side, q_in, row, act)

    def out_spread(row, act, half):
        spread(out_view, r_up, r_down, r_side, r_in, row, act, half)

    slot_no = lax.broadcasted_iota(jnp.int32, hidden.shape, 0)
    lane_no = lax.broadcasted_iota(jnp.int32, hidden.shape, 1)
    dead = jnp.logical_and(slot_no >= counts_ref[0, me], lane_no == 0)
    hidden[...] = jnp.where(dead, DEAD, 0.0).astype(jnp.bfloat16)
    for slot in range(2):
        v_turn[slot, HD:, :] = jnp.ones((16, v_turn.shape[2]), jnp.bfloat16)
    first_row = jnp.where(
        lax.broadcasted_iota(jnp.int32, (HD, PAIR * tokens), 0) == 0, 1.0, 0.0
    ).astype(jnp.bfloat16)
    slots = hidden.shape[0]
    block = slots // BLOCKS

    def normalize(i, carry):
        p = piece_at(i)

        @pl.when(has_source)
        def _():
            shift_side(p).wait_recv()

        @pl.when(jnp.logical_and(takes_half, i < PIECES // 2))
        def _():
            shift_side(p).start()

        @pl.when(jnp.logical_and(layer == 0, i == 0))
        def _():
            fresh_load.wait()

        rows = rows_of_piece(p)
        widened = cur[rows, :].astype(jnp.float32)
        normed[rows, :] = (
            widened
            * lax.rsqrt(jnp.mean(widened * widened, axis=-1, keepdims=True) + EPSILON)
            * gain_ref[...]
        ).astype(jnp.bfloat16)
        return carry

    lax.fori_loop(0, PIECES, normalize, 0)

    def rotated(part):
        half = HD // 2
        turned = jnp.concatenate([part[:, half:], part[:, :half]], axis=1)
        return part * cos_ref[...] + turned * sin_ref[...]

    loads[0].wait()
    projected = jnp.dot(normed[...], wq[...], preferred_element_type=jnp.float32)
    for h in range(heads):
        cols = slice(h * HD, (h + 1) * HD)
        qall[me, :, h * tokens : (h + 1) * tokens] = (rotated(projected[:, cols]) * to_log2).T.astype(jnp.bfloat16)

    def one_head(k_part, q_part, v_turned, masked):
        scores = jnp.dot(k_part, q_part, preferred_element_type=jnp.float32) + masked
        highest = jnp.max(scores, axis=0, keepdims=True)
        weights = jnp.exp2(scores - highest).astype(jnp.bfloat16)
        mixed = jnp.dot(v_turned, weights, preferred_element_type=jnp.float32)
        totals = mixed[HD : HD + 1]
        partial = (mixed[:HD] / totals).astype(jnp.bfloat16)
        return partial, highest + jnp.log2(totals)

    def with_ones(v_part):
        return jnp.concatenate(
            [v_part.T, jnp.ones((16, v_part.shape[0]), jnp.bfloat16)], axis=0
        )

    def log_rows(rows):
        return jnp.concatenate(rows + [jnp.zeros((8 - heads, tokens), jnp.float32)], axis=0)

    def y_copies(row):
        return (
            remote(parts.at[ROWS + row], oy_rx.at[row], oy_out.at[row], oy_in.at[row], other),
            remote(logs.at[ROWS + row], ly_rx.at[row], ly_out.at[row], ly_in.at[row], other),
        )

    def z_copies(row):
        peer = row * 2 + y
        return (
            remote(oz_tx.at[row], oz_rx.at[z], oz_out.at[row], oz_in.at[z], peer),
            remote(lz_tx.at[row], lz_rx.at[z], lz_out.at[row], lz_in.at[z], peer),
        )

    def merge(row, away):
        for copy in y_copies(row):
            copy.wait_recv()
        l_a, l_b = logs[row], ly_rx[row]
        top = jnp.maximum(l_a, l_b)
        f_a, f_b = jnp.exp2(l_a - top), jnp.exp2(l_b - top)
        total = f_a + f_b
        f_a, f_b = f_a / total, f_b / total
        o_dst, l_dst, at = (oz_tx, lz_tx, row) if away else (oz_rx, lz_rx, z)
        l_dst[at] = top + jnp.log2(total)
        for h in range(heads):
            part = slice(h * tokens, (h + 1) * tokens)
            o_dst[at, :, part] = (
                f_a[h : h + 1] * parts[row, :, part].astype(jnp.float32)
                + f_b[h : h + 1] * oy_rx[row, :, part].astype(jnp.float32)
            ).astype(jnp.bfloat16)
        if away:
            for copy in z_copies(row):
                copy.start()

    def chunk_at(t):
        row = near_first(z, t // 2)
        return row, row * 2 + jnp.where(t % 2 == 0, y, 1 - y)

    def group_of(c):
        return pl.ds(pl.multiple_of(c * HD, HD), HD)

    def turn_values(c, slot, b):
        rows = slice(b * block, (b + 1) * block)
        v_turn[slot, :HD, rows] = vbuf[rows, group_of(c)].T

    q_spread(z, start)
    loads[1].wait()
    both = jnp.dot(normed[...], wkv[...], preferred_element_type=jnp.float32)
    own_k[...] = rotated(both[:, :HD]).astype(jnp.bfloat16)
    own_v[...] = both[:, HD:].astype(jnp.bfloat16)
    loads[2].wait()
    loads[3].wait()
    for b in range(BLOCKS):
        turn_values(me, 0, b)

    def visit(t, carry):
        second = t % 2
        row, c = chunk_at(t)
        following_c = chunk_at(t + 1)[1]

        @pl.when(t > 0)
        def _():
            remote(q_view(c), q_view(c), q_side.at[row], q_in.at[c], other).wait_recv()

        @pl.when(jnp.logical_and(t > 0, second == 0))
        def _():
            q_spread(row, start)

        group = group_of(c)
        to = second * ROWS + row
        wide, pairs = PAIR * tokens, heads // PAIR

        def score_block(h, b, highest):
            rows = slice(b * block, (b + 1) * block)
            keys = jnp.concatenate([kbuf[rows, group], hidden[rows, :]], axis=1)
            asked = jnp.concatenate(
                [qall[c, :, h * wide : (h + 1) * wide], first_row], axis=0
            )
            scores = jnp.dot(keys, asked, preferred_element_type=jnp.float32)
            s_buf[h % 2, rows, :] = scores
            here = jnp.max(scores, axis=0, keepdims=True)
            return here if highest is None else jnp.maximum(highest, here)

        def weigh_block(h, b, highest):
            fine = block // FINE
            for i in range(FINE):
                rows = slice(b * block + i * fine, b * block + (i + 1) * fine)
                p_buf[h % 2, rows, :] = jnp.exp2(s_buf[h % 2, rows, :] - highest).astype(
                    jnp.bfloat16
                )

        def value_block(h, b, total):
            rows = slice(b * block, (b + 1) * block)
            here = jnp.dot(
                v_turn[second, :, rows], p_buf[h % 2, rows, :], preferred_element_type=jnp.float32
            )
            return here if total is None else total + here

        totals = []
        highest = None
        for b in range(BLOCKS):
            highest = score_block(0, b, highest)
        for h in range(pairs):
            following, mixed = None, None
            for b in range(BLOCKS):
                if h + 1 < pairs:
                    following = score_block(h + 1, b, following)
                weigh_block(h, b, highest)
                if b % pairs == h:
                    turn_values(following_c, 1 - second, b)
                if b > 0:
                    mixed = value_block(h, b - 1, mixed)
            mixed = value_block(h, BLOCKS - 1, mixed)
            total = mixed[HD : HD + 1]
            parts[to, :, h * wide : (h + 1) * wide] = (mixed[:HD] / total).astype(jnp.bfloat16)
            log_total = highest + jnp.log2(total)
            totals += [log_total[:, i * tokens : (i + 1) * tokens] for i in range(PAIR)]
            highest = following
        logs[to] = log_rows(totals)

        @pl.when(second == 1)
        def _():
            for copy in y_copies(row):
                copy.start()

        @pl.when(t == 3)
        def _():
            merge(near_first(z, 0), False)

        @pl.when(t == 5)
        def _():
            merge(near_first(z, 1), True)

        @pl.when(t == 7)
        def _():
            merge(near_first(z, 2), True)

        return carry

    lax.fori_loop(0, 2 * ROWS, visit, 0)

    key_no = lax.broadcasted_iota(jnp.int32, (tokens, tokens), 0)
    token_no = lax.broadcasted_iota(jnp.int32, (tokens, tokens), 1)
    causal = jnp.where(token_no >= key_no, 0.0, -jnp.inf)
    own, own_logs = [], []
    own_turned = with_ones(own_v[...])
    for h in range(heads):
        partial, log_total = one_head(
            own_k[...], qall[me, :, h * tokens : (h + 1) * tokens], own_turned, causal
        )
        own_logs.append(log_total)
        own.append(partial)

    merge(near_first(z, 3), True)

    def from_row(row):
        return (
            remote(oz_tx.at[row], oz_rx.at[row], oz_out.at[row], oz_in.at[row], row * 2 + y),
            remote(lz_tx.at[row], lz_rx.at[row], lz_out.at[row], lz_in.at[row], row * 2 + y),
        )

    for step in range(1, ROWS):
        for copy in from_row(near_first(z, step)):
            copy.wait_recv()
    all_logs = [log_rows(own_logs)] + [lz_rx[row] for row in range(ROWS)]
    top = all_logs[0]
    for log_total in all_logs[1:]:
        top = jnp.maximum(top, log_total)
    factors = [jnp.exp2(log_total - top) for log_total in all_logs]
    total = factors[0]
    for factor in factors[1:]:
        total = total + factor
    factors = [factor / total for factor in factors]
    for h in range(heads):
        part = slice(h * tokens, (h + 1) * tokens)
        summed = factors[0][h : h + 1] * own[h].astype(jnp.float32)
        for row in range(ROWS):
            summed = summed + factors[row + 1][h : h + 1] * oz_rx[row, :, part].astype(
                jnp.float32
            )
        att[:, h * HD : (h + 1) * HD] = summed.T.astype(jnp.bfloat16)

    def term(c):
        return jnp.dot(att[...], wo[:, own_cols(c)], preferred_element_type=jnp.float32)

    def side_terms(row, half):
        rows, slot = half_rows(half), half * ROWS + row
        return remote(
            hy_tx.at[row, rows], hy_rx.at[row, rows], hy_out.at[slot], hy_in.at[slot], other
        )

    def row_terms(row, at, half):
        rows = half_rows(half)
        return remote(
            hz_tx.at[row, rows], hz_rx.at[at, rows],
            hz_out.at[half * ROWS + row], hz_in.at[half * ROWS + at], row * 2 + y,
        )

    loads[4].wait()

    def send_side(i, carry):
        row = near_first(z, ROWS - 1 - i)
        hy_tx[row] = term(row * 2 + 1 - y).astype(jnp.bfloat16)
        side_terms(row, 0).start()
        return carry

    def keep_own(i, carry):
        row = near_first(z, ROWS - 1 - i)
        hk[row] = term(row * 2 + y)
        return carry

    lax.fori_loop(0, ROWS, send_side, 0)
    for half in range(1, HALVES):
        for step in range(ROWS - 1, -1, -1):
            side_terms(near_first(z, step), half).start()
    lax.fori_loop(0, ROWS, keep_own, 0)

    def reduce_row(step, half):
        row, rows = near_first(z, step), half_rows(half)
        side_terms(row, half).wait_recv()
        hz_tx[row, rows, :] = (
            hk[row, rows, :] + hy_rx[row, rows, :].astype(jnp.float32)
        ).astype(jnp.bfloat16)
        row_terms(row, z, half).start()

    def settle(half):
        rows = half_rows(half)
        side_terms(z, half).wait_recv()
        summed = (
            cur[rows, own_cols(me)].astype(jnp.float32)
            + hk[z, rows, :]
            + hy_rx[z, rows, :].astype(jnp.float32)
        )
        for step in range(1, ROWS):
            row = near_first(z, step)
            row_terms(row, row, half).wait_recv()
            summed = summed + hz_rx[row, rows, :].astype(jnp.float32)
        out_ref[rows, own_cols(me)] = summed.astype(jnp.bfloat16)
        out_spread(z, start, half)

    def out_arrived(c, half):
        view = out_view(c, half)
        in_sem = r_in.at[half * 2 * ROWS + c]
        remote(view, view, r_side.at[0], in_sem, other).wait_recv()

    def pass_on(step, half):
        row = near_first(z, step)
        out_arrived(row * 2 + y, half)
        out_spread(row, start, half)

    for step in range(ROWS - 1, 0, -1):
        reduce_row(step, 0)
    settle(0)
    for half in range(1, HALVES):
        for step in range(ROWS - 1, 0, -1):
            reduce_row(step, half)
            pass_on(ROWS - step, half - 1)
        settle(half)
    for step in range(1, ROWS):
        pass_on(step, HALVES - 1)
    for half in range(HALVES):
        for row in range(ROWS):
            out_arrived(row * 2 + 1 - y, half)

    each_shift(finish)

    def side_done(i, carry):
        @pl.when(takes_half)
        def _():
            shift_side(piece_at(i)).wait_send()

        return carry

    lax.fori_loop(0, PIECES // 2, side_done, 0)
    for row in range(ROWS):
        q_spread(row, finish)
        for half in range(HALVES):
            out_spread(row, finish, half)
            side_terms(row, half).wait_send()
        for copy in y_copies(row):
            copy.wait_send()
    for step in range(1, ROWS):
        row = near_first(z, step)
        for copy in z_copies(row):
            copy.wait_send()
        for half in range(HALVES):
            row_terms(row, z, half).wait_send()


def plane_call(counts, gain, cosine, sine, fresh, previous, w_query, w_keyval, keys, values, w_out):
    tokens, features = fresh.shape
    width = w_query.shape[1]
    slots = keys.shape[0]
    bf16, f32 = jnp.bfloat16, jnp.float32
    vmem = pl.BlockSpec(memory_space=pltpu.VMEM)
    anywhere = pl.BlockSpec(memory_space=pl.ANY)
    turned = lambda count: pltpu.VMEM((count, HD, width // HD * tokens), bf16)
    chunks = lambda count, kind: pltpu.VMEM((count, tokens, width), kind)
    logs = lambda count: pltpu.VMEM((count, 8, tokens), f32)
    sems = lambda count: pltpu.SemaphoreType.DMA((count,))
    like = lambda array: pltpu.VMEM(array.shape, array.dtype)
    return pl.pallas_call(
        plane_kernel,
        out_shape=jax.ShapeDtypeStruct(fresh.shape, bf16),
        in_specs=[pl.BlockSpec(memory_space=pltpu.SMEM)] + [vmem] * 3 + [anywhere] * 7,
        out_specs=vmem,
        scratch_shapes=[
            like(fresh), like(fresh), like(w_query), like(w_keyval),
            pltpu.VMEM((tokens, HD), bf16), pltpu.VMEM((tokens, HD), bf16),
            pltpu.VMEM((slots, HD), bf16),
            pltpu.VMEM((2, slots, PAIR * tokens), f32),
            pltpu.VMEM((2, slots, PAIR * tokens), bf16),
            pltpu.VMEM((2, HD + 16, slots), bf16),
            turned(2 * ROWS), like(keys), like(values), like(w_out),
            turned(2 * ROWS), logs(2 * ROWS), turned(ROWS), logs(ROWS),
            turned(ROWS), logs(ROWS), turned(ROWS), logs(ROWS),
            pltpu.VMEM((tokens, width), bf16),
            chunks(ROWS, f32), chunks(ROWS, bf16), chunks(ROWS, bf16),
            chunks(ROWS, bf16), chunks(ROWS, bf16),
            sems(6), sems(PIECES), sems(PIECES), sems(PIECES),
            sems(ROWS), sems(ROWS), sems(ROWS), sems(2 * ROWS),
        ] + [sems(ROWS)] * 8 + [sems(HALVES * ROWS)] * 7 + [sems(2 * HALVES * ROWS)],
        compiler_params=pltpu.CompilerParams(
            collective_id=0, has_side_effects=True, vmem_limit_bytes=60 * 1024 * 1024
        ),
        cost_estimate=pl.CostEstimate(
            flops=4 * tokens * width * slots * 8, bytes_accessed=20 << 20,
            transcendentals=tokens * slots * 32,
        ),
    )(counts, gain, cosine, sine, fresh, previous, w_query, w_keyval, keys, values, w_out)


def plane_shards(
    fresh, previous, span_index, cache_counts, norm_gain,
    w_query, w_keyval, w_out, cache_keys, cache_values,
):
    length = fresh.shape[0]
    half_width = HD // 2
    positions = (span_index[0] * length + jnp.arange(length, dtype=jnp.int32)).astype(jnp.float32)
    inverse = ROPE_BASE ** (-(jnp.arange(half_width, dtype=jnp.float32) * 2.0) / HD)
    angles = positions[:, None] * inverse[None, :]
    cosine, sine = jnp.cos(angles), jnp.sin(angles)
    mixed = plane_call(
        cache_counts, norm_gain,
        jnp.concatenate([cosine, cosine], axis=1), jnp.concatenate([-sine, sine], axis=1),
        fresh, previous[0], w_query[0], w_keyval[0], cache_keys[0], cache_values[0], w_out[0],
    )
    return mixed[None]


def solution(mesh):
    placed = (
        P(),
        P("segment", None, None),
        P("segment"),
        P("segment", None),
        P("segment", None),
        P("segment", None, "blk"),
        P("segment", None, "blk"),
        P("segment", "blk", None),
        P("segment", "blk", None),
        P("segment", "blk", None),
    )
    body = plane_shards if mesh.shape["blk"] == KVH else shards
    return jax.shard_map(
        body, mesh=mesh, in_specs=placed, out_specs=P("segment", None, None), check_vma=False
    )
```

```python
import math

import jax
import jax.numpy as jnp
from jax import lax
from jax.experimental import pallas as pl
from jax.experimental.pallas import tpu as pltpu
from jax.sharding import PartitionSpec as P

KVH = 8
HD = 128


ROPE_BASE = 500000.0
EPSILON = 1e-05


def passed_along(block, axis, distance):
    devices = range(lax.axis_size(axis))
    route = [(i - distance, i) for i in devices if i - distance in devices]
    return lax.ppermute(block, axis, route)


def swapped(block, axis, distance):
    count = lax.axis_size(axis)
    route = []
    for low in range(count):
        high = low | 1 << distance
        if high != low and high < count:
            route += [(low, high), (high, low)]
    return lax.ppermute(block, axis, route)


def rotate(projected, first_span):
    length = projected.shape[0]
    half_width = projected.shape[-1] // 2
    positions = (first_span * length + jnp.arange(length, dtype=jnp.int32)).astype(jnp.float32)
    inverse = ROPE_BASE ** (
        -(jnp.arange(half_width, dtype=jnp.float32) * 2.0) / projected.shape[-1]
    )
    angles = positions[:, None] * inverse[None, :]
    cosine = jnp.cos(angles)[:, None, :]
    sine_table = jnp.sin(angles)[:, None, :]
    left_part = projected[..., :half_width]
    right_part = projected[..., half_width:]
    return jnp.concatenate(
        [
            left_part * cosine - right_part * sine_table,
            right_part * cosine + left_part * sine_table,
        ],
        axis=-1,
    )


def attend_rows(query_rows, key_rows, value_rows, allowed):
    scores = lax.dot_general(
        query_rows, key_rows, (((1,), (1,)), ((), ())), preferred_element_type=jnp.float32
    ) * query_rows.shape[-1] ** (-0.5)
    scores = jnp.where(allowed, scores, -jnp.inf)
    highest = jnp.max(scores, axis=-1, keepdims=True)
    weights = jnp.exp(scores - highest)
    totals = jnp.sum(weights, axis=-1, keepdims=True)
    partial_out = (
        jnp.dot(weights.astype(jnp.bfloat16), value_rows, preferred_element_type=jnp.float32)
        / totals
    ).astype(jnp.bfloat16)
    return (partial_out, (highest + jnp.log(totals))[:, 0])


def shards(
    fresh,
    previous,
    span_index,
    cache_counts,
    norm_gain,
    w_query,
    w_keyval,
    w_out,
    cache_keys,
    cache_values,
):
    blocks = lax.axis_size("blk")
    position = lax.axis_index("blk")
    span_rows = fresh.shape[0]
    arrived = passed_along(previous[0], "segment", 1)
    current = jnp.where(lax.axis_index("segment") == 0, fresh, arrived)
    widened = current.astype(jnp.float32)
    normed = (
        widened
        * lax.rsqrt(jnp.mean(widened * widened, axis=-1, keepdims=True) + EPSILON)
        * norm_gain[0]
    ).astype(jnp.bfloat16)
    first_span = span_index[0]
    heads_here = w_query.shape[2] // HD
    ratio = blocks // KVH
    queries = jnp.dot(normed, w_query[0], preferred_element_type=jnp.float32).reshape(
        span_rows, heads_here, HD
    )
    queries = rotate(queries, first_span).astype(jnp.bfloat16).reshape(span_rows, heads_here * HD)
    projected = jnp.dot(normed, w_keyval[0], preferred_element_type=jnp.float32)
    if ratio == 2:
        odd_member = position % 2 == 1
        as_key = rotate(projected[:, None, :], first_span)[:, 0, :].astype(jnp.bfloat16)
        mine = jnp.where(odd_member, projected.astype(jnp.bfloat16), as_key)
        partner = swapped(mine, "blk", 0)
        own_keys = jnp.where(odd_member, partner, mine)
        own_values = jnp.where(odd_member, mine, partner)
    else:
        own_keys = rotate(projected[:, None, :HD], first_span)[:, 0, :].astype(jnp.bfloat16)
        own_values = projected[:, HD:].astype(jnp.bfloat16)
    query_rows = queries.reshape(span_rows * heads_here, HD)
    row_tokens = jnp.arange(span_rows * heads_here, dtype=jnp.int32) // heads_here
    causal = row_tokens[:, None] >= jnp.arange(span_rows, dtype=jnp.int32)[None, :]
    own_out, own_log = attend_rows(query_rows, own_keys, own_values, causal)
    own_out = own_out.reshape(span_rows, heads_here * HD)
    own_log = own_log.reshape(span_rows, heads_here).T
    cache_rows = cache_keys.shape[1]
    offsets = jnp.arange(cache_rows, dtype=jnp.int32)
    every_query = lax.all_gather(queries, "blk", axis=0, tiled=True)
    live = cache_counts[0, position]

    def holder(source):
        query_block = lax.dynamic_slice_in_dim(
            every_query, source * span_rows, span_rows, 0
        ).reshape(span_rows * heads_here, HD)
        head_start = source // ratio * HD
        key_rows = lax.dynamic_slice_in_dim(cache_keys[0], head_start, HD, 1)
        value_rows = lax.dynamic_slice_in_dim(cache_values[0], head_start, HD, 1)
        partial_out, log_totals = attend_rows(
            query_block, key_rows, value_rows, (offsets < live)[None, :]
        )
        return (
            partial_out.reshape(span_rows, heads_here * HD),
            log_totals.reshape(span_rows, heads_here).T,
        )

    held_outs, held_logs = lax.map(holder, jnp.arange(blocks, dtype=jnp.int32))
    shard_outs = lax.all_to_all(held_outs, "blk", split_axis=0, concat_axis=0, tiled=True)
    shard_logs = lax.all_to_all(held_logs, "blk", split_axis=0, concat_axis=0, tiled=True)
    all_outs = (
        jnp.concatenate([own_out[None], shard_outs], axis=0)
        .astype(jnp.float32)
        .reshape(blocks + 1, span_rows, heads_here, HD)
    )
    all_logs = jnp.concatenate([own_log[None], shard_logs], axis=0).transpose(0, 2, 1)
    ceiling = jnp.max(all_logs, axis=0)
    factors = jnp.exp(all_logs - ceiling)
    attended = (
        jnp.sum(factors[..., None] * all_outs, axis=0) / jnp.sum(factors, axis=0)[..., None]
    ).astype(jnp.bfloat16)
    attended = attended.reshape(span_rows, heads_here * HD)
    head_terms = lax.optimization_barrier(
        jnp.dot(attended, w_out[0], preferred_element_type=jnp.float32).astype(jnp.bfloat16)
    ).astype(jnp.float32)
    summed = lax.psum(head_terms.astype(jnp.bfloat16), "blk").astype(jnp.float32)
    mixed = (widened + summed).astype(jnp.bfloat16)
    return mixed[None]


ROWS = 4
PIECES = 8
PAIR = 2
HALVES = 1
BLOCKS = 4
FINE = 4
DEAD = -1e30
MESH = pl.DeviceIdType.MESH


def near_first(z, step):
    half = z // 2
    if isinstance(step, int):
        return (z, z + 1 - 2 * (z % 2), 2 - half, 3 - 3 * half)[step]
    pair = z + 1 - 2 * (z % 2)
    later = jnp.where(step == 2, 2 - half, 3 - 3 * half)
    return jnp.where(step == 0, z, jnp.where(step == 1, pair, later))


def plane_kernel(
    counts_ref, gain_ref, cos_ref, sin_ref, fresh_hbm, prev_hbm, wq_hbm, wkv_hbm,
    kc_hbm, vc_hbm, wo_hbm, out_ref,
    cur, normed, wq, wkv, own_k, own_v, hidden, s_buf, p_buf, v_turn,
    qall, kbuf, vbuf, wo, parts, logs, oy_rx, ly_rx,
    oz_tx, lz_tx, oz_rx, lz_rx, att, hk, hy_tx, hy_rx, hz_tx, hz_rx,
    load_sem, x_out, x_side, x_in, q_up, q_down, q_side, q_in, oy_out, oy_in, ly_out, ly_in,
    oz_out, oz_in, lz_out, lz_in, hy_out, hy_in, hz_out, hz_in,
    r_up, r_down, r_side, r_in,
):
    me = lax.axis_index("blk")
    layer = lax.axis_index("segment")
    layers = lax.axis_size("segment")
    z, y = me // 2, me % 2
    other = z * 2 + 1 - y
    tokens, width = cur.shape[0], wq.shape[1]
    heads = width // HD
    to_log2 = HD ** (-0.5) * math.log2(math.e)
    piece = tokens // PIECES

    def own_cols(c):
        return pl.ds(pl.multiple_of(c * width, width), width)

    loads = [
        pltpu.make_async_copy(wq_hbm, wq, load_sem.at[0]),
        pltpu.make_async_copy(wkv_hbm, wkv, load_sem.at[1]),
        pltpu.make_async_copy(kc_hbm, kbuf, load_sem.at[2]),
        pltpu.make_async_copy(vc_hbm, vbuf, load_sem.at[3]),
        pltpu.make_async_copy(wo_hbm, wo, load_sem.at[4]),
    ]
    fresh_load = pltpu.make_async_copy(fresh_hbm, cur, load_sem.at[5])

    @pl.when(layer == 0)
    def _():
        fresh_load.start()

    for load in loads:
        load.start()

    has_source, has_next = layer > 0, layer < layers - 1
    barrier = pltpu.get_barrier_semaphore()
    pl.semaphore_signal(barrier, inc=1, device_id={"blk": other}, device_id_type=MESH)
    for step in range(1, ROWS):
        pl.semaphore_signal(
            barrier, inc=1, device_id={"blk": near_first(z, step) * 2 + y}, device_id_type=MESH
        )

    @pl.when(has_source)
    def _():
        pl.semaphore_signal(
            barrier, inc=1, device_id={"segment": layer - 1}, device_id_type=MESH
        )

    @pl.when(has_next)
    def _():
        pl.semaphore_signal(
            barrier, inc=1, device_id={"segment": layer + 1}, device_id_type=MESH
        )

    pl.semaphore_wait(
        barrier, ROWS + has_source.astype(jnp.int32) + has_next.astype(jnp.int32)
    )

    def remote(src, dst, out_sem, in_sem, device):
        return pltpu.make_async_remote_copy(
            src_ref=src, dst_ref=dst, send_sem=out_sem, recv_sem=in_sem,
            device_id={"blk": device}, device_id_type=MESH,
        )

    def rows_of_piece(p):
        return pl.ds(pl.multiple_of(p * piece, piece), piece)

    def shift_copy(p):
        rows = rows_of_piece(p)
        return pltpu.make_async_remote_copy(
            src_ref=prev_hbm.at[rows], dst_ref=cur.at[rows],
            send_sem=x_out.at[p], recv_sem=x_in.at[p],
            device_id={"segment": layer + 1}, device_id_type=MESH,
        )

    def shift_side(p):
        rows = rows_of_piece(p)
        return remote(cur.at[rows], cur.at[rows], x_side.at[p], x_in.at[p], other)

    def piece_at(i):
        return (y * (PIECES // 2) + i) % PIECES

    to_core = layer % 2 == 0
    takes_half = jnp.logical_and(has_source, to_core)

    def each_shift(act):
        def step(i, carry):
            @pl.when(jnp.logical_and(has_next, jnp.logical_or(to_core, i < PIECES // 2)))
            def _():
                act(shift_copy(piece_at(i)))

            return carry

        lax.fori_loop(0, PIECES, step, 0)

    def spread(view, up, down, side, arrived, row, act, half=0):
        part = view(row * 2 + y, half)
        in_sem = arrived.at[half * 2 * ROWS + row * 2 + y]
        slot = half * ROWS + row

        @pl.when(jnp.logical_and(row <= z, z < ROWS - 1))
        def _():
            act(remote(part, part, up.at[slot], in_sem, me + 2))

        @pl.when(jnp.logical_and(row >= z, z > 0))
        def _():
            act(remote(part, part, down.at[slot], in_sem, me - 2))

        act(remote(part, part, side.at[slot], in_sem, other))

    def start(copy):
        copy.start()

    def finish(copy):
        copy.wait_send()

    each_shift(start)

    def q_view(c, half=0):
        return qall.at[c]

    def half_rows(half):
        return pl.ds(half * (tokens // HALVES), tokens // HALVES)

    def out_view(c, half):
        return out_ref.at[half_rows(half), own_cols(c)]

    def q_spread(row, act):
        spread(q_view, q_up, q_down, q_side, q_in, row, act)

    def out_spread(row, act, half):
        spread(out_view, r_up, r_down, r_side, r_in, row, act, half)

    slot_no = lax.broadcasted_iota(jnp.int32, hidden.shape, 0)
    lane_no = lax.broadcasted_iota(jnp.int32, hidden.shape, 1)
    dead = jnp.logical_and(slot_no >= counts_ref[0, me], lane_no == 0)
    hidden[...] = jnp.where(dead, DEAD, 0.0).astype(jnp.bfloat16)
    for slot in range(2):
        v_turn[slot, HD:, :] = jnp.ones((16, v_turn.shape[2]), jnp.bfloat16)
    first_row = jnp.where(
        lax.broadcasted_iota(jnp.int32, (HD, PAIR * tokens), 0) == 0, 1.0, 0.0
    ).astype(jnp.bfloat16)
    slots = hidden.shape[0]
    block = slots // BLOCKS

    def normalize(i, carry):
        p = piece_at(i)

        @pl.when(has_source)
        def _():
            shift_side(p).wait_recv()

        @pl.when(jnp.logical_and(takes_half, i < PIECES // 2))
        def _():
            shift_side(p).start()

        @pl.when(jnp.logical_and(layer == 0, i == 0))
        def _():
            fresh_load.wait()

        rows = rows_of_piece(p)
        widened = cur[rows, :].astype(jnp.float32)
        normed[rows, :] = (
            widened
            * lax.rsqrt(jnp.mean(widened * widened, axis=-1, keepdims=True) + EPSILON)
            * gain_ref[...]
        ).astype(jnp.bfloat16)
        return carry

    lax.fori_loop(0, PIECES, normalize, 0)

    def rotated(part):
        half = HD // 2
        turned = jnp.concatenate([part[:, half:], part[:, :half]], axis=1)
        return part * cos_ref[...] + turned * sin_ref[...]

    loads[0].wait()
    projected = jnp.dot(normed[...], wq[...], preferred_element_type=jnp.float32)
    for h in range(heads):
        cols = slice(h * HD, (h + 1) * HD)
        qall[me, :, h * tokens : (h + 1) * tokens] = (rotated(projected[:, cols]) * to_log2).T.astype(jnp.bfloat16)

    def one_head(k_part, q_part, v_turned, masked):
        scores = jnp.dot(k_part, q_part, preferred_element_type=jnp.float32) + masked
        highest = jnp.max(scores, axis=0, keepdims=True)
        weights = jnp.exp2(scores - highest).astype(jnp.bfloat16)
        mixed = jnp.dot(v_turned, weights, preferred_element_type=jnp.float32)
        totals = mixed[HD : HD + 1]
        partial = (mixed[:HD] / totals).astype(jnp.bfloat16)
        return partial, highest + jnp.log2(totals)

    def with_ones(v_part):
        return jnp.concatenate(
            [v_part.T, jnp.ones((16, v_part.shape[0]), jnp.bfloat16)], axis=0
        )

    def log_rows(rows):
        return jnp.concatenate(rows + [jnp.zeros((8 - heads, tokens), jnp.float32)], axis=0)

    def y_copies(row):
        return (
            remote(parts.at[ROWS + row], oy_rx.at[row], oy_out.at[row], oy_in.at[row], other),
            remote(logs.at[ROWS + row], ly_rx.at[row], ly_out.at[row], ly_in.at[row], other),
        )

    def z_copies(row):
        peer = row * 2 + y
        return (
            remote(oz_tx.at[row], oz_rx.at[z], oz_out.at[row], oz_in.at[z], peer),
            remote(lz_tx.at[row], lz_rx.at[z], lz_out.at[row], lz_in.at[z], peer),
        )

    def merge(row, away):
        for copy in y_copies(row):
            copy.wait_recv()
        l_a, l_b = logs[row], ly_rx[row]
        top = jnp.maximum(l_a, l_b)
        f_a, f_b = jnp.exp2(l_a - top), jnp.exp2(l_b - top)
        total = f_a + f_b
        f_a, f_b = f_a / total, f_b / total
        o_dst, l_dst, at = (oz_tx, lz_tx, row) if away else (oz_rx, lz_rx, z)
        l_dst[at] = top + jnp.log2(total)
        for h in range(heads):
            part = slice(h * tokens, (h + 1) * tokens)
            o_dst[at, :, part] = (
                f_a[h : h + 1] * parts[row, :, part].astype(jnp.float32)
                + f_b[h : h + 1] * oy_rx[row, :, part].astype(jnp.float32)
            ).astype(jnp.bfloat16)
        if away:
            for copy in z_copies(row):
                copy.start()

    def chunk_at(t):
        row = near_first(z, t // 2)
        return row, row * 2 + jnp.where(t % 2 == 0, y, 1 - y)

    def group_of(c):
        return pl.ds(pl.multiple_of(c * HD, HD), HD)

    def turn_values(c, slot, b):
        rows = slice(b * block, (b + 1) * block)
        v_turn[slot, :HD, rows] = vbuf[rows, group_of(c)].T

    q_spread(z, start)
    loads[1].wait()
    both = jnp.dot(normed[...], wkv[...], preferred_element_type=jnp.float32)
    own_k[...] = rotated(both[:, :HD]).astype(jnp.bfloat16)
    own_v[...] = both[:, HD:].astype(jnp.bfloat16)
    loads[2].wait()
    loads[3].wait()
    for b in range(BLOCKS):
        turn_values(me, 0, b)

    def visit(t, carry):
        second = t % 2
        row, c = chunk_at(t)
        following_c = chunk_at(t + 1)[1]

        @pl.when(t > 0)
        def _():
            remote(q_view(c), q_view(c), q_side.at[row], q_in.at[c], other).wait_recv()

        @pl.when(jnp.logical_and(t > 0, second == 0))
        def _():
            q_spread(row, start)

        group = group_of(c)
        to = second * ROWS + row
        wide, pairs = PAIR * tokens, heads // PAIR

        def score_block(h, b, highest):
            rows = slice(b * block, (b + 1) * block)
            keys = jnp.concatenate([kbuf[rows, group], hidden[rows, :]], axis=1)
            asked = jnp.concatenate(
                [qall[c, :, h * wide : (h + 1) * wide], first_row], axis=0
            )
            scores = jnp.dot(keys, asked, preferred_element_type=jnp.float32)
            s_buf[h % 2, rows, :] = scores
            here = jnp.max(scores, axis=0, keepdims=True)
            return here if highest is None else jnp.maximum(highest, here)

        def weigh_block(h, b, highest):
            fine = block // FINE
            for i in range(FINE):
                rows = slice(b * block + i * fine, b * block + (i + 1) * fine)
                lowered = (s_buf[h % 2, rows, :] - highest).astype(jnp.bfloat16)
                p_buf[h % 2, rows, :] = jnp.exp2(lowered)

        def value_block(h, b, total):
            rows = slice(b * block, (b + 1) * block)
            here = jnp.dot(
                v_turn[second, :, rows], p_buf[h % 2, rows, :], preferred_element_type=jnp.float32
            )
            return here if total is None else total + here

        totals = []
        highest = None
        for b in range(BLOCKS):
            highest = score_block(0, b, highest)
        for h in range(pairs):
            following, mixed = None, None
            for b in range(BLOCKS):
                if h + 1 < pairs:
                    following = score_block(h + 1, b, following)
                weigh_block(h, b, highest)
                if b % pairs == h:
                    turn_values(following_c, 1 - second, b)
                if b > 0:
                    mixed = value_block(h, b - 1, mixed)
            mixed = value_block(h, BLOCKS - 1, mixed)
            total = mixed[HD : HD + 1]
            parts[to, :, h * wide : (h + 1) * wide] = (mixed[:HD] / total).astype(jnp.bfloat16)
            log_total = highest + jnp.log2(total)
            totals += [log_total[:, i * tokens : (i + 1) * tokens] for i in range(PAIR)]
            highest = following
        logs[to] = log_rows(totals)

        @pl.when(second == 1)
        def _():
            for copy in y_copies(row):
                copy.start()

        @pl.when(t == 3)
        def _():
            merge(near_first(z, 0), False)

        @pl.when(t == 5)
        def _():
            merge(near_first(z, 1), True)

        @pl.when(t == 7)
        def _():
            merge(near_first(z, 2), True)

        return carry

    lax.fori_loop(0, 2 * ROWS, visit, 0)

    key_no = lax.broadcasted_iota(jnp.int32, (tokens, tokens), 0)
    token_no = lax.broadcasted_iota(jnp.int32, (tokens, tokens), 1)
    causal = jnp.where(token_no >= key_no, 0.0, -jnp.inf)
    own, own_logs = [], []
    own_turned = with_ones(own_v[...])
    for h in range(heads):
        partial, log_total = one_head(
            own_k[...], qall[me, :, h * tokens : (h + 1) * tokens], own_turned, causal
        )
        own_logs.append(log_total)
        own.append(partial)

    merge(near_first(z, 3), True)

    def from_row(row):
        return (
            remote(oz_tx.at[row], oz_rx.at[row], oz_out.at[row], oz_in.at[row], row * 2 + y),
            remote(lz_tx.at[row], lz_rx.at[row], lz_out.at[row], lz_in.at[row], row * 2 + y),
        )

    for step in range(1, ROWS):
        for copy in from_row(near_first(z, step)):
            copy.wait_recv()
    all_logs = [log_rows(own_logs)] + [lz_rx[row] for row in range(ROWS)]
    top = all_logs[0]
    for log_total in all_logs[1:]:
        top = jnp.maximum(top, log_total)
    factors = [jnp.exp2(log_total - top) for log_total in all_logs]
    total = factors[0]
    for factor in factors[1:]:
        total = total + factor
    factors = [factor / total for factor in factors]
    for h in range(heads):
        part = slice(h * tokens, (h + 1) * tokens)
        summed = factors[0][h : h + 1] * own[h].astype(jnp.float32)
        for row in range(ROWS):
            summed = summed + factors[row + 1][h : h + 1] * oz_rx[row, :, part].astype(
                jnp.float32
            )
        att[:, h * HD : (h + 1) * HD] = summed.T.astype(jnp.bfloat16)

    def term(c):
        return jnp.dot(att[...], wo[:, own_cols(c)], preferred_element_type=jnp.float32)

    def side_terms(row, half):
        rows, slot = half_rows(half), half * ROWS + row
        return remote(
            hy_tx.at[row, rows], hy_rx.at[row, rows], hy_out.at[slot], hy_in.at[slot], other
        )

    def row_terms(row, at, half):
        rows = half_rows(half)
        return remote(
            hz_tx.at[row, rows], hz_rx.at[at, rows],
            hz_out.at[half * ROWS + row], hz_in.at[half * ROWS + at], row * 2 + y,
        )

    loads[4].wait()

    def send_side(i, carry):
        row = near_first(z, ROWS - 1 - i)
        hy_tx[row] = term(row * 2 + 1 - y).astype(jnp.bfloat16)
        side_terms(row, 0).start()
        return carry

    def keep_own(i, carry):
        row = near_first(z, ROWS - 1 - i)
        hk[row] = term(row * 2 + y)
        return carry

    lax.fori_loop(0, ROWS, send_side, 0)
    for half in range(1, HALVES):
        for step in range(ROWS - 1, -1, -1):
            side_terms(near_first(z, step), half).start()
    lax.fori_loop(0, ROWS, keep_own, 0)

    def reduce_row(step, half):
        row, rows = near_first(z, step), half_rows(half)
        side_terms(row, half).wait_recv()
        hz_tx[row, rows, :] = (
            hk[row, rows, :] + hy_rx[row, rows, :].astype(jnp.float32)
        ).astype(jnp.bfloat16)
        row_terms(row, z, half).start()

    def settle(half):
        rows = half_rows(half)
        side_terms(z, half).wait_recv()
        summed = (
            cur[rows, own_cols(me)].astype(jnp.float32)
            + hk[z, rows, :]
            + hy_rx[z, rows, :].astype(jnp.float32)
        )
        for step in range(1, ROWS):
            row = near_first(z, step)
            row_terms(row, row, half).wait_recv()
            summed = summed + hz_rx[row, rows, :].astype(jnp.float32)
        out_ref[rows, own_cols(me)] = summed.astype(jnp.bfloat16)
        out_spread(z, start, half)

    def out_arrived(c, half):
        view = out_view(c, half)
        in_sem = r_in.at[half * 2 * ROWS + c]
        remote(view, view, r_side.at[0], in_sem, other).wait_recv()

    def pass_on(step, half):
        row = near_first(z, step)
        out_arrived(row * 2 + y, half)
        out_spread(row, start, half)

    for step in range(ROWS - 1, 0, -1):
        reduce_row(step, 0)
    settle(0)
    for half in range(1, HALVES):
        for step in range(ROWS - 1, 0, -1):
            reduce_row(step, half)
            pass_on(ROWS - step, half - 1)
        settle(half)
    for step in range(1, ROWS):
        pass_on(step, HALVES - 1)
    for half in range(HALVES):
        for row in range(ROWS):
            out_arrived(row * 2 + 1 - y, half)

    each_shift(finish)

    def side_done(i, carry):
        @pl.when(takes_half)
        def _():
            shift_side(piece_at(i)).wait_send()

        return carry

    lax.fori_loop(0, PIECES // 2, side_done, 0)
    for row in range(ROWS):
        q_spread(row, finish)
        for half in range(HALVES):
            out_spread(row, finish, half)
            side_terms(row, half).wait_send()
        for copy in y_copies(row):
            copy.wait_send()
    for step in range(1, ROWS):
        row = near_first(z, step)
        for copy in z_copies(row):
            copy.wait_send()
        for half in range(HALVES):
            row_terms(row, z, half).wait_send()


def plane_call(counts, gain, cosine, sine, fresh, previous, w_query, w_keyval, keys, values, w_out):
    tokens, features = fresh.shape
    width = w_query.shape[1]
    slots = keys.shape[0]
    bf16, f32 = jnp.bfloat16, jnp.float32
    vmem = pl.BlockSpec(memory_space=pltpu.VMEM)
    anywhere = pl.BlockSpec(memory_space=pl.ANY)
    turned = lambda count: pltpu.VMEM((count, HD, width // HD * tokens), bf16)
    chunks = lambda count, kind: pltpu.VMEM((count, tokens, width), kind)
    logs = lambda count: pltpu.VMEM((count, 8, tokens), f32)
    sems = lambda count: pltpu.SemaphoreType.DMA((count,))
    like = lambda array: pltpu.VMEM(array.shape, array.dtype)
    return pl.pallas_call(
        plane_kernel,
        out_shape=jax.ShapeDtypeStruct(fresh.shape, bf16),
        in_specs=[pl.BlockSpec(memory_space=pltpu.SMEM)] + [vmem] * 3 + [anywhere] * 7,
        out_specs=vmem,
        scratch_shapes=[
            like(fresh), like(fresh), like(w_query), like(w_keyval),
            pltpu.VMEM((tokens, HD), bf16), pltpu.VMEM((tokens, HD), bf16),
            pltpu.VMEM((slots, HD), bf16),
            pltpu.VMEM((2, slots, PAIR * tokens), f32),
            pltpu.VMEM((2, slots, PAIR * tokens), bf16),
            pltpu.VMEM((2, HD + 16, slots), bf16),
            turned(2 * ROWS), like(keys), like(values), like(w_out),
            turned(2 * ROWS), logs(2 * ROWS), turned(ROWS), logs(ROWS),
            turned(ROWS), logs(ROWS), turned(ROWS), logs(ROWS),
            pltpu.VMEM((tokens, width), bf16),
            chunks(ROWS, f32), chunks(ROWS, bf16), chunks(ROWS, bf16),
            chunks(ROWS, bf16), chunks(ROWS, bf16),
            sems(6), sems(PIECES), sems(PIECES), sems(PIECES),
            sems(ROWS), sems(ROWS), sems(ROWS), sems(2 * ROWS),
        ] + [sems(ROWS)] * 8 + [sems(HALVES * ROWS)] * 7 + [sems(2 * HALVES * ROWS)],
        compiler_params=pltpu.CompilerParams(
            collective_id=0, has_side_effects=True, vmem_limit_bytes=60 * 1024 * 1024
        ),
        cost_estimate=pl.CostEstimate(
            flops=4 * tokens * width * slots * 8, bytes_accessed=20 << 20,
            transcendentals=tokens * slots * 32,
        ),
    )(counts, gain, cosine, sine, fresh, previous, w_query, w_keyval, keys, values, w_out)


def plane_shards(
    fresh, previous, span_index, cache_counts, norm_gain,
    w_query, w_keyval, w_out, cache_keys, cache_values,
):
    length = fresh.shape[0]
    half_width = HD // 2
    positions = (span_index[0] * length + jnp.arange(length, dtype=jnp.int32)).astype(jnp.float32)
    inverse = ROPE_BASE ** (-(jnp.arange(half_width, dtype=jnp.float32) * 2.0) / HD)
    angles = positions[:, None] * inverse[None, :]
    cosine, sine = jnp.cos(angles), jnp.sin(angles)
    mixed = plane_call(
        cache_counts, norm_gain,
        jnp.concatenate([cosine, cosine], axis=1), jnp.concatenate([-sine, sine], axis=1),
        fresh, previous[0], w_query[0], w_keyval[0], cache_keys[0], cache_values[0], w_out[0],
    )
    return mixed[None]


def solution(mesh):
    placed = (
        P(),
        P("segment", None, None),
        P("segment"),
        P("segment", None),
        P("segment", None),
        P("segment", None, "blk"),
        P("segment", None, "blk"),
        P("segment", "blk", None),
        P("segment", "blk", None),
        P("segment", "blk", None),
    )
    body = plane_shards if mesh.shape["blk"] == KVH else shards
    return jax.shard_map(
        body, mesh=mesh, in_specs=placed, out_specs=P("segment", None, None), check_vma=False
    )
```

```python
import math

import jax
import jax.numpy as jnp
from jax import lax
from jax.experimental import pallas as pl
from jax.experimental.pallas import tpu as pltpu
from jax.sharding import PartitionSpec as P

KVH = 8
HD = 128


ROPE_BASE = 500000.0
EPSILON = 1e-05


def passed_along(block, axis, distance):
    devices = range(lax.axis_size(axis))
    route = [(i - distance, i) for i in devices if i - distance in devices]
    return lax.ppermute(block, axis, route)


def swapped(block, axis, distance):
    count = lax.axis_size(axis)
    route = []
    for low in range(count):
        high = low | 1 << distance
        if high != low and high < count:
            route += [(low, high), (high, low)]
    return lax.ppermute(block, axis, route)


def rotate(projected, first_span):
    length = projected.shape[0]
    half_width = projected.shape[-1] // 2
    positions = (first_span * length + jnp.arange(length, dtype=jnp.int32)).astype(jnp.float32)
    inverse = ROPE_BASE ** (
        -(jnp.arange(half_width, dtype=jnp.float32) * 2.0) / projected.shape[-1]
    )
    angles = positions[:, None] * inverse[None, :]
    cosine = jnp.cos(angles)[:, None, :]
    sine_table = jnp.sin(angles)[:, None, :]
    left_part = projected[..., :half_width]
    right_part = projected[..., half_width:]
    return jnp.concatenate(
        [
            left_part * cosine - right_part * sine_table,
            right_part * cosine + left_part * sine_table,
        ],
        axis=-1,
    )


def attend_rows(query_rows, key_rows, value_rows, allowed):
    scores = lax.dot_general(
        query_rows, key_rows, (((1,), (1,)), ((), ())), preferred_element_type=jnp.float32
    ) * query_rows.shape[-1] ** (-0.5)
    scores = jnp.where(allowed, scores, -jnp.inf)
    highest = jnp.max(scores, axis=-1, keepdims=True)
    weights = jnp.exp(scores - highest)
    totals = jnp.sum(weights, axis=-1, keepdims=True)
    partial_out = (
        jnp.dot(weights.astype(jnp.bfloat16), value_rows, preferred_element_type=jnp.float32)
        / totals
    ).astype(jnp.bfloat16)
    return (partial_out, (highest + jnp.log(totals))[:, 0])


def shards(
    fresh,
    previous,
    span_index,
    cache_counts,
    norm_gain,
    w_query,
    w_keyval,
    w_out,
    cache_keys,
    cache_values,
):
    blocks = lax.axis_size("blk")
    position = lax.axis_index("blk")
    span_rows = fresh.shape[0]
    arrived = passed_along(previous[0], "segment", 1)
    current = jnp.where(lax.axis_index("segment") == 0, fresh, arrived)
    widened = current.astype(jnp.float32)
    normed = (
        widened
        * lax.rsqrt(jnp.mean(widened * widened, axis=-1, keepdims=True) + EPSILON)
        * norm_gain[0]
    ).astype(jnp.bfloat16)
    first_span = span_index[0]
    heads_here = w_query.shape[2] // HD
    ratio = blocks // KVH
    queries = jnp.dot(normed, w_query[0], preferred_element_type=jnp.float32).reshape(
        span_rows, heads_here, HD
    )
    queries = rotate(queries, first_span).astype(jnp.bfloat16).reshape(span_rows, heads_here * HD)
    projected = jnp.dot(normed, w_keyval[0], preferred_element_type=jnp.float32)
    if ratio == 2:
        odd_member = position % 2 == 1
        as_key = rotate(projected[:, None, :], first_span)[:, 0, :].astype(jnp.bfloat16)
        mine = jnp.where(odd_member, projected.astype(jnp.bfloat16), as_key)
        partner = swapped(mine, "blk", 0)
        own_keys = jnp.where(odd_member, partner, mine)
        own_values = jnp.where(odd_member, mine, partner)
    else:
        own_keys = rotate(projected[:, None, :HD], first_span)[:, 0, :].astype(jnp.bfloat16)
        own_values = projected[:, HD:].astype(jnp.bfloat16)
    query_rows = queries.reshape(span_rows * heads_here, HD)
    row_tokens = jnp.arange(span_rows * heads_here, dtype=jnp.int32) // heads_here
    causal = row_tokens[:, None] >= jnp.arange(span_rows, dtype=jnp.int32)[None, :]
    own_out, own_log = attend_rows(query_rows, own_keys, own_values, causal)
    own_out = own_out.reshape(span_rows, heads_here * HD)
    own_log = own_log.reshape(span_rows, heads_here).T
    cache_rows = cache_keys.shape[1]
    offsets = jnp.arange(cache_rows, dtype=jnp.int32)
    every_query = lax.all_gather(queries, "blk", axis=0, tiled=True)
    live = cache_counts[0, position]

    def holder(source):
        query_block = lax.dynamic_slice_in_dim(
            every_query, source * span_rows, span_rows, 0
        ).reshape(span_rows * heads_here, HD)
        head_start = source // ratio * HD
        key_rows = lax.dynamic_slice_in_dim(cache_keys[0], head_start, HD, 1)
        value_rows = lax.dynamic_slice_in_dim(cache_values[0], head_start, HD, 1)
        partial_out, log_totals = attend_rows(
            query_block, key_rows, value_rows, (offsets < live)[None, :]
        )
        return (
            partial_out.reshape(span_rows, heads_here * HD),
            log_totals.reshape(span_rows, heads_here).T,
        )

    held_outs, held_logs = lax.map(holder, jnp.arange(blocks, dtype=jnp.int32))
    shard_outs = lax.all_to_all(held_outs, "blk", split_axis=0, concat_axis=0, tiled=True)
    shard_logs = lax.all_to_all(held_logs, "blk", split_axis=0, concat_axis=0, tiled=True)
    all_outs = (
        jnp.concatenate([own_out[None], shard_outs], axis=0)
        .astype(jnp.float32)
        .reshape(blocks + 1, span_rows, heads_here, HD)
    )
    all_logs = jnp.concatenate([own_log[None], shard_logs], axis=0).transpose(0, 2, 1)
    ceiling = jnp.max(all_logs, axis=0)
    factors = jnp.exp(all_logs - ceiling)
    attended = (
        jnp.sum(factors[..., None] * all_outs, axis=0) / jnp.sum(factors, axis=0)[..., None]
    ).astype(jnp.bfloat16)
    attended = attended.reshape(span_rows, heads_here * HD)
    head_terms = lax.optimization_barrier(
        jnp.dot(attended, w_out[0], preferred_element_type=jnp.float32).astype(jnp.bfloat16)
    ).astype(jnp.float32)
    summed = lax.psum(head_terms.astype(jnp.bfloat16), "blk").astype(jnp.float32)
    mixed = (widened + summed).astype(jnp.bfloat16)
    return mixed[None]


ROWS = 4
PIECES = 8
PAIR = 1
HALVES = 2
BLOCKS = 4
FINE = 4
DEAD = -1e30
MESH = pl.DeviceIdType.MESH


def near_first(z, step):
    half = z // 2
    if isinstance(step, int):
        return (z, z + 1 - 2 * (z % 2), 2 - half, 3 - 3 * half)[step]
    pair = z + 1 - 2 * (z % 2)
    later = jnp.where(step == 2, 2 - half, 3 - 3 * half)
    return jnp.where(step == 0, z, jnp.where(step == 1, pair, later))


def plane_kernel(
    counts_ref, gain_ref, cos_ref, sin_ref, fresh_hbm, prev_hbm, wq_hbm, wkv_hbm,
    kc_hbm, vc_hbm, wo_hbm, out_ref,
    cur, normed, wq, wkv, own_k, own_v, hidden, s_buf, p_buf, v_turn,
    qall, kbuf, vbuf, wo, parts, logs, oy_rx, ly_rx,
    oz_tx, lz_tx, oz_rx, lz_rx, att, hk, hy_tx, hy_rx, hz_tx, hz_rx,
    load_sem, x_out, x_side, x_in, q_up, q_down, q_side, q_in, oy_out, oy_in, ly_out, ly_in,
    oz_out, oz_in, lz_out, lz_in, hy_out, hy_in, hz_out, hz_in,
    r_up, r_down, r_side, r_in,
):
    me = lax.axis_index("blk")
    layer = lax.axis_index("segment")
    layers = lax.axis_size("segment")
    z, y = me // 2, me % 2
    other = z * 2 + 1 - y
    tokens, width = cur.shape[0], wq.shape[1]
    heads = width // HD
    to_log2 = HD ** (-0.5) * math.log2(math.e)
    piece = tokens // PIECES

    def own_cols(c):
        return pl.ds(pl.multiple_of(c * width, width), width)

    loads = [
        pltpu.make_async_copy(wq_hbm, wq, load_sem.at[0]),
        pltpu.make_async_copy(wkv_hbm, wkv, load_sem.at[1]),
        pltpu.make_async_copy(kc_hbm, kbuf, load_sem.at[2]),
        pltpu.make_async_copy(vc_hbm, vbuf, load_sem.at[3]),
        pltpu.make_async_copy(wo_hbm, wo, load_sem.at[4]),
    ]
    fresh_load = pltpu.make_async_copy(fresh_hbm, cur, load_sem.at[5])

    @pl.when(layer == 0)
    def _():
        fresh_load.start()

    for load in loads:
        load.start()

    has_source, has_next = layer > 0, layer < layers - 1
    barrier = pltpu.get_barrier_semaphore()
    pl.semaphore_signal(barrier, inc=1, device_id={"blk": other}, device_id_type=MESH)
    for step in range(1, ROWS):
        pl.semaphore_signal(
            barrier, inc=1, device_id={"blk": near_first(z, step) * 2 + y}, device_id_type=MESH
        )

    @pl.when(has_source)
    def _():
        pl.semaphore_signal(
            barrier, inc=1, device_id={"segment": layer - 1}, device_id_type=MESH
        )

    @pl.when(has_next)
    def _():
        pl.semaphore_signal(
            barrier, inc=1, device_id={"segment": layer + 1}, device_id_type=MESH
        )

    pl.semaphore_wait(
        barrier, ROWS + has_source.astype(jnp.int32) + has_next.astype(jnp.int32)
    )

    def remote(src, dst, out_sem, in_sem, device):
        return pltpu.make_async_remote_copy(
            src_ref=src, dst_ref=dst, send_sem=out_sem, recv_sem=in_sem,
            device_id={"blk": device}, device_id_type=MESH,
        )

    def rows_of_piece(p):
        return pl.ds(pl.multiple_of(p * piece, piece), piece)

    def shift_copy(p):
        rows = rows_of_piece(p)
        return pltpu.make_async_remote_copy(
            src_ref=prev_hbm.at[rows], dst_ref=cur.at[rows],
            send_sem=x_out.at[p], recv_sem=x_in.at[p],
            device_id={"segment": layer + 1}, device_id_type=MESH,
        )

    def shift_side(p):
        rows = rows_of_piece(p)
        return remote(cur.at[rows], cur.at[rows], x_side.at[p], x_in.at[p], other)

    def piece_at(i):
        return (y * (PIECES // 2) + i) % PIECES

    to_core = layer % 2 == 0
    takes_half = jnp.logical_and(has_source, to_core)

    def each_shift(act):
        def step(i, carry):
            @pl.when(jnp.logical_and(has_next, jnp.logical_or(to_core, i < PIECES // 2)))
            def _():
                act(shift_copy(piece_at(i)))

            return carry

        lax.fori_loop(0, PIECES, step, 0)

    def spread(view, up, down, side, arrived, row, act, half=0):
        part = view(row * 2 + y, half)
        in_sem = arrived.at[half * 2 * ROWS + row * 2 + y]
        slot = half * ROWS + row

        @pl.when(jnp.logical_and(row <= z, z < ROWS - 1))
        def _():
            act(remote(part, part, up.at[slot], in_sem, me + 2))

        @pl.when(jnp.logical_and(row >= z, z > 0))
        def _():
            act(remote(part, part, down.at[slot], in_sem, me - 2))

        act(remote(part, part, side.at[slot], in_sem, other))

    def start(copy):
        copy.start()

    def finish(copy):
        copy.wait_send()

    each_shift(start)

    def q_view(c, half=0):
        return qall.at[c]

    def half_rows(half):
        return pl.ds(half * (tokens // HALVES), tokens // HALVES)

    def out_view(c, half):
        return out_ref.at[half_rows(half), own_cols(c)]

    def q_spread(row, act):
        spread(q_view, q_up, q_down, q_side, q_in, row, act)

    def out_spread(row, act, half):
        spread(out_view, r_up, r_down, r_side, r_in, row, act, half)

    slot_no = lax.broadcasted_iota(jnp.int32, hidden.shape, 0)
    lane_no = lax.broadcasted_iota(jnp.int32, hidden.shape, 1)
    dead = jnp.logical_and(slot_no >= counts_ref[0, me], lane_no == 0)
    hidden[...] = jnp.where(dead, DEAD, 0.0).astype(jnp.bfloat16)
    for slot in range(2):
        v_turn[slot, HD:, :] = jnp.ones((16, v_turn.shape[2]), jnp.bfloat16)
    first_row = jnp.where(
        lax.broadcasted_iota(jnp.int32, (HD, PAIR * tokens), 0) == 0, 1.0, 0.0
    ).astype(jnp.bfloat16)
    slots = hidden.shape[0]
    block = slots // BLOCKS

    def normalize(i, carry):
        p = piece_at(i)

        @pl.when(has_source)
        def _():
            shift_side(p).wait_recv()

        @pl.when(jnp.logical_and(takes_half, i < PIECES // 2))
        def _():
            shift_side(p).start()

        @pl.when(jnp.logical_and(layer == 0, i == 0))
        def _():
            fresh_load.wait()

        rows = rows_of_piece(p)
        widened = cur[rows, :].astype(jnp.float32)
        normed[rows, :] = (
            widened
            * lax.rsqrt(jnp.mean(widened * widened, axis=-1, keepdims=True) + EPSILON)
            * gain_ref[...]
        ).astype(jnp.bfloat16)
        return carry

    lax.fori_loop(0, PIECES, normalize, 0)

    def rotated(part):
        half = HD // 2
        turned = jnp.concatenate([part[:, half:], part[:, :half]], axis=1)
        return part * cos_ref[...] + turned * sin_ref[...]

    loads[0].wait()
    projected = jnp.dot(normed[...], wq[...], preferred_element_type=jnp.float32)
    for h in range(heads):
        cols = slice(h * HD, (h + 1) * HD)
        qall[me, :, h * tokens : (h + 1) * tokens] = (rotated(projected[:, cols]) * to_log2).T.astype(jnp.bfloat16)

    def one_head(k_part, q_part, v_turned, masked):
        scores = jnp.dot(k_part, q_part, preferred_element_type=jnp.float32) + masked
        highest = jnp.max(scores, axis=0, keepdims=True)
        weights = jnp.exp2(scores - highest).astype(jnp.bfloat16)
        mixed = jnp.dot(v_turned, weights, preferred_element_type=jnp.float32)
        totals = mixed[HD : HD + 1]
        partial = (mixed[:HD] / totals).astype(jnp.bfloat16)
        return partial, highest + jnp.log2(totals)

    def with_ones(v_part):
        return jnp.concatenate(
            [v_part.T, jnp.ones((16, v_part.shape[0]), jnp.bfloat16)], axis=0
        )

    def log_rows(rows):
        return jnp.concatenate(rows + [jnp.zeros((8 - heads, tokens), jnp.float32)], axis=0)

    def y_copies(row):
        return (
            remote(parts.at[ROWS + row], oy_rx.at[row], oy_out.at[row], oy_in.at[row], other),
            remote(logs.at[ROWS + row], ly_rx.at[row], ly_out.at[row], ly_in.at[row], other),
        )

    def z_copies(row):
        peer = row * 2 + y
        return (
            remote(oz_tx.at[row], oz_rx.at[z], oz_out.at[row], oz_in.at[z], peer),
            remote(lz_tx.at[row], lz_rx.at[z], lz_out.at[row], lz_in.at[z], peer),
        )

    def merge(row, away):
        for copy in y_copies(row):
            copy.wait_recv()
        l_a, l_b = logs[row], ly_rx[row]
        top = jnp.maximum(l_a, l_b)
        f_a, f_b = jnp.exp2(l_a - top), jnp.exp2(l_b - top)
        total = f_a + f_b
        f_a, f_b = f_a / total, f_b / total
        o_dst, l_dst, at = (oz_tx, lz_tx, row) if away else (oz_rx, lz_rx, z)
        l_dst[at] = top + jnp.log2(total)
        for h in range(heads):
            part = slice(h * tokens, (h + 1) * tokens)
            o_dst[at, :, part] = (
                f_a[h : h + 1] * parts[row, :, part].astype(jnp.float32)
                + f_b[h : h + 1] * oy_rx[row, :, part].astype(jnp.float32)
            ).astype(jnp.bfloat16)
        if away:
            for copy in z_copies(row):
                copy.start()

    def chunk_at(t):
        row = near_first(z, (t + 1) // 2 % ROWS)
        second = jnp.where(t == 0, 0, jnp.where(t == 2 * ROWS - 1, 1, (t + 1) % 2))
        return row, row * 2 + jnp.where(second == 0, y, 1 - y), second

    def group_of(c):
        return pl.ds(pl.multiple_of(c * HD, HD), HD)

    def turn_values(c, slot, b):
        rows = slice(b * block, (b + 1) * block)
        v_turn[slot, :HD, rows] = vbuf[rows, group_of(c)].T

    q_spread(z, start)
    loads[1].wait()
    both = jnp.dot(normed[...], wkv[...], preferred_element_type=jnp.float32)
    own_k[...] = rotated(both[:, :HD]).astype(jnp.bfloat16)
    own_v[...] = both[:, HD:].astype(jnp.bfloat16)
    loads[2].wait()
    loads[3].wait()
    for b in range(BLOCKS):
        turn_values(me, 0, b)

    def visit(t, carry):
        slot = t % 2
        row, c, second = chunk_at(t)
        following_c = chunk_at(t + 1)[1]

        @pl.when(t > 0)
        def _():
            remote(q_view(c), q_view(c), q_side.at[row], q_in.at[c], other).wait_recv()

        @pl.when(jnp.logical_and(t > 0, second == 0))
        def _():
            q_spread(row, start)

        group = group_of(c)
        to = second * ROWS + row
        wide, pairs = PAIR * tokens, heads // PAIR

        def score_block(h, b, highest):
            rows = slice(b * block, (b + 1) * block)
            keys = jnp.concatenate([kbuf[rows, group], hidden[rows, :]], axis=1)
            asked = jnp.concatenate(
                [qall[c, :, h * wide : (h + 1) * wide], first_row], axis=0
            )
            scores = jnp.dot(keys, asked, preferred_element_type=jnp.float32)
            s_buf[h % 2, rows, :] = scores
            here = jnp.max(scores, axis=0, keepdims=True)
            return here if highest is None else jnp.maximum(highest, here)

        def weigh_block(h, b, highest):
            fine = block // FINE
            for i in range(FINE):
                rows = slice(b * block + i * fine, b * block + (i + 1) * fine)
                p_buf[h % 2, rows, :] = jnp.exp2(s_buf[h % 2, rows, :] - highest).astype(
                    jnp.bfloat16
                )

        def value_block(h, b, total):
            rows = slice(b * block, (b + 1) * block)
            here = jnp.dot(
                v_turn[slot, :, rows], p_buf[h % 2, rows, :], preferred_element_type=jnp.float32
            )
            return here if total is None else total + here

        totals = []
        highest = None
        for b in range(BLOCKS):
            highest = score_block(0, b, highest)
        for h in range(pairs):
            following, mixed = None, None
            for b in range(BLOCKS):
                if h + 1 < pairs:
                    following = score_block(h + 1, b, following)
                weigh_block(h, b, highest)
                if b % pairs == h:
                    turn_values(following_c, 1 - slot, b)
                if b > 0:
                    mixed = value_block(h, b - 1, mixed)
            mixed = value_block(h, BLOCKS - 1, mixed)
            total = mixed[HD : HD + 1]
            parts[to, :, h * wide : (h + 1) * wide] = (mixed[:HD] / total).astype(jnp.bfloat16)
            log_total = highest + jnp.log2(total)
            totals += [log_total[:, i * tokens : (i + 1) * tokens] for i in range(PAIR)]
            highest = following
        logs[to] = log_rows(totals)

        @pl.when(second == 1)
        def _():
            for copy in y_copies(row):
                copy.start()

        @pl.when(t == 4)
        def _():
            merge(near_first(z, 1), True)

        @pl.when(t == 6)
        def _():
            merge(near_first(z, 2), True)

        return carry

    lax.fori_loop(0, 2 * ROWS, visit, 0)

    key_no = lax.broadcasted_iota(jnp.int32, (tokens, tokens), 0)
    token_no = lax.broadcasted_iota(jnp.int32, (tokens, tokens), 1)
    causal = jnp.where(token_no >= key_no, 0.0, -jnp.inf)
    own, own_logs = [], []
    own_turned = with_ones(own_v[...])
    for h in range(heads):
        partial, log_total = one_head(
            own_k[...], qall[me, :, h * tokens : (h + 1) * tokens], own_turned, causal
        )
        own_logs.append(log_total)
        own.append(partial)

    merge(near_first(z, 3), True)
    merge(z, False)

    def from_row(row):
        return (
            remote(oz_tx.at[row], oz_rx.at[row], oz_out.at[row], oz_in.at[row], row * 2 + y),
            remote(lz_tx.at[row], lz_rx.at[row], lz_out.at[row], lz_in.at[row], row * 2 + y),
        )

    for step in range(1, ROWS):
        for copy in from_row(near_first(z, step)):
            copy.wait_recv()
    all_logs = [log_rows(own_logs)] + [lz_rx[row] for row in range(ROWS)]
    top = all_logs[0]
    for log_total in all_logs[1:]:
        top = jnp.maximum(top, log_total)
    factors = [jnp.exp2(log_total - top) for log_total in all_logs]
    total = factors[0]
    for factor in factors[1:]:
        total = total + factor
    factors = [factor / total for factor in factors]
    for h in range(heads):
        part = slice(h * tokens, (h + 1) * tokens)
        summed = factors[0][h : h + 1] * own[h].astype(jnp.float32)
        for row in range(ROWS):
            summed = summed + factors[row + 1][h : h + 1] * oz_rx[row, :, part].astype(
                jnp.float32
            )
        att[:, h * HD : (h + 1) * HD] = summed.T.astype(jnp.bfloat16)

    def term(c):
        return jnp.dot(att[...], wo[:, own_cols(c)], preferred_element_type=jnp.float32)

    def side_terms(row, half):
        rows, slot = half_rows(half), half * ROWS + row
        return remote(
            hy_tx.at[row, rows], hy_rx.at[row, rows], hy_out.at[slot], hy_in.at[slot], other
        )

    def row_terms(row, at, half):
        rows = half_rows(half)
        return remote(
            hz_tx.at[row, rows], hz_rx.at[at, rows],
            hz_out.at[half * ROWS + row], hz_in.at[half * ROWS + at], row * 2 + y,
        )

    loads[4].wait()

    def send_side(i, carry):
        row = near_first(z, ROWS - 1 - i)
        hy_tx[row] = term(row * 2 + 1 - y).astype(jnp.bfloat16)
        side_terms(row, 0).start()
        return carry

    def keep_own(i, carry):
        row = near_first(z, ROWS - 1 - i)
        hk[row] = term(row * 2 + y)
        return carry

    lax.fori_loop(0, ROWS, send_side, 0)
    for half in range(1, HALVES):
        for step in range(ROWS - 1, -1, -1):
            side_terms(near_first(z, step), half).start()
    lax.fori_loop(0, ROWS, keep_own, 0)

    def reduce_row(step, half):
        row, rows = near_first(z, step), half_rows(half)
        side_terms(row, half).wait_recv()
        hz_tx[row, rows, :] = (
            hk[row, rows, :] + hy_rx[row, rows, :].astype(jnp.float32)
        ).astype(jnp.bfloat16)
        row_terms(row, z, half).start()

    def settle(half):
        rows = half_rows(half)
        side_terms(z, half).wait_recv()
        summed = (
            cur[rows, own_cols(me)].astype(jnp.float32)
            + hk[z, rows, :]
            + hy_rx[z, rows, :].astype(jnp.float32)
        )
        for step in range(1, ROWS):
            row = near_first(z, step)
            row_terms(row, row, half).wait_recv()
            summed = summed + hz_rx[row, rows, :].astype(jnp.float32)
        out_ref[rows, own_cols(me)] = summed.astype(jnp.bfloat16)
        out_spread(z, start, half)

    def out_arrived(c, half):
        view = out_view(c, half)
        in_sem = r_in.at[half * 2 * ROWS + c]
        remote(view, view, r_side.at[0], in_sem, other).wait_recv()

    def pass_on(step, half):
        row = near_first(z, step)
        out_arrived(row * 2 + y, half)
        out_spread(row, start, half)

    for step in range(ROWS - 1, 0, -1):
        reduce_row(step, 0)
    settle(0)
    for half in range(1, HALVES):
        for step in range(ROWS - 1, 0, -1):
            reduce_row(step, half)
            pass_on(ROWS - step, half - 1)
        settle(half)
    for step in range(1, ROWS):
        pass_on(step, HALVES - 1)
    for half in range(HALVES):
        for row in range(ROWS):
            out_arrived(row * 2 + 1 - y, half)

    each_shift(finish)

    def side_done(i, carry):
        @pl.when(takes_half)
        def _():
            shift_side(piece_at(i)).wait_send()

        return carry

    lax.fori_loop(0, PIECES // 2, side_done, 0)
    for row in range(ROWS):
        q_spread(row, finish)
        for half in range(HALVES):
            out_spread(row, finish, half)
            side_terms(row, half).wait_send()
        for copy in y_copies(row):
            copy.wait_send()
    for step in range(1, ROWS):
        row = near_first(z, step)
        for copy in z_copies(row):
            copy.wait_send()
        for half in range(HALVES):
            row_terms(row, z, half).wait_send()


def plane_call(counts, gain, cosine, sine, fresh, previous, w_query, w_keyval, keys, values, w_out):
    tokens, features = fresh.shape
    width = w_query.shape[1]
    slots = keys.shape[0]
    bf16, f32 = jnp.bfloat16, jnp.float32
    vmem = pl.BlockSpec(memory_space=pltpu.VMEM)
    anywhere = pl.BlockSpec(memory_space=pl.ANY)
    turned = lambda count: pltpu.VMEM((count, HD, width // HD * tokens), bf16)
    chunks = lambda count, kind: pltpu.VMEM((count, tokens, width), kind)
    logs = lambda count: pltpu.VMEM((count, 8, tokens), f32)
    sems = lambda count: pltpu.SemaphoreType.DMA((count,))
    like = lambda array: pltpu.VMEM(array.shape, array.dtype)
    return pl.pallas_call(
        plane_kernel,
        out_shape=jax.ShapeDtypeStruct(fresh.shape, bf16),
        in_specs=[pl.BlockSpec(memory_space=pltpu.SMEM)] + [vmem] * 3 + [anywhere] * 7,
        out_specs=vmem,
        scratch_shapes=[
            like(fresh), like(fresh), like(w_query), like(w_keyval),
            pltpu.VMEM((tokens, HD), bf16), pltpu.VMEM((tokens, HD), bf16),
            pltpu.VMEM((slots, HD), bf16),
            pltpu.VMEM((2, slots, PAIR * tokens), f32),
            pltpu.VMEM((2, slots, PAIR * tokens), bf16),
            pltpu.VMEM((2, HD + 16, slots), bf16),
            turned(2 * ROWS), like(keys), like(values), like(w_out),
            turned(2 * ROWS), logs(2 * ROWS), turned(ROWS), logs(ROWS),
            turned(ROWS), logs(ROWS), turned(ROWS), logs(ROWS),
            pltpu.VMEM((tokens, width), bf16),
            chunks(ROWS, f32), chunks(ROWS, bf16), chunks(ROWS, bf16),
            chunks(ROWS, bf16), chunks(ROWS, bf16),
            sems(6), sems(PIECES), sems(PIECES), sems(PIECES),
            sems(ROWS), sems(ROWS), sems(ROWS), sems(2 * ROWS),
        ] + [sems(ROWS)] * 8 + [sems(HALVES * ROWS)] * 7 + [sems(2 * HALVES * ROWS)],
        compiler_params=pltpu.CompilerParams(
            collective_id=0, has_side_effects=True, vmem_limit_bytes=60 * 1024 * 1024
        ),
        cost_estimate=pl.CostEstimate(
            flops=4 * tokens * width * slots * 8, bytes_accessed=20 << 20,
            transcendentals=tokens * slots * 32,
        ),
    )(counts, gain, cosine, sine, fresh, previous, w_query, w_keyval, keys, values, w_out)


def plane_shards(
    fresh, previous, span_index, cache_counts, norm_gain,
    w_query, w_keyval, w_out, cache_keys, cache_values,
):
    length = fresh.shape[0]
    half_width = HD // 2
    positions = (span_index[0] * length + jnp.arange(length, dtype=jnp.int32)).astype(jnp.float32)
    inverse = ROPE_BASE ** (-(jnp.arange(half_width, dtype=jnp.float32) * 2.0) / HD)
    angles = positions[:, None] * inverse[None, :]
    cosine, sine = jnp.cos(angles), jnp.sin(angles)
    mixed = plane_call(
        cache_counts, norm_gain,
        jnp.concatenate([cosine, cosine], axis=1), jnp.concatenate([-sine, sine], axis=1),
        fresh, previous[0], w_query[0], w_keyval[0], cache_keys[0], cache_values[0], w_out[0],
    )
    return mixed[None]


def solution(mesh):
    placed = (
        P(),
        P("segment", None, None),
        P("segment"),
        P("segment", None),
        P("segment", None),
        P("segment", None, "blk"),
        P("segment", None, "blk"),
        P("segment", "blk", None),
        P("segment", "blk", None),
        P("segment", "blk", None),
    )
    body = plane_shards if mesh.shape["blk"] == KVH else shards
    return jax.shard_map(
        body, mesh=mesh, in_specs=placed, out_specs=P("segment", None, None), check_vma=False
    )
```
